32 devices in a mesh: seq: 8 (over z, x), grp: 4 (over y, core).
Axes of the slice: x: 2, y: 2, z: 4, core: 2. Of those that a mesh axis runs over, the one named last changes fastest.
Arguments:
- streams: float32 [3, 2048, 4096], P(None, 'seq', 'grp'), may hold values from -6 to 6
- short_filters: float32 [3, 3, 4096], P(None, None, 'grp'), may hold values from -3.5 to 3.5
- skip_gain: float32 [4096], P('grp'), may hold values from -4 to 4
- long_filter: float32 [2048, 256], P('seq', 'grp'), may hold values from -0.125 to 0.125
Outputs:
- hyena_output: float32 [256, 8, 4096], P('seq', None, 'grp')
The draws below stay inside these ranges and needn't reach their ends.
All inputs are finite; a program needn't handle non-finite values.
Results may differ from the reference program's by a relative error of at most 0.00011.
Values sent between devices are 32-bit elements; how exact they have to be, the bound alone decides.
No kernel may reach another device: no remote copies, remote signals or barrier semaphores. Data moves between devices by JAX's collectives and lax.ppermute only.
A program may use at most 64 MiB of HBM per device.

```python
import jax
import jax.numpy as jnp
from jax import lax

D = 4096
FILTERS = 256
TOK_DEV = 256
PANELS = 8
TOKENS = 2048


def levels(own_key, dims, pieces, least, largest):
    factor_of = 1.0
    for position, parts in pieces:
        heights = jax.random.uniform(jax.random.fold_in(jax.random.fold_in(own_key, 6), position), (parts,), jnp.float32, least / len(pieces), largest / len(pieces))
        factor_of = factor_of * jnp.repeat(jnp.exp(heights), dims[position] // parts).reshape((-1,) + (1,) * (len(dims) - 1 - position))
    return factor_of


def scatter_about(stream_key, dims, width, most, pieces=(), dtype=jnp.bfloat16):
    array = jax.random.normal(stream_key, dims, jnp.float32) * width
    if len(pieces) > 0:
        array = levels(stream_key, dims, pieces, -0.22, 0.18) * array
    return jnp.clip(array, min=-most, max=most).astype(dtype)


def setup_inputs(seed: int = 0) -> dict:
    arg_keys = jax.random.split(jax.random.key(seed), 5)
    streams = scatter_about(arg_keys[0], (3, TOKENS, D), 1.0, 6.0, ((1, 8), (2, 4)), jnp.float32)
    short_filters = scatter_about(arg_keys[1], (3, 3, D), 3 ** -0.5, 3.5, ((2, 4),), jnp.float32)
    skip_gain = scatter_about(arg_keys[2], (D,), 1.0, 4.0, ((0, 4),), jnp.float32)
    long_filter = scatter_about(arg_keys[3], (TOKENS, FILTERS), TOKENS ** -0.5, 0.125, ((0, 8), (1, 4)), jnp.float32)
    return {"streams": streams, "short_filters": short_filters, "skip_gain": skip_gain, "long_filter": long_filter}


def featurize(streams, short_filters):
    length = streams.shape[1]
    padded = jnp.pad(streams, ((0, 0), (2, 0), (0, 0)))
    return (short_filters[:, 0:1, :] * padded[:, 2:, :]
            + short_filters[:, 1:2, :] * padded[:, 1:length + 1, :]
            + short_filters[:, 2:3, :] * padded[:, 0:length, :])


def reference(streams, short_filters, skip_gain, long_filter):
    featured = featurize(streams, short_filters)
    query_rows = featured[0]
    gated_rows = featured[1] * featured[2]
    points = 2 * TOKENS
    blocks = gated_rows.reshape(TOKENS, D // FILTERS, FILTERS).transpose(2, 0, 1)
    filter_cols = long_filter.T

    def convolve(operands):
        block_rows, filter_taps = operands
        spectrum = jnp.fft.rfft(block_rows, n=points, axis=0) * jnp.fft.rfft(filter_taps, n=points)[:, None]
        return jnp.fft.irfft(spectrum, n=points, axis=0)[:TOKENS]

    convolved = lax.map(convolve, (blocks, filter_cols))
    convolved = convolved.transpose(1, 2, 0).reshape(TOKENS, D)
    output_rows = query_rows * (convolved + skip_gain * gated_rows)
    return output_rows.reshape(PANELS, TOK_DEV, D).transpose(1, 0, 2)
```

```python
import functools
import math

import jax
import jax.numpy as jnp
import numpy as np
from jax import lax
from jax.experimental import pallas as pl
from jax.experimental.pallas import tpu as pltpu
from jax.sharding import PartitionSpec as P

LANES = 128
ROWS = 8
VMEM_BYTES = 56 * 1024 * 1024


def passed_along(block, axis, distance):
    devices = range(lax.axis_size(axis))
    route = [(i - distance, i) for i in devices if i - distance in devices]
    return lax.ppermute(block, axis, route)


def contract(pattern, matrix, values):
    return jnp.einsum(pattern, matrix, values, precision=lax.Precision.HIGHEST)


def unit_roots(row_index, col_index, period):
    phase_steps = row_index[:, None] * col_index[None, :] % period
    phases = -2.0 * math.pi / period * phase_steps.astype(jnp.float32)
    return (jnp.cos(phases), jnp.sin(phases))


def rotate(real_part, imag_part, cos_part, sin_part):
    return (
        real_part * cos_part - imag_part * sin_part,
        real_part * sin_part + imag_part * cos_part,
    )


def unrotate(real_part, imag_part, cos_part, sin_part):
    return (
        real_part * cos_part + imag_part * sin_part,
        imag_part * cos_part - real_part * sin_part,
    )


def fine_forward(cos_table, sin_table, real_part, imag_part):
    pattern = "km,imc->ikc"
    return (
        contract(pattern, cos_table, real_part) - contract(pattern, sin_table, imag_part),
        contract(pattern, cos_table, imag_part) + contract(pattern, sin_table, real_part),
    )


def fine_inverse(cos_table, sin_table, real_part, imag_part):
    pattern = "km,ikc->imc"
    return (
        contract(pattern, cos_table, real_part) + contract(pattern, sin_table, imag_part),
        contract(pattern, cos_table, imag_part) - contract(pattern, sin_table, real_part),
    )


def narrow_body(streams, short_filters, skip_gain, long_filter):
    panels = lax.axis_size("seq")
    my_panel = lax.axis_index("seq")
    length = streams.shape[1]
    channels = streams.shape[2]
    slice_len = length // panels
    points = 2 * panels * length
    rim_rows = passed_along(streams[:, length - 2 :, :], "seq", 1)
    extended = jnp.concatenate([rim_rows, streams], axis=1)
    featured = (
        short_filters[:, 0:1, :] * extended[:, 2:, :]
        + short_filters[:, 1:2, :] * extended[:, 1 : length + 1, :]
        + short_filters[:, 2:3, :] * extended[:, 0:length, :]
    )
    query_rows = featured[0]
    gated_rows = featured[1] * featured[2]
    query_cols, gated_cols, filter_cols = (
        lax.all_to_all(
            query_rows.reshape(length, 1, channels), "seq", split_axis=0, concat_axis=1, tiled=True
        ),
        lax.all_to_all(
            gated_rows.reshape(length, 1, channels), "seq", split_axis=0, concat_axis=1, tiled=True
        ),
        lax.all_to_all(
            long_filter.reshape(length, 1, long_filter.shape[1]),
            "seq",
            split_axis=0,
            concat_axis=1,
            tiled=True,
        ),
    )
    coarse = jnp.arange(2 * panels, dtype=jnp.int32)
    cross_cos, cross_sin = unit_roots(coarse, jnp.arange(panels, dtype=jnp.int32), 2 * panels)
    fine_index = jnp.arange(length, dtype=jnp.int32)
    local_cos, local_sin = unit_roots(fine_index, fine_index, length)
    own_rows = my_panel * slice_len + jnp.arange(slice_len, dtype=jnp.int32)
    twist_cos, twist_sin = unit_roots(coarse, own_rows, points)
    own_bins = 2 * my_panel + jnp.arange(2, dtype=jnp.int32)
    turn_cos, turn_sin = unit_roots(own_bins, fine_index, points)
    pattern = "kr,mrc->kmc"
    tap_real, tap_imag = rotate(
        contract(pattern, cross_cos, filter_cols),
        contract(pattern, cross_sin, filter_cols),
        twist_cos[:, :, None],
        twist_sin[:, :, None],
    )
    act_real = contract(pattern, cross_cos, gated_cols)
    act_imag = contract(pattern, cross_sin, gated_cols)
    act_real, act_imag = rotate(act_real, act_imag, twist_cos[:, :, None], twist_sin[:, :, None])
    act_real, act_imag, tap_real, tap_imag = (
        lax.all_to_all(act_real, "seq", split_axis=0, concat_axis=1, tiled=True),
        lax.all_to_all(act_imag, "seq", split_axis=0, concat_axis=1, tiled=True),
        lax.all_to_all(tap_real, "seq", split_axis=0, concat_axis=1, tiled=True),
        lax.all_to_all(tap_imag, "seq", split_axis=0, concat_axis=1, tiled=True),
    )
    act_real, act_imag = fine_forward(local_cos, local_sin, act_real, act_imag)
    tap_real, tap_imag = fine_forward(local_cos, local_sin, tap_real, tap_imag)
    tap_real, tap_imag = (
        lax.all_gather(tap_real, "grp", axis=2, tiled=True),
        lax.all_gather(tap_imag, "grp", axis=2, tiled=True),
    )
    filter_count = tap_real.shape[2]
    blocks = act_real.shape[2] // filter_count
    wide_real = act_real.reshape(2, length, blocks, filter_count)
    wide_imag = act_imag.reshape(2, length, blocks, filter_count)
    tap_wide_real = tap_real[:, :, None, :]
    tap_wide_imag = tap_imag[:, :, None, :]
    prod_real = (wide_real * tap_wide_real - wide_imag * tap_wide_imag).reshape(
        2, length, blocks * filter_count
    )
    prod_imag = (wide_real * tap_wide_imag + wide_imag * tap_wide_real).reshape(
        2, length, blocks * filter_count
    )
    back_real, back_imag = fine_inverse(local_cos, local_sin, prod_real, prod_imag)
    back_real, back_imag = unrotate(
        back_real, back_imag, turn_cos[:, :, None], turn_sin[:, :, None]
    )
    back_real, back_imag = (
        lax.all_to_all(back_real, "seq", split_axis=1, concat_axis=0, tiled=True),
        lax.all_to_all(back_imag, "seq", split_axis=1, concat_axis=0, tiled=True),
    )
    inverse_scale = 1.0 / points
    inverse_pattern = "kr,kmc->mrc"
    convolved = (
        contract(inverse_pattern, cross_cos, back_real)
        + contract(inverse_pattern, cross_sin, back_imag)
    ) * inverse_scale
    return query_cols * (convolved + skip_gain * gated_cols)


def split16(values):
    high = values.astype(jnp.bfloat16)
    low = (values - high.astype(jnp.float32)).astype(jnp.bfloat16)
    return high, low


def transform_tables(length):
    bins = np.arange(length, dtype=np.int64)[:, None]
    taps = np.arange(length, dtype=np.int64)[None, :]
    phases = ((2 * bins + 1) * taps % (4 * length)).astype(np.float64) * (math.pi / (2 * length))
    table = np.concatenate([np.cos(phases), -np.sin(phases)], axis=0).astype(np.float32)
    high = table.astype(jnp.bfloat16)
    low = (table - high.astype(np.float32)).astype(jnp.bfloat16)
    forward = np.concatenate([high, high, low], axis=1)
    inverse = np.concatenate([high.T, high.T, low.T], axis=1)
    return forward, inverse


def tile_of(t):
    return slice(t * LANES, (t + 1) * LANES)


def later(now, before, rows):
    index = lax.broadcasted_iota(jnp.int32, now.shape, 0)
    return pltpu.roll(jnp.where(index >= ROWS - rows, before, now), rows, 0)


def short_filtered(taps, s, buffer, base, columns):
    now = buffer[pl.ds(base + ROWS, ROWS), columns]
    before = buffer[pl.ds(base, ROWS), columns]
    return (
        taps[s, 0:1, columns] * now
        + taps[s, 1:2, columns] * later(now, before, 1)
        + taps[s, 2:3, columns] * later(now, before, 2)
    )


def swap_tiles_and_slots(tiles, width):
    count = len(tiles)
    lane = lax.broadcasted_iota(jnp.int32, tiles[0].shape, tiles[0].ndim - 1)
    slot = lane // width % count
    step = 1
    while step < count:
        upper = (slot & step) != 0
        turned = list(tiles)
        for t in range(count):
            if t & step:
                continue
            low, high = tiles[t], tiles[t | step]
            shift = step * width
            turned[t] = jnp.where(upper, pltpu.roll(high, shift, high.ndim - 1), low)
            turned[t | step] = jnp.where(
                upper, high, pltpu.roll(low, LANES - shift, low.ndim - 1)
            )
        tiles = turned
        step *= 2
    return tiles


def gate_kernel(count, width, me_ref, streams, taps, skip, long_filter, *rest):
    messages, rest = rest[:count], rest[count:]
    params, filter_out, key, value, packed, packed_params, in_sems, out_sems = rest
    length = streams.shape[1]
    me = me_ref[0]
    pieces = in_sems.shape[0] // 2
    part = length // pieces
    loads = []
    for s, buffer in ((1, key), (2, value)):
        for piece in range(pieces):
            load = pltpu.make_async_copy(
                streams.at[s, pl.ds(piece * part, part)],
                buffer.at[pl.ds(ROWS + piece * part, part)],
                in_sems.at[(s - 1) * pieces + piece],
            )
            load.start()
            loads.append(load)
    key[0:ROWS, :] = jnp.zeros((ROWS, key.shape[1]), jnp.float32)
    value[0:ROWS, :] = jnp.zeros((ROWS, key.shape[1]), jnp.float32)
    transposed = long_filter[...].T
    for j in range(count):
        filter_out[j] = transposed[j * width : (j + 1) * width, :]
    rows = jnp.concatenate(
        [taps[1], taps[2], skip[...], jnp.zeros((1, key.shape[1]), jnp.float32)], axis=0
    )
    own = swap_tiles_and_slots([rows[:, tile_of(t)] for t in range(count)], width)
    for j in range(count):
        packed_params[j] = own[j]
    params_copy = pltpu.make_async_copy(packed_params.at[me], params, out_sems.at[count])
    params_copy.start()

    def block(i, _):
        base = pl.multiple_of(i * ROWS, ROWS)
        tiles = []
        for t in range(count):
            tiles.append(
                short_filtered(taps, 1, key, base, tile_of(t))
                * short_filtered(taps, 2, value, base, tile_of(t))
            )
        tiles = swap_tiles_and_slots(tiles, width)
        for j in range(count):
            packed[j, pl.ds(base, ROWS), :] = tiles[j]
        return 0

    per_piece = part // ROWS
    for piece in range(pieces):
        loads[piece].wait()
        loads[pieces + piece].wait()
        lax.fori_loop(piece * per_piece, (piece + 1) * per_piece, block, 0)
    rim = jnp.concatenate(
        [
            key[length + ROWS - 2 : length + ROWS, :],
            value[length + ROWS - 2 : length + ROWS, :],
            key[ROWS : ROWS + 2, :],
            value[ROWS : ROWS + 2, :],
        ],
        axis=0,
    )
    rim = swap_tiles_and_slots([rim[:, tile_of(t)] for t in range(count)], width)
    for j in range(count):
        packed[j, length : length + ROWS, :] = rim[j]
    stores = []
    for k in range(count):
        store = pltpu.make_async_copy(packed.at[me ^ k], messages[k], out_sems.at[k])
        store.start()
        stores.append(store)
    params_copy.wait()
    for store in stores:
        store.wait()


def gate(me, streams, short_filters, skip_gain, long_filter, count, width):
    length, channels = streams.shape[1], streams.shape[2]
    message = jax.ShapeDtypeStruct((length + ROWS, LANES), jnp.float32)
    whole = pl.BlockSpec(memory_space=pltpu.VMEM)
    outside = pl.BlockSpec(memory_space=pl.ANY)
    pieces = 4
    return pl.pallas_call(
        functools.partial(gate_kernel, count, width),
        out_shape=[message] * count
        + [
            jax.ShapeDtypeStruct((ROWS, LANES), jnp.float32),
            jax.ShapeDtypeStruct((count, width, length), jnp.float32),
        ],
        in_specs=[
            pl.BlockSpec(memory_space=pltpu.SMEM),
            outside,
            whole,
            whole,
            whole,
        ],
        out_specs=[outside] * (count + 1) + [whole],
        scratch_shapes=[
            pltpu.VMEM((length + ROWS, channels), jnp.float32),
            pltpu.VMEM((length + ROWS, channels), jnp.float32),
            pltpu.VMEM((count, length + ROWS, LANES), jnp.float32),
            pltpu.VMEM((count, ROWS, LANES), jnp.float32),
            pltpu.SemaphoreType.DMA((2 * pieces,)),
            pltpu.SemaphoreType.DMA((count + 1,)),
        ],
        compiler_params=pltpu.CompilerParams(vmem_limit_bytes=VMEM_BYTES),
        name="gate",
    )(me, streams, short_filters, skip_gain.reshape(1, channels), long_filter)


def query_kernel(streams, rim, taps, out, extended, sem):
    length = streams.shape[1]
    part = out.shape[2]
    load = pltpu.make_async_copy(streams.at[0], extended.at[pl.ds(ROWS, length)], sem)
    load.start()
    extended[ROWS - 2 : ROWS, :] = rim[...]
    load.wait()

    def block(i, _):
        base = pl.multiple_of(i * ROWS, ROWS)
        at = pl.multiple_of(base % part, ROWS)
        for t in range(out.shape[1]):
            out[base // part, t, pl.ds(at, ROWS), :] = short_filtered(
                taps, 0, extended, base, tile_of(t)
            )
        return 0

    lax.fori_loop(0, length // ROWS, block, 0)


def query(streams, rim, short_filters, count):
    length, channels = streams.shape[1], streams.shape[2]
    whole = pl.BlockSpec(memory_space=pltpu.VMEM)
    return pl.pallas_call(
        query_kernel,
        out_shape=jax.ShapeDtypeStruct(
            (count, channels // LANES, length // count, LANES), jnp.float32
        ),
        in_specs=[pl.BlockSpec(memory_space=pl.ANY), whole, whole],
        out_specs=whole,
        scratch_shapes=[
            pltpu.VMEM((length + ROWS, channels), jnp.float32),
            pltpu.SemaphoreType.DMA,
        ],
        compiler_params=pltpu.CompilerParams(vmem_limit_bytes=VMEM_BYTES),
        name="query",
    )(streams, rim, short_filters)


def filter_kernel(count, width, gathered, forward, out, columns, spectrum):
    length = gathered.shape[-1]
    halves = LANES // (count * width)
    for p in range(count):
        for h in range(halves):
            for t in range(count):
                owner = (t * halves + h) % gathered.shape[0]
                at = (h * count + t) * width
                columns[at : at + width, :] = gathered[owner, p]
        high, low = split16(columns[...])
        stacked = jnp.concatenate([high, low, high], axis=1)
        spectrum[p] = lax.dot_general(
            forward[...], stacked, (((1,), (1,)), ((), ())), preferred_element_type=jnp.float32
        )
    parity = lax.broadcasted_iota(jnp.int32, (length, LANES), 0) % 2
    sign = 1.0 - 2.0 * parity.astype(jnp.float32)
    for d in range(count):
        real = spectrum[d, 0:length, :]
        imag = spectrum[d, length : 2 * length, :]
        if d > 0:
            real = real - sign * spectrum[d - 1, length : 2 * length, :]
            imag = imag + sign * spectrum[d - 1, 0:length, :]
        out[d, 0:length, :] = real
        out[d, length : 2 * length, :] = imag


def filter_spectra(gathered, forward, count, width):
    length = gathered.shape[-1]
    whole = pl.BlockSpec(memory_space=pltpu.VMEM)
    return pl.pallas_call(
        functools.partial(filter_kernel, count, width),
        out_shape=jax.ShapeDtypeStruct((count, 2 * length, LANES), jnp.float32),
        in_specs=[whole, whole],
        out_specs=whole,
        scratch_shapes=[
            pltpu.VMEM((LANES, length), jnp.float32),
            pltpu.VMEM((count, 2 * length, LANES), jnp.float32),
        ],
        compiler_params=pltpu.CompilerParams(vmem_limit_bytes=VMEM_BYTES),
        name="filter_spectra",
    )(gathered, forward)


def convolve_kernel(count, me_ref, params, forward, inverse, spectra, *rest):
    messages, rest = rest[:count], rest[count:]
    outs, rest = rest[:count], rest[count:]
    gated, kernel_bins, bins, halves, result, in_sems, out_sems = rest
    length = gated.shape[1] - ROWS
    me = me_ref[0]
    loads = []
    for k in range(count):
        load = pltpu.make_async_copy(messages[k], gated.at[me ^ k], in_sems.at[k])
        load.start()
        loads.append(load)
    spectra_load = pltpu.make_async_copy(spectra, kernel_bins, in_sems.at[count])
    spectra_load.start()
    for load in loads:
        load.wait()
    key_taps = [params[a : a + 1, :] for a in range(3)]
    value_taps = [params[3 + a : 4 + a, :] for a in range(3)]
    skip = params[6:7, :]

    def feature(taps, now, before, earlier):
        return taps[0] * now + taps[1] * before + taps[2] * earlier

    for p in range(count):
        rim = gated[p, length : length + ROWS, :]
        if p == 0:
            past = jnp.zeros((ROWS, LANES), jnp.float32)
        else:
            past = gated[p - 1, length : length + ROWS, :]
        k254, k255, v254, v255 = (past[a : a + 1, :] for a in range(4))
        k0, k1, v0, v1 = (rim[4 + a : 5 + a, :] for a in range(4))
        gated[p, 0:1, :] = feature(key_taps, k0, k255, k254) * feature(value_taps, v0, v255, v254)
        gated[p, 1:2, :] = feature(key_taps, k1, k0, k255) * feature(value_taps, v1, v0, v255)
    for p in range(count):
        high, low = split16(gated[p, 0:length, :])
        halves[0:length, tile_of(p)] = high
        halves[length : 2 * length, tile_of(p)] = low
        halves[2 * length : 3 * length, tile_of(p)] = high
    bins[...] = jnp.dot(
        forward[...], halves[0 : 3 * length, :], preferred_element_type=jnp.float32
    )
    spectra_load.wait()

    def block(i, _):
        rows = []
        for half in range(2):
            at = pl.multiple_of(i * 2 * ROWS, 2 * ROWS) + half * ROWS
            real = [bins[pl.ds(at, ROWS), tile_of(r)] for r in range(count)]
            imag = [bins[pl.ds(length + at, ROWS), tile_of(r)] for r in range(count)]
            tap_real = [kernel_bins[d, pl.ds(at, ROWS), :] for d in range(count)]
            tap_imag = [kernel_bins[d, pl.ds(length + at, ROWS), :] for d in range(count)]
            sums = []
            for r in range(count):
                sum_real = real[r] * tap_real[0] - imag[r] * tap_imag[0]
                sum_imag = real[r] * tap_imag[0] + imag[r] * tap_real[0]
                for d in range(1, r + 1):
                    sum_real += real[r - d] * tap_real[d] - imag[r - d] * tap_imag[d]
                    sum_imag += real[r - d] * tap_imag[d] + imag[r - d] * tap_real[d]
                sums.append((sum_real, sum_imag))
            rows.append(sums)
        at = pl.multiple_of(i * 2 * ROWS, 2 * ROWS)
        for r in range(count):
            for part in range(2):
                both = jnp.concatenate([rows[0][r][part], rows[1][r][part]], axis=0)
                high, low = split16(both)
                base = at + part * length
                halves[pl.ds(base, 2 * ROWS), tile_of(r)] = high
                halves[pl.ds(base + 2 * length, 2 * ROWS), tile_of(r)] = low
                halves[pl.ds(base + 4 * length, 2 * ROWS), tile_of(r)] = high
        return 0

    lax.fori_loop(0, length // (2 * ROWS), block, 0)
    scale = 1.0 / length
    part = length // count
    for p in range(count):
        own = jnp.dot(
            inverse[p * part : (p + 1) * part, :],
            halves[...],
            preferred_element_type=jnp.float32,
        )
        for r in range(count):
            result[p, r] = own[:, tile_of(r)] * scale + skip * gated[r, p * part : (p + 1) * part, :]
    stores = []
    for k in range(count):
        store = pltpu.make_async_copy(result.at[me ^ k], outs[k], out_sems.at[k])
        store.start()
        stores.append(store)
    for store in stores:
        store.wait()


def convolve(me, params, forward, inverse, spectra, messages, count):
    length = messages[0].shape[0] - ROWS
    part = length // count
    whole = pl.BlockSpec(memory_space=pltpu.VMEM)
    outside = pl.BlockSpec(memory_space=pl.ANY)
    return pl.pallas_call(
        functools.partial(convolve_kernel, count),
        out_shape=[jax.ShapeDtypeStruct((count, part, LANES), jnp.float32)] * count,
        in_specs=[pl.BlockSpec(memory_space=pltpu.SMEM), whole, whole, whole, outside]
        + [outside] * count,
        out_specs=[outside] * count,
        scratch_shapes=[
            pltpu.VMEM((count, length + ROWS, LANES), jnp.float32),
            pltpu.VMEM((count, 2 * length, LANES), jnp.float32),
            pltpu.VMEM((2 * length, count * LANES), jnp.float32),
            pltpu.VMEM((6 * length, count * LANES), jnp.bfloat16),
            pltpu.VMEM((count, count, part, LANES), jnp.float32),
            pltpu.SemaphoreType.DMA((count + 1,)),
            pltpu.SemaphoreType.DMA((count,)),
        ],
        compiler_params=pltpu.CompilerParams(vmem_limit_bytes=VMEM_BYTES),
        name="convolve",
    )(me, params, forward, inverse, spectra, *messages)


def finish_kernel(count, width, me_ref, query_rows, *rest):
    messages, rest = rest[:count], rest[count:]
    out, homes, sems = rest
    part = out.shape[0]
    me = me_ref[0]
    loads = []
    for k in range(count):
        load = pltpu.make_async_copy(messages[k], homes.at[me ^ k], sems.at[k])
        load.start()
        loads.append(load)
    for load in loads:
        load.wait()

    def row(m, _):
        tiles = [homes[j, pl.ds(m, count, stride=part), :] for j in range(count)]
        tiles = swap_tiles_and_slots(tiles, width)
        for t in range(count):
            out[m, :, tile_of(t)] = (
                query_rows[pl.ds(t * part + m, count, stride=count * part), :] * tiles[t]
            )
        return 0

    lax.fori_loop(0, part, row, 0)


def finish(me, query_rows, messages, count, width):
    part = messages[0].shape[0] // count
    channels = query_rows.size // (count * part)
    whole = pl.BlockSpec(memory_space=pltpu.VMEM)
    outside = pl.BlockSpec(memory_space=pl.ANY)
    return pl.pallas_call(
        functools.partial(finish_kernel, count, width),
        out_shape=jax.ShapeDtypeStruct((part, count, channels), jnp.float32),
        in_specs=[pl.BlockSpec(memory_space=pltpu.SMEM), whole] + [outside] * count,
        out_specs=whole,
        scratch_shapes=[
            pltpu.VMEM((count, count * part, LANES), jnp.float32),
            pltpu.SemaphoreType.DMA((count,)),
        ],
        compiler_params=pltpu.CompilerParams(vmem_limit_bytes=VMEM_BYTES),
        name="finish",
    )(me, query_rows, *messages)


def exchanged(messages):
    count = len(messages)
    half = count // 2
    order = list(range(half, count)) + list(range(half - 1, 0, -1))
    received = {0: messages[0]}
    for k in order:
        received[k] = lax.ppermute(messages[k], "seq", [(i, i ^ k) for i in range(count)])
    return [received[k] for k in range(count)]


def wide_body(streams, short_filters, skip_gain, long_filter):
    count = lax.axis_size("seq")
    me = lax.axis_index("seq").astype(jnp.int32).reshape(1)
    length = streams.shape[1]
    width = long_filter.shape[1] // count
    forward, inverse = (jnp.asarray(table) for table in transform_tables(length))
    rim = passed_along(streams[0, length - 2 :, :], "seq", 1)
    *gated, params, taps = gate(
        me, streams, short_filters, skip_gain, long_filter, count, width
    )
    gated = exchanged(gated)
    taps = lax.all_to_all(taps, "seq", split_axis=0, concat_axis=0, tiled=True)
    taps = lax.all_gather(taps, "grp", axis=0, tiled=False)
    query_rows = query(streams, rim, short_filters, count)
    query_rows = lax.all_to_all(query_rows, "seq", split_axis=0, concat_axis=0, tiled=True)
    spectra = filter_spectra(taps, forward, count, width)
    convolved = convolve(me, params, forward, inverse, spectra, gated, count)
    convolved = exchanged(convolved)
    part = length // count
    return finish(
        me,
        query_rows.reshape(-1, LANES),
        [block.reshape(count * part, LANES) for block in convolved],
        count,
        width,
    )


def body(streams, short_filters, skip_gain, long_filter):
    count = lax.axis_size("seq")
    width = long_filter.shape[1] // count
    one_tile = streams.shape[2] == count * LANES and count == ROWS
    if one_tile and width % ROWS == 0 and LANES % (count * width) == 0:
        return wide_body(streams, short_filters, skip_gain, long_filter)
    return narrow_body(streams, short_filters, skip_gain, long_filter)


def solution(mesh):
    return jax.shard_map(
        body,
        mesh=mesh,
        in_specs=(P(None, "seq", "grp"), P(None, None, "grp"), P("grp"), P("seq", "grp")),
        out_specs=P("seq", None, "grp"),
        check_vma=False,
    )
```

```python
import functools
import math

import jax
import jax.numpy as jnp
import numpy as np
from jax import lax
from jax.experimental import pallas as pl
from jax.experimental.pallas import tpu as pltpu
from jax.sharding import PartitionSpec as P

LANES = 128
ROWS = 8
VMEM_BYTES = 40 * 1024 * 1024


def passed_along(block, axis, distance):
    devices = range(lax.axis_size(axis))
    route = [(i - distance, i) for i in devices if i - distance in devices]
    return lax.ppermute(block, axis, route)


def contract(pattern, matrix, values):
    return jnp.einsum(pattern, matrix, values, precision=lax.Precision.HIGHEST)


def unit_roots(row_index, col_index, period):
    phase_steps = row_index[:, None] * col_index[None, :] % period
    phases = -2.0 * math.pi / period * phase_steps.astype(jnp.float32)
    return (jnp.cos(phases), jnp.sin(phases))


def rotate(real_part, imag_part, cos_part, sin_part):
    return (
        real_part * cos_part - imag_part * sin_part,
        real_part * sin_part + imag_part * cos_part,
    )


def unrotate(real_part, imag_part, cos_part, sin_part):
    return (
        real_part * cos_part + imag_part * sin_part,
        imag_part * cos_part - real_part * sin_part,
    )


def fine_forward(cos_table, sin_table, real_part, imag_part):
    pattern = "km,imc->ikc"
    return (
        contract(pattern, cos_table, real_part) - contract(pattern, sin_table, imag_part),
        contract(pattern, cos_table, imag_part) + contract(pattern, sin_table, real_part),
    )


def fine_inverse(cos_table, sin_table, real_part, imag_part):
    pattern = "km,ikc->imc"
    return (
        contract(pattern, cos_table, real_part) + contract(pattern, sin_table, imag_part),
        contract(pattern, cos_table, imag_part) - contract(pattern, sin_table, real_part),
    )


def narrow_body(streams, short_filters, skip_gain, long_filter):
    panels = lax.axis_size("seq")
    my_panel = lax.axis_index("seq")
    length = streams.shape[1]
    channels = streams.shape[2]
    slice_len = length // panels
    points = 2 * panels * length
    rim_rows = passed_along(streams[:, length - 2 :, :], "seq", 1)
    extended = jnp.concatenate([rim_rows, streams], axis=1)
    featured = (
        short_filters[:, 0:1, :] * extended[:, 2:, :]
        + short_filters[:, 1:2, :] * extended[:, 1 : length + 1, :]
        + short_filters[:, 2:3, :] * extended[:, 0:length, :]
    )
    query_rows = featured[0]
    gated_rows = featured[1] * featured[2]
    query_cols, gated_cols, filter_cols = (
        lax.all_to_all(
            query_rows.reshape(length, 1, channels), "seq", split_axis=0, concat_axis=1, tiled=True
        ),
        lax.all_to_all(
            gated_rows.reshape(length, 1, channels), "seq", split_axis=0, concat_axis=1, tiled=True
        ),
        lax.all_to_all(
            long_filter.reshape(length, 1, long_filter.shape[1]),
            "seq",
            split_axis=0,
            concat_axis=1,
            tiled=True,
        ),
    )
    coarse = jnp.arange(2 * panels, dtype=jnp.int32)
    cross_cos, cross_sin = unit_roots(coarse, jnp.arange(panels, dtype=jnp.int32), 2 * panels)
    fine_index = jnp.arange(length, dtype=jnp.int32)
    local_cos, local_sin = unit_roots(fine_index, fine_index, length)
    own_rows = my_panel * slice_len + jnp.arange(slice_len, dtype=jnp.int32)
    twist_cos, twist_sin = unit_roots(coarse, own_rows, points)
    own_bins = 2 * my_panel + jnp.arange(2, dtype=jnp.int32)
    turn_cos, turn_sin = unit_roots(own_bins, fine_index, points)
    pattern = "kr,mrc->kmc"
    tap_real, tap_imag = rotate(
        contract(pattern, cross_cos, filter_cols),
        contract(pattern, cross_sin, filter_cols),
        twist_cos[:, :, None],
        twist_sin[:, :, None],
    )
    act_real = contract(pattern, cross_cos, gated_cols)
    act_imag = contract(pattern, cross_sin, gated_cols)
    act_real, act_imag = rotate(act_real, act_imag, twist_cos[:, :, None], twist_sin[:, :, None])
    act_real, act_imag, tap_real, tap_imag = (
        lax.all_to_all(act_real, "seq", split_axis=0, concat_axis=1, tiled=True),
        lax.all_to_all(act_imag, "seq", split_axis=0, concat_axis=1, tiled=True),
        lax.all_to_all(tap_real, "seq", split_axis=0, concat_axis=1, tiled=True),
        lax.all_to_all(tap_imag, "seq", split_axis=0, concat_axis=1, tiled=True),
    )
    act_real, act_imag = fine_forward(local_cos, local_sin, act_real, act_imag)
    tap_real, tap_imag = fine_forward(local_cos, local_sin, tap_real, tap_imag)
    tap_real, tap_imag = (
        lax.all_gather(tap_real, "grp", axis=2, tiled=True),
        lax.all_gather(tap_imag, "grp", axis=2, tiled=True),
    )
    filter_count = tap_real.shape[2]
    blocks = act_real.shape[2] // filter_count
    wide_real = act_real.reshape(2, length, blocks, filter_count)
    wide_imag = act_imag.reshape(2, length, blocks, filter_count)
    tap_wide_real = tap_real[:, :, None, :]
    tap_wide_imag = tap_imag[:, :, None, :]
    prod_real = (wide_real * tap_wide_real - wide_imag * tap_wide_imag).reshape(
        2, length, blocks * filter_count
    )
    prod_imag = (wide_real * tap_wide_imag + wide_imag * tap_wide_real).reshape(
        2, length, blocks * filter_count
    )
    back_real, back_imag = fine_inverse(local_cos, local_sin, prod_real, prod_imag)
    back_real, back_imag = unrotate(
        back_real, back_imag, turn_cos[:, :, None], turn_sin[:, :, None]
    )
    back_real, back_imag = (
        lax.all_to_all(back_real, "seq", split_axis=1, concat_axis=0, tiled=True),
        lax.all_to_all(back_imag, "seq", split_axis=1, concat_axis=0, tiled=True),
    )
    inverse_scale = 1.0 / points
    inverse_pattern = "kr,kmc->mrc"
    convolved = (
        contract(inverse_pattern, cross_cos, back_real)
        + contract(inverse_pattern, cross_sin, back_imag)
    ) * inverse_scale
    return query_cols * (convolved + skip_gain * gated_cols)


def split16(values):
    high = values.astype(jnp.bfloat16)
    low = (values - high.astype(jnp.float32)).astype(jnp.bfloat16)
    return high, low


def transform_tables(length):
    bins = np.arange(length, dtype=np.int64)[:, None]
    taps = np.arange(length, dtype=np.int64)[None, :]
    phases = ((2 * bins + 1) * taps % (4 * length)).astype(np.float64) * (math.pi / (2 * length))
    table = np.concatenate([np.cos(phases), -np.sin(phases)], axis=0).astype(np.float32)
    high = table.astype(jnp.bfloat16)
    low = (table - high.astype(np.float32)).astype(jnp.bfloat16)
    forward = np.concatenate([high, high, low], axis=1)
    inverse = np.concatenate([high.T, high.T, low.T], axis=1)
    return forward, inverse


def tile_of(t):
    return slice(t * LANES, (t + 1) * LANES)


def aligned(start, size):
    return pl.ds(pl.multiple_of(start, size), size)


def swap_tiles_and_slots(tiles, width, me, tiles_out):
    count = len(tiles)
    lane = lax.broadcasted_iota(jnp.int32, tiles[0].shape, 1)
    slot = lane // width % count
    mine = slot ^ me
    step = 1
    while step < count:
        upper = (slot & step) != 0
        other = (mine & step) != 0
        first, second = (upper, other) if tiles_out else (other, upper)
        partner = lane ^ (step * width)
        turned = list(tiles)
        for t in range(count):
            if t & step:
                continue
            low, high = tiles[t], tiles[t | step]
            moved = jnp.take_along_axis(jnp.where(first, low, high), partner, axis=1)
            kept = jnp.where(first, high, low)
            turned[t] = jnp.where(second, moved, kept)
            turned[t | step] = jnp.where(second, kept, moved)
        tiles = turned
        step *= 2
    return tiles


def short_filtered(taps, s, columns, now, before):
    shape = now.shape
    row = lax.broadcasted_iota(jnp.int32, shape, 0) % ROWS

    def later(rows):
        mixed = jnp.where(row >= ROWS - rows, before, now)
        blocks = mixed.reshape(shape[0] // ROWS, ROWS, shape[1])
        return pltpu.roll(blocks, rows, 1).reshape(shape)

    return (
        taps[s, 0:1, columns] * now
        + taps[s, 1:2, columns] * later(1)
        + taps[s, 2:3, columns] * later(2)
    )


def in_vmem():
    return pl.BlockSpec(memory_space=pltpu.VMEM)


def in_smem():
    return pl.BlockSpec(memory_space=pltpu.SMEM)


def in_any():
    return pl.BlockSpec(memory_space=pl.ANY)


def params_of(limit=VMEM_BYTES):
    return pltpu.CompilerParams(vmem_limit_bytes=limit)


def far_first(count):
    half = count // 2
    return [half, half + 1] + list(range(half)) + list(range(half + 2, count))


def by_partner(refs):
    ordered = [None] * len(refs)
    for k, ref in zip(far_first(len(refs)), refs):
        ordered[k] = ref
    return ordered


def far_first_operands(messages):
    return [messages[k] for k in far_first(len(messages))]


def gate_kernel(count, width, pieces, me_ref, streams, *rest):
    small, rest = rest[:3], rest[3:]
    messages, rest = rest[:count], rest[count:]
    params, key, value, taps, skip, long_filter, sems = rest
    length = streams.shape[1]
    fetches = [
        pltpu.make_async_copy(source, target, sems.at[2 * pieces + i])
        for i, (source, target) in enumerate(zip(small, (taps, skip, long_filter)))
    ]
    for fetch in fetches:
        fetch.start()
    channels = streams.shape[2]
    me = me_ref[0]
    part = length // pieces
    loads = []
    for piece in range(pieces):
        for s, buffer in ((1, key), (2, value)):
            load = pltpu.make_async_copy(
                streams.at[s, pl.ds(piece * part, part)],
                buffer.at[pl.ds(ROWS + piece * part, part)],
                sems.at[2 * piece + s - 1],
            )
            load.start()
            loads.append(load)
    key[0:ROWS, :] = jnp.zeros((ROWS, channels), jnp.float32)
    value[0:ROWS, :] = jnp.zeros((ROWS, channels), jnp.float32)
    for fetch in fetches:
        fetch.wait()
    rows = jnp.concatenate(
        [taps[1], taps[2], skip[...], jnp.zeros((1, channels), jnp.float32)], axis=0
    )
    tiles = [rows[:, tile_of(t)] for t in range(count)]
    params[...] = swap_tiles_and_slots(tiles, width, me, True)[0]
    for k in range(count):
        for t in range(length // LANES):
            at = length + ROWS + t * width
            messages[k][at : at + width, :] = long_filter[aligned((me ^ k) * width, width), tile_of(t)]
    step = 8 * ROWS

    def block(i, _):
        base = i * step
        tiles = []
        for t in range(count):
            features = []
            for s, buffer in ((1, key), (2, value)):
                now = buffer[pl.ds(pl.multiple_of(base + ROWS, ROWS), step), tile_of(t)]
                before = buffer[aligned(base, step), tile_of(t)]
                features.append(short_filtered(taps, s, tile_of(t), now, before))
            tiles.append(features[0] * features[1])
        tiles = swap_tiles_and_slots(tiles, width, me, True)
        for k in range(count):
            messages[k][aligned(base, step), :] = tiles[k]
        return 0

    for piece in range(pieces):
        loads[2 * piece].wait()
        loads[2 * piece + 1].wait()
        lax.fori_loop(piece * part // step, (piece + 1) * part // step, block, 0)
    rim = jnp.concatenate(
        [
            key[length + ROWS - 2 : length + ROWS, :],
            value[length + ROWS - 2 : length + ROWS, :],
            key[ROWS : ROWS + 2, :],
            value[ROWS : ROWS + 2, :],
        ],
        axis=0,
    )
    tiles = [rim[:, tile_of(t)] for t in range(count)]
    tiles = swap_tiles_and_slots(tiles, width, me, True)
    for k in range(count):
        messages[k][length : length + ROWS, :] = tiles[k]


def gate(me, streams, short_filters, skip_gain, long_filter, count, width):
    length, channels = streams.shape[1], streams.shape[2]
    rows = length + ROWS + width * length // LANES
    message = jax.ShapeDtypeStruct((rows, LANES), jnp.float32)
    pieces = 4
    return pl.pallas_call(
        functools.partial(gate_kernel, count, width, pieces),
        out_shape=[message] * count + [jax.ShapeDtypeStruct((ROWS, LANES), jnp.float32)],
        in_specs=[in_smem()] + [in_any()] * 4,
        out_specs=[in_vmem()] * (count + 1),
        scratch_shapes=[
            pltpu.VMEM((length + ROWS, channels), jnp.float32),
            pltpu.VMEM((length + ROWS, channels), jnp.float32),
            pltpu.VMEM(short_filters.shape, jnp.float32),
            pltpu.VMEM((1, channels), jnp.float32),
            pltpu.VMEM(long_filter.shape[::-1], jnp.float32),
            pltpu.SemaphoreType.DMA((2 * pieces + 3,)),
        ],
        compiler_params=params_of(60 * 1024 * 1024),
        name="gate",
    )(me, streams, short_filters, skip_gain.reshape(1, channels), long_filter.T)


def collect_kernel(count, width, me_ref, *rest):
    messages, out = by_partner(rest[:count]), rest[count]
    me = me_ref[0]
    size = out.shape[1]
    for k in range(count):
        rows = messages[k].shape[0]
        out[me ^ k] = messages[k][rows - size : rows, :]


def collect_taps(me, messages, count, width, length):
    size = width * length // LANES
    return pl.pallas_call(
        functools.partial(collect_kernel, count, width),
        out_shape=jax.ShapeDtypeStruct((count, size, LANES), jnp.float32),
        in_specs=[in_smem()] + [in_vmem()] * count,
        out_specs=in_vmem(),
        compiler_params=params_of(),
        name="collect_taps",
    )(me, *far_first_operands(messages))


def filter_kernel(count, width, group_ref, params, forward, *rest):
    groups = len(rest) - 3
    taps, (out, columns, spectrum) = rest[:groups], rest[groups:]
    length = out.shape[1] // 2
    halves = LANES // (count * width)
    group = group_ref[0]
    for p in range(count):
        for k in range(groups):
            owner = group ^ k
            for turn in range(count * halves // groups):
                at = (owner + turn * groups) // halves + (owner % halves) * count
                for t in range(length // LANES):
                    columns[p, aligned(at * width, width), tile_of(t)] = taps[k][
                        p, t * width : (t + 1) * width, :
                    ]
    for p in range(count):
        high, low = split16(columns[p])
        stacked = jnp.concatenate([high, low, high], axis=1)
        spectrum[p] = lax.dot_general(
            forward[...], stacked, (((1,), (1,)), ((), ())), preferred_element_type=jnp.float32
        )
    parity = lax.broadcasted_iota(jnp.int32, (length, LANES), 0) % 2
    sign = 1.0 - 2.0 * parity.astype(jnp.float32)
    skip = params[6:7, :]
    for d in range(count):
        real = spectrum[d, 0:length, :]
        imag = spectrum[d, length : 2 * length, :]
        if d > 0:
            real = real - sign * spectrum[d - 1, length : 2 * length, :]
            imag = imag + sign * spectrum[d - 1, 0:length, :]
        else:
            real = real + skip
        out[d, 0:length, :] = real
        out[d, length : 2 * length, :] = imag


def filter_spectra(group, params, forward, taps, count, width):
    length = taps[0].shape[1] // width * LANES
    return pl.pallas_call(
        functools.partial(filter_kernel, count, width),
        out_shape=jax.ShapeDtypeStruct((count, 2 * length, LANES), jnp.float32),
        in_specs=[in_smem()] + [in_vmem()] * (2 + len(taps)),
        out_specs=in_vmem(),
        scratch_shapes=[
            pltpu.VMEM((count, LANES, length), jnp.float32),
            pltpu.VMEM((count, 2 * length, LANES), jnp.float32),
        ],
        compiler_params=params_of(),
        name="filter_spectra",
    )(group, params, forward, *taps)


def convolve_kernel(count, length, me_ref, params, forward, inverse, spectra, *rest):
    messages, rest = by_partner(rest[:count]), rest[count:]
    outs, rest = rest[:count], rest[count:]
    rims, bins, halves, result = rest
    me = me_ref[0]
    rims[0] = jnp.zeros((ROWS, LANES), jnp.float32)
    for k in range(count):
        rims[(me ^ k) + 1] = messages[k][length : length + ROWS, :]
    key_taps = [params[a : a + 1, :] for a in range(3)]
    value_taps = [params[3 + a : 4 + a, :] for a in range(3)]

    def feature(taps, now, before, earlier):
        return taps[0] * now + taps[1] * before + taps[2] * earlier

    pair = 2 * ROWS
    row = lax.broadcasted_iota(jnp.int32, (pair, LANES), 0)
    for k in range(count):
        at = aligned((me ^ k) * LANES, LANES)
        past = rims[me ^ k]
        rim = messages[k][length : length + ROWS, :]
        k254, k255, v254, v255 = (past[a : a + 1, :] for a in range(4))
        k0, k1, v0, v1 = (rim[4 + a : 5 + a, :] for a in range(4))
        first = feature(key_taps, k0, k255, k254) * feature(value_taps, v0, v255, v254)
        second = feature(key_taps, k1, k0, k255) * feature(value_taps, v1, v0, v255)
        top = jnp.where(row == 0, first, jnp.where(row == 1, second, messages[k][0:pair, :]))
        for a, b, values in ((0, pair, top), (pair, length, messages[k][pair:length, :])):
            high, low = split16(values)
            halves[a:b, at] = high
            halves[length + a : length + b, at] = low
            halves[2 * length + a : 2 * length + b, at] = high
    for c in range(0, count, 2):
        columns = slice(c * LANES, (c + 2) * LANES)
        bins[:, columns] = jnp.dot(
            forward[...], halves[0 : 3 * length, columns], preferred_element_type=jnp.float32
        )

    def block(i, _):
        start = pl.multiple_of(i * pair, pair)
        rows = []
        for at in (start, start + ROWS):
            real = [bins[pl.ds(at, ROWS), tile_of(r)] for r in range(count)]
            imag = [bins[pl.ds(length + at, ROWS), tile_of(r)] for r in range(count)]
            tap_real = [spectra[d, pl.ds(at, ROWS), :] for d in range(count)]
            tap_imag = [spectra[d, pl.ds(length + at, ROWS), :] for d in range(count)]
            sums = []
            for r in range(count):
                sum_real = real[r] * tap_real[0] - imag[r] * tap_imag[0]
                sum_imag = real[r] * tap_imag[0] + imag[r] * tap_real[0]
                for d in range(1, r + 1):
                    sum_real += real[r - d] * tap_real[d] - imag[r - d] * tap_imag[d]
                    sum_imag += real[r - d] * tap_imag[d] + imag[r - d] * tap_real[d]
                sums.append((sum_real, sum_imag))
            rows.append(sums)
        for r in range(count):
            for part in range(2):
                both = jnp.concatenate([rows[0][r][part], rows[1][r][part]], axis=0)
                high, low = split16(both)
                base = start + part * length
                halves[pl.ds(base, pair), tile_of(r)] = high
                halves[pl.ds(base + 2 * length, pair), tile_of(r)] = low
                halves[pl.ds(base + 4 * length, pair), tile_of(r)] = high
        return 0

    lax.fori_loop(0, length // pair, block, 0)
    for c in range(0, count, 2):
        columns = slice(c * LANES, (c + 2) * LANES)
        result[:, columns] = jnp.dot(
            inverse[...], halves[:, columns], preferred_element_type=jnp.float32
        )
    scale = 1.0 / length
    part = length // count
    for k in range(count):
        for m in range(0, part, ROWS):
            for r in range(count):
                outs[k][pl.ds(m * count + r, ROWS, stride=count), :] = (
                    result[aligned((me ^ k) * part + m, ROWS), tile_of(r)] * scale
                )


def convolve(me, params, forward, inverse, spectra, messages, count):
    length = spectra.shape[1] // 2
    return pl.pallas_call(
        functools.partial(convolve_kernel, count, length),
        out_shape=[jax.ShapeDtypeStruct((length, LANES), jnp.float32)] * count,
        in_specs=[in_smem()] + [in_vmem()] * (4 + count),
        out_specs=[in_vmem()] * count,
        scratch_shapes=[
            pltpu.VMEM((count + 1, ROWS, LANES), jnp.float32),
            pltpu.VMEM((2 * length, count * LANES), jnp.float32),
            pltpu.VMEM((6 * length, count * LANES), jnp.bfloat16),
            pltpu.VMEM((length, count * LANES), jnp.float32),
        ],
        compiler_params=params_of(),
        name="convolve",
    )(me, params, forward, inverse, spectra, *far_first_operands(messages))


def query_kernel(half, me_ref, streams, taps_in, _, near, far, rows, taps, sems):
    length, channels = streams.shape[1:]
    tiles = channels // LANES
    load = pltpu.make_async_copy(streams.at[0], rows.at[pl.ds(ROWS, length)], sems.at[0])
    fetch = pltpu.make_async_copy(taps_in, taps, sems.at[1])
    load.start()
    fetch.start()
    rows[0:ROWS, :] = jnp.zeros((ROWS, channels), jnp.float32)
    side = me_ref[0] // half
    fetch.wait()
    load.wait()
    step = length // (2 * half)
    for out, at in ((far, 1 - side), (near, side)):

        def block(i, _):
            base = pl.multiple_of(at * (length // 2) + i * step, step)
            for t in range(tiles):
                now = rows[pl.ds(pl.multiple_of(base + ROWS, ROWS), step), tile_of(t)]
                before = rows[aligned(base, step), tile_of(t)]
                target = pl.multiple_of((i * tiles + t) * step, step)
                out[pl.ds(target, step), :] = short_filtered(taps, 0, tile_of(t), now, before)
            return 0

        lax.fori_loop(0, half, block, 0)
    last = rows[length + ROWS - 1 : length + ROWS, :]
    last_but_one = rows[length + ROWS - 2 : length + ROWS - 1, :]
    first = taps[0, 1:2, :] * last + taps[0, 2:3, :] * last_but_one
    second = taps[0, 2:3, :] * last
    end = tiles * (length // 2)
    for t in range(tiles):
        both = jnp.concatenate([first[:, tile_of(t)], second[:, tile_of(t)]], axis=0)
        for out in (near, far):
            out[end + 2 * t : end + 2 * t + 2, :] = both


def query(me, streams, short_filters, params, count):
    length, channels = streams.shape[1:]
    tiles = channels // LANES
    rows = jax.ShapeDtypeStruct((tiles * (length // 2 + 2), LANES), jnp.float32)
    return pl.pallas_call(
        functools.partial(query_kernel, count // 2),
        out_shape=[rows, rows],
        in_specs=[in_smem(), in_any(), in_any(), in_any()],
        out_specs=[in_vmem()] * 2,
        scratch_shapes=[
            pltpu.VMEM((length + ROWS, channels), jnp.float32),
            pltpu.VMEM(short_filters.shape, jnp.float32),
            pltpu.SemaphoreType.DMA((2,)),
        ],
        compiler_params=params_of(60 * 1024 * 1024),
        name="query",
    )(me, streams, short_filters, params)


def hold_kernel(*refs):
    del refs


def hold(value, *others):
    return pl.pallas_call(
        hold_kernel,
        out_shape=jax.ShapeDtypeStruct(value.shape, value.dtype),
        in_specs=[in_any()] * (1 + len(others)),
        out_specs=in_any(),
        input_output_aliases={0: 0},
        compiler_params=params_of(),
        name="hold",
    )(value, *others)


def deal_kernel(half, tiles, me_ref, near, far, *rest):
    results, outs = rest[:half], rest[half:]
    share = (near.shape[0] - 2 * tiles) // half
    place = me_ref[0] % half
    for k in range(half):
        start = pl.multiple_of((place ^ k) * share, share)
        outs[k][0:share, :] = near[pl.ds(start, share), :]
        outs[k][share : 2 * share, :] = far[pl.ds(start, share), :]
        at = 2 * share
        for source in (near, far):
            outs[k][at : at + 2 * tiles, :] = source[half * share : half * share + 2 * tiles, :]
            at += 2 * tiles
        outs[k][at : at + results[k].shape[0], :] = results[k][...]


def deal(me, near, far, results, tiles, count):
    half = count // 2
    size = 2 * (near.shape[0] - 2 * tiles) // half + 4 * tiles + results[0].shape[0]
    return pl.pallas_call(
        functools.partial(deal_kernel, half, tiles),
        out_shape=[jax.ShapeDtypeStruct((size, LANES), jnp.float32)] * half,
        in_specs=[in_smem()] + [in_vmem()] * (2 + half),
        out_specs=[in_vmem()] * half,
        compiler_params=params_of(),
        name="deal",
    )(me, near, far, *results[:half])


def arrange_query(count, me, dealt, out, lacking):
    half = count // 2
    tiles, rows = out.shape[:2]
    part = rows // count
    lacking[...] = jnp.zeros(lacking.shape, jnp.float32)
    for k in range(half):
        for i in range(2):
            r = me ^ k ^ (i * half)
            for t in range(tiles):
                for m in range(0, part, ROWS):
                    at = (i * tiles + t) * part + m
                    out[t, pl.ds(m * count + r, ROWS, stride=count), :] = dealt[k][
                        at : at + ROWS, :
                    ]
                at = 2 * tiles * part + (i * tiles + t) * 2
                lacking[t, pl.ds(r + 1, 2, stride=2 * count), :] = dealt[k][at : at + 2, :]
    first = (me == 0).astype(jnp.float32)
    for t in range(tiles):
        for m in range(2):
            at = slice(m * count, (m + 1) * count)
            out[t, at, :] += first * lacking[t, 2 * m * count : (2 * m + 1) * count, :]


def finish_kernel(count, width, pieces, me_ref, *rest):
    messages, (out, rows, query_rows, lacking, sems) = by_partner(rest[:count]), rest[count:]
    me = me_ref[0]
    part = out.shape[0]
    arrange_query(count, me, messages[: count // 2], query_rows, lacking)
    step = 4
    stores = []

    def block(i, _):
        at = aligned(i * step * count, step * count)
        tiles = []
        for message in messages:
            ahead = message.shape[0] - part * count
            start = pl.multiple_of(ahead + i * step * count, step * count)
            tiles.append(message[pl.ds(start, step * count), :])
        tiles = swap_tiles_and_slots(tiles, width, me, False)
        for t in range(count):
            product = query_rows[t, at, :] * tiles[t]
            for m in range(step):
                rows[i * step + m, :, tile_of(t)] = product[m * count : (m + 1) * count]
        return 0

    size = part // pieces
    for piece in range(pieces):
        lax.fori_loop(piece * size // step, (piece + 1) * size // step, block, 0)
        done = pl.ds(piece * size, size)
        store = pltpu.make_async_copy(rows.at[done], out.at[done], sems.at[piece])
        store.start()
        stores.append(store)
    for store in stores:
        store.wait()


def finish(me, messages, tiles, count, width):
    rows = messages[-1].shape[0]
    part = rows // count
    pieces = 4
    return pl.pallas_call(
        functools.partial(finish_kernel, count, width, pieces),
        out_shape=jax.ShapeDtypeStruct((part, count, tiles * LANES), jnp.float32),
        in_specs=[in_smem()] + [in_vmem()] * count,
        out_specs=in_any(),
        scratch_shapes=[
            pltpu.VMEM((part, count, tiles * LANES), jnp.float32),
            pltpu.VMEM((tiles, rows, LANES), jnp.float32),
            pltpu.VMEM((tiles, 4 * count, LANES), jnp.float32),
            pltpu.SemaphoreType.DMA((pieces,)),
        ],
        compiler_params=params_of(),
        name="finish",
    )(me, *far_first_operands(messages))


def swapped(block, axis, k):
    return lax.ppermute(block, axis, [(i, i ^ k) for i in range(lax.axis_size(axis))])


def exchanged(messages, axis):
    received = {0: messages[0]}
    for k in range(1, len(messages)):
        received[k] = swapped(messages[k], axis, k)
    return [received[k] for k in range(len(messages))]


def wide_body(streams, short_filters, skip_gain, long_filter):
    count = lax.axis_size("seq")
    groups = lax.axis_size("grp")
    place = lax.axis_index("seq").astype(jnp.int32)
    me = place.reshape(1)
    group = lax.axis_index("grp").astype(jnp.int32).reshape(1)
    length = streams.shape[1]
    width = long_filter.shape[1] // count
    forward, inverse = (jnp.asarray(table) for table in transform_tables(length))
    *gated, params = gate(me, streams, short_filters, skip_gain, long_filter, count, width)
    gated = exchanged(gated, "seq")
    half = count // 2
    tiles = streams.shape[2] // LANES
    near, far = query(me, streams, short_filters, params, count)
    far = hold(far, *far_first_operands(gated))
    taps = collect_taps(me, gated, count, width, length)
    taps = [taps] + [swapped(taps, "grp", k) for k in range(1, groups)]
    far = swapped(far, "seq", half)
    spectra = filter_spectra(group, params, forward, taps, count, width)
    convolved = convolve(me, params, forward, inverse, spectra, gated, count)
    dealt = exchanged(deal(me, near, far, convolved, tiles, count), "seq")
    convolved = dealt + [swapped(convolved[k], "seq", k) for k in range(half, count)]
    return finish(me, convolved, tiles, count, width)


def body(streams, short_filters, skip_gain, long_filter):
    count = lax.axis_size("seq")
    width = long_filter.shape[1] // count
    one_tile = streams.shape[2] == count * LANES and count == ROWS
    if one_tile and width == ROWS and LANES % (count * width) == 0:
        return wide_body(streams, short_filters, skip_gain, long_filter)
    return narrow_body(streams, short_filters, skip_gain, long_filter)


def solution(mesh):
    return jax.shard_map(
        body,
        mesh=mesh,
        in_specs=(P(None, "seq", "grp"), P(None, None, "grp"), P("grp"), P("seq", "grp")),
        out_specs=P("seq", None, "grp"),
        check_vma=False,
    )
```

```python
import functools
import math

import jax
import jax.numpy as jnp
import numpy as np
from jax import lax
from jax.experimental import pallas as pl
from jax.experimental.pallas import tpu as pltpu
from jax.sharding import PartitionSpec as P

LANES = 128
ROWS = 8
VMEM_BYTES = 20 * 1024 * 1024


def passed_along(block, axis, distance):
    devices = range(lax.axis_size(axis))
    route = [(i - distance, i) for i in devices if i - distance in devices]
    return lax.ppermute(block, axis, route)


def contract(pattern, matrix, values):
    return jnp.einsum(pattern, matrix, values, precision=lax.Precision.HIGHEST)


def unit_roots(row_index, col_index, period):
    phase_steps = row_index[:, None] * col_index[None, :] % period
    phases = -2.0 * math.pi / period * phase_steps.astype(jnp.float32)
    return (jnp.cos(phases), jnp.sin(phases))


def rotate(real_part, imag_part, cos_part, sin_part):
    return (
        real_part * cos_part - imag_part * sin_part,
        real_part * sin_part + imag_part * cos_part,
    )


def unrotate(real_part, imag_part, cos_part, sin_part):
    return (
        real_part * cos_part + imag_part * sin_part,
        imag_part * cos_part - real_part * sin_part,
    )


def fine_forward(cos_table, sin_table, real_part, imag_part):
    pattern = "km,imc->ikc"
    return (
        contract(pattern, cos_table, real_part) - contract(pattern, sin_table, imag_part),
        contract(pattern, cos_table, imag_part) + contract(pattern, sin_table, real_part),
    )


def fine_inverse(cos_table, sin_table, real_part, imag_part):
    pattern = "km,ikc->imc"
    return (
        contract(pattern, cos_table, real_part) + contract(pattern, sin_table, imag_part),
        contract(pattern, cos_table, imag_part) - contract(pattern, sin_table, real_part),
    )


def narrow_body(streams, short_filters, skip_gain, long_filter):
    panels = lax.axis_size("seq")
    my_panel = lax.axis_index("seq")
    length = streams.shape[1]
    channels = streams.shape[2]
    slice_len = length // panels
    points = 2 * panels * length
    rim_rows = passed_along(streams[:, length - 2 :, :], "seq", 1)
    extended = jnp.concatenate([rim_rows, streams], axis=1)
    featured = (
        short_filters[:, 0:1, :] * extended[:, 2:, :]
        + short_filters[:, 1:2, :] * extended[:, 1 : length + 1, :]
        + short_filters[:, 2:3, :] * extended[:, 0:length, :]
    )
    query_rows = featured[0]
    gated_rows = featured[1] * featured[2]
    query_cols, gated_cols, filter_cols = (
        lax.all_to_all(
            query_rows.reshape(length, 1, channels), "seq", split_axis=0, concat_axis=1, tiled=True
        ),
        lax.all_to_all(
            gated_rows.reshape(length, 1, channels), "seq", split_axis=0, concat_axis=1, tiled=True
        ),
        lax.all_to_all(
            long_filter.reshape(length, 1, long_filter.shape[1]),
            "seq",
            split_axis=0,
            concat_axis=1,
            tiled=True,
        ),
    )
    coarse = jnp.arange(2 * panels, dtype=jnp.int32)
    cross_cos, cross_sin = unit_roots(coarse, jnp.arange(panels, dtype=jnp.int32), 2 * panels)
    fine_index = jnp.arange(length, dtype=jnp.int32)
    local_cos, local_sin = unit_roots(fine_index, fine_index, length)
    own_rows = my_panel * slice_len + jnp.arange(slice_len, dtype=jnp.int32)
    twist_cos, twist_sin = unit_roots(coarse, own_rows, points)
    own_bins = 2 * my_panel + jnp.arange(2, dtype=jnp.int32)
    turn_cos, turn_sin = unit_roots(own_bins, fine_index, points)
    pattern = "kr,mrc->kmc"
    tap_real, tap_imag = rotate(
        contract(pattern, cross_cos, filter_cols),
        contract(pattern, cross_sin, filter_cols),
        twist_cos[:, :, None],
        twist_sin[:, :, None],
    )
    act_real = contract(pattern, cross_cos, gated_cols)
    act_imag = contract(pattern, cross_sin, gated_cols)
    act_real, act_imag = rotate(act_real, act_imag, twist_cos[:, :, None], twist_sin[:, :, None])
    act_real, act_imag, tap_real, tap_imag = (
        lax.all_to_all(act_real, "seq", split_axis=0, concat_axis=1, tiled=True),
        lax.all_to_all(act_imag, "seq", split_axis=0, concat_axis=1, tiled=True),
        lax.all_to_all(tap_real, "seq", split_axis=0, concat_axis=1, tiled=True),
        lax.all_to_all(tap_imag, "seq", split_axis=0, concat_axis=1, tiled=True),
    )
    act_real, act_imag = fine_forward(local_cos, local_sin, act_real, act_imag)
    tap_real, tap_imag = fine_forward(local_cos, local_sin, tap_real, tap_imag)
    tap_real, tap_imag = (
        lax.all_gather(tap_real, "grp", axis=2, tiled=True),
        lax.all_gather(tap_imag, "grp", axis=2, tiled=True),
    )
    filter_count = tap_real.shape[2]
    blocks = act_real.shape[2] // filter_count
    wide_real = act_real.reshape(2, length, blocks, filter_count)
    wide_imag = act_imag.reshape(2, length, blocks, filter_count)
    tap_wide_real = tap_real[:, :, None, :]
    tap_wide_imag = tap_imag[:, :, None, :]
    prod_real = (wide_real * tap_wide_real - wide_imag * tap_wide_imag).reshape(
        2, length, blocks * filter_count
    )
    prod_imag = (wide_real * tap_wide_imag + wide_imag * tap_wide_real).reshape(
        2, length, blocks * filter_count
    )
    back_real, back_imag = fine_inverse(local_cos, local_sin, prod_real, prod_imag)
    back_real, back_imag = unrotate(
        back_real, back_imag, turn_cos[:, :, None], turn_sin[:, :, None]
    )
    back_real, back_imag = (
        lax.all_to_all(back_real, "seq", split_axis=1, concat_axis=0, tiled=True),
        lax.all_to_all(back_imag, "seq", split_axis=1, concat_axis=0, tiled=True),
    )
    inverse_scale = 1.0 / points
    inverse_pattern = "kr,kmc->mrc"
    convolved = (
        contract(inverse_pattern, cross_cos, back_real)
        + contract(inverse_pattern, cross_sin, back_imag)
    ) * inverse_scale
    return query_cols * (convolved + skip_gain * gated_cols)


def split16(values):
    high = values.astype(jnp.bfloat16)
    low = (values - high.astype(jnp.float32)).astype(jnp.bfloat16)
    return high, low


def transform_tables(length):
    bins = np.arange(length, dtype=np.int64)[:, None]
    taps = np.arange(length, dtype=np.int64)[None, :]
    phases = ((2 * bins + 1) * taps % (4 * length)).astype(np.float64) * (math.pi / (2 * length))
    table = np.concatenate([np.cos(phases), -np.sin(phases)], axis=0).astype(np.float32)
    high = table.astype(jnp.bfloat16)
    low = (table - high.astype(np.float32)).astype(jnp.bfloat16)
    forward = np.concatenate([high, high, low], axis=1)
    inverse = np.concatenate([high.T, high.T, low.T], axis=1)
    return forward, inverse


def tile_of(t):
    return slice(t * LANES, (t + 1) * LANES)


def aligned(start, size):
    return pl.ds(pl.multiple_of(start, size), size)


def swap_tiles_and_slots(tiles, width, me, tiles_out):
    count = len(tiles)
    lane = lax.broadcasted_iota(jnp.int32, tiles[0].shape, 1)
    slot = lane // width % count
    mine = slot ^ me
    step = 1
    while step < count:
        upper = (slot & step) != 0
        other = (mine & step) != 0
        first, second = (upper, other) if tiles_out else (other, upper)
        partner = lane ^ (step * width)
        turned = list(tiles)
        for t in range(count):
            if t & step:
                continue
            low, high = tiles[t], tiles[t | step]
            moved = jnp.take_along_axis(jnp.where(first, low, high), partner, axis=1)
            kept = jnp.where(first, high, low)
            turned[t] = jnp.where(second, moved, kept)
            turned[t | step] = jnp.where(second, kept, moved)
        tiles = turned
        step *= 2
    return tiles


def short_filtered(taps, s, columns, now, before):
    shape = now.shape
    row = lax.broadcasted_iota(jnp.int32, shape, 0) % ROWS

    def later(rows):
        mixed = jnp.where(row >= ROWS - rows, before, now)
        blocks = mixed.reshape(shape[0] // ROWS, ROWS, shape[1])
        return pltpu.roll(blocks, rows, 1).reshape(shape)

    return (
        taps[s, 0:1, columns] * now
        + taps[s, 1:2, columns] * later(1)
        + taps[s, 2:3, columns] * later(2)
    )


def in_vmem():
    return pl.BlockSpec(memory_space=pltpu.VMEM)


def in_smem():
    return pl.BlockSpec(memory_space=pltpu.SMEM)


def in_any():
    return pl.BlockSpec(memory_space=pl.ANY)


def params_of(limit=VMEM_BYTES):
    return pltpu.CompilerParams(vmem_limit_bytes=limit)


def far_first(count):
    half = count // 2
    return [half, half + 1] + list(range(half)) + list(range(half + 2, count))


def by_partner(refs):
    ordered = [None] * len(refs)
    for k, ref in zip(far_first(len(refs)), refs):
        ordered[k] = ref
    return ordered


def far_first_operands(messages):
    return [messages[k] for k in far_first(len(messages))]


def gate_kernel(count, width, pieces, me_ref, streams, *rest):
    small, rest = rest[:3], rest[3:]
    messages, rest = rest[:count], rest[count:]
    params, key, value, taps, skip, long_filter, sems = rest
    length = streams.shape[1]
    fetches = [
        pltpu.make_async_copy(source, target, sems.at[2 * pieces + i])
        for i, (source, target) in enumerate(zip(small, (taps, skip, long_filter)))
    ]
    for fetch in fetches:
        fetch.start()
    channels = streams.shape[2]
    me = me_ref[0]
    part = length // pieces
    loads = []
    for piece in range(pieces):
        for s, buffer in ((1, key), (2, value)):
            load = pltpu.make_async_copy(
                streams.at[s, pl.ds(piece * part, part)],
                buffer.at[pl.ds(ROWS + piece * part, part)],
                sems.at[2 * piece + s - 1],
            )
            load.start()
            loads.append(load)
    key[0:ROWS, :] = jnp.zeros((ROWS, channels), jnp.float32)
    value[0:ROWS, :] = jnp.zeros((ROWS, channels), jnp.float32)
    for fetch in fetches:
        fetch.wait()
    rows = jnp.concatenate(
        [taps[1], taps[2], skip[...], jnp.zeros((1, channels), jnp.float32)], axis=0
    )
    tiles = [rows[:, tile_of(t)] for t in range(count)]
    params[...] = swap_tiles_and_slots(tiles, width, me, True)[0]
    for k in range(count):
        for t in range(length // LANES):
            at = length + ROWS + t * width
            messages[k][at : at + width, :] = long_filter[aligned((me ^ k) * width, width), tile_of(t)]
    step = 8 * ROWS

    def block(i, _):
        base = i * step
        tiles = []
        for t in range(count):
            features = []
            for s, buffer in ((1, key), (2, value)):
                now = buffer[pl.ds(pl.multiple_of(base + ROWS, ROWS), step), tile_of(t)]
                before = buffer[aligned(base, step), tile_of(t)]
                features.append(short_filtered(taps, s, tile_of(t), now, before))
            tiles.append(features[0] * features[1])
        tiles = swap_tiles_and_slots(tiles, width, me, True)
        for k in range(count):
            messages[k][aligned(base, step), :] = tiles[k]
        return 0

    for piece in range(pieces):
        loads[2 * piece].wait()
        loads[2 * piece + 1].wait()
        lax.fori_loop(piece * part // step, (piece + 1) * part // step, block, 0)
    rim = jnp.concatenate(
        [
            key[length + ROWS - 2 : length + ROWS, :],
            value[length + ROWS - 2 : length + ROWS, :],
            key[ROWS : ROWS + 2, :],
            value[ROWS : ROWS + 2, :],
        ],
        axis=0,
    )
    tiles = [rim[:, tile_of(t)] for t in range(count)]
    tiles = swap_tiles_and_slots(tiles, width, me, True)
    for k in range(count):
        messages[k][length : length + ROWS, :] = tiles[k]


def gate(me, streams, short_filters, skip_gain, long_filter, count, width):
    length, channels = streams.shape[1], streams.shape[2]
    rows = length + ROWS + width * length // LANES
    message = jax.ShapeDtypeStruct((rows, LANES), jnp.float32)
    pieces = 4
    return pl.pallas_call(
        functools.partial(gate_kernel, count, width, pieces),
        out_shape=[message] * count + [jax.ShapeDtypeStruct((ROWS, LANES), jnp.float32)],
        in_specs=[in_smem()] + [in_any()] * 4,
        out_specs=[in_vmem()] * (count + 1),
        scratch_shapes=[
            pltpu.VMEM((length + ROWS, channels), jnp.float32),
            pltpu.VMEM((length + ROWS, channels), jnp.float32),
            pltpu.VMEM(short_filters.shape, jnp.float32),
            pltpu.VMEM((1, channels), jnp.float32),
            pltpu.VMEM(long_filter.shape[::-1], jnp.float32),
            pltpu.SemaphoreType.DMA((2 * pieces + 3,)),
        ],
        compiler_params=params_of(60 * 1024 * 1024),
        name="gate",
    )(me, streams, short_filters, skip_gain.reshape(1, channels), long_filter.T)


def collect_kernel(count, width, me_ref, *rest):
    messages, out = by_partner(rest[:count]), rest[count]
    me = me_ref[0]
    rows = messages[0].shape[0]
    for k in range(count):
        out[me ^ k] = messages[k][rows - out.shape[1] : rows, :]


def collect_taps(me, messages, count, width, length):
    size = width * length // LANES
    return pl.pallas_call(
        functools.partial(collect_kernel, count, width),
        out_shape=jax.ShapeDtypeStruct((count, size, LANES), jnp.float32),
        in_specs=[in_smem()] + [in_vmem()] * count,
        out_specs=in_vmem(),
        compiler_params=params_of(),
        name="collect_taps",
    )(me, *far_first_operands(messages))


def filter_kernel(count, width, group_ref, params, forward, *rest):
    groups = len(rest) - 3
    taps, (out, columns, spectrum) = rest[:groups], rest[groups:]
    length = out.shape[1] // 2
    halves = LANES // (count * width)
    group = group_ref[0]
    for p in range(count):
        for k in range(groups):
            owner = group ^ k
            for turn in range(count * halves // groups):
                at = (owner + turn * groups) // halves + (owner % halves) * count
                for t in range(length // LANES):
                    columns[p, aligned(at * width, width), tile_of(t)] = taps[k][
                        p, t * width : (t + 1) * width, :
                    ]
    for p in range(count):
        high, low = split16(columns[p])
        stacked = jnp.concatenate([high, low, high], axis=1)
        spectrum[p] = lax.dot_general(
            forward[...], stacked, (((1,), (1,)), ((), ())), preferred_element_type=jnp.float32
        )
    parity = lax.broadcasted_iota(jnp.int32, (length, LANES), 0) % 2
    sign = 1.0 - 2.0 * parity.astype(jnp.float32)
    skip = params[6:7, :]
    for d in range(count):
        real = spectrum[d, 0:length, :]
        imag = spectrum[d, length : 2 * length, :]
        if d > 0:
            real = real - sign * spectrum[d - 1, length : 2 * length, :]
            imag = imag + sign * spectrum[d - 1, 0:length, :]
        else:
            real = real + skip
        out[d, 0:length, :] = real
        out[d, length : 2 * length, :] = imag


def filter_spectra(group, params, forward, taps, count, width):
    length = taps[0].shape[1] // width * LANES
    return pl.pallas_call(
        functools.partial(filter_kernel, count, width),
        out_shape=jax.ShapeDtypeStruct((count, 2 * length, LANES), jnp.float32),
        in_specs=[in_smem()] + [in_vmem()] * (2 + len(taps)),
        out_specs=in_vmem(),
        scratch_shapes=[
            pltpu.VMEM((count, LANES, length), jnp.float32),
            pltpu.VMEM((count, 2 * length, LANES), jnp.float32),
        ],
        compiler_params=params_of(),
        name="filter_spectra",
    )(group, params, forward, *taps)


def convolve_kernel(count, length, me_ref, params, forward, inverse, spectra, *rest):
    messages, rest = by_partner(rest[:count]), rest[count:]
    outs, rest = rest[:count], rest[count:]
    rims, bins, halves, result = rest
    me = me_ref[0]
    rims[0] = jnp.zeros((ROWS, LANES), jnp.float32)
    for k in range(count):
        rims[(me ^ k) + 1] = messages[k][length : length + ROWS, :]
    key_taps = [params[a : a + 1, :] for a in range(3)]
    value_taps = [params[3 + a : 4 + a, :] for a in range(3)]

    def feature(taps, now, before, earlier):
        return taps[0] * now + taps[1] * before + taps[2] * earlier

    pair = 2 * ROWS
    row = lax.broadcasted_iota(jnp.int32, (pair, LANES), 0)
    for k in range(count):
        at = aligned((me ^ k) * LANES, LANES)
        past = rims[me ^ k]
        rim = messages[k][length : length + ROWS, :]
        k254, k255, v254, v255 = (past[a : a + 1, :] for a in range(4))
        k0, k1, v0, v1 = (rim[4 + a : 5 + a, :] for a in range(4))
        first = feature(key_taps, k0, k255, k254) * feature(value_taps, v0, v255, v254)
        second = feature(key_taps, k1, k0, k255) * feature(value_taps, v1, v0, v255)
        top = jnp.where(row == 0, first, jnp.where(row == 1, second, messages[k][0:pair, :]))
        for a, b, values in ((0, pair, top), (pair, length, messages[k][pair:length, :])):
            high, low = split16(values)
            halves[a:b, at] = high
            halves[length + a : length + b, at] = low
            halves[2 * length + a : 2 * length + b, at] = high
    for c in range(0, count, 2):
        columns = slice(c * LANES, (c + 2) * LANES)
        bins[:, columns] = jnp.dot(
            forward[...], halves[0 : 3 * length, columns], preferred_element_type=jnp.float32
        )

    def block(i, _):
        start = pl.multiple_of(i * pair, pair)
        rows = []
        for at in (start, start + ROWS):
            real = [bins[pl.ds(at, ROWS), tile_of(r)] for r in range(count)]
            imag = [bins[pl.ds(length + at, ROWS), tile_of(r)] for r in range(count)]
            tap_real = [spectra[d, pl.ds(at, ROWS), :] for d in range(count)]
            tap_imag = [spectra[d, pl.ds(length + at, ROWS), :] for d in range(count)]
            sums = []
            for r in range(count):
                sum_real = real[r] * tap_real[0] - imag[r] * tap_imag[0]
                sum_imag = real[r] * tap_imag[0] + imag[r] * tap_real[0]
                for d in range(1, r + 1):
                    sum_real += real[r - d] * tap_real[d] - imag[r - d] * tap_imag[d]
                    sum_imag += real[r - d] * tap_imag[d] + imag[r - d] * tap_real[d]
                sums.append((sum_real, sum_imag))
            rows.append(sums)
        for r in range(count):
            for part in range(2):
                both = jnp.concatenate([rows[0][r][part], rows[1][r][part]], axis=0)
                high, low = split16(both)
                base = start + part * length
                halves[pl.ds(base, pair), tile_of(r)] = high
                halves[pl.ds(base + 2 * length, pair), tile_of(r)] = low
                halves[pl.ds(base + 4 * length, pair), tile_of(r)] = high
        return 0

    lax.fori_loop(0, length // pair, block, 0)
    for c in range(0, count, 2):
        columns = slice(c * LANES, (c + 2) * LANES)
        result[:, columns] = jnp.dot(
            inverse[...], halves[:, columns], preferred_element_type=jnp.float32
        )
    scale = 1.0 / length
    part = length // count
    for k in range(count):
        for m in range(0, part, ROWS):
            for r in range(count):
                outs[k][pl.ds(m * count + r, ROWS, stride=count), :] = (
                    result[aligned((me ^ k) * part + m, ROWS), tile_of(r)] * scale
                )


def convolve(me, params, forward, inverse, spectra, messages, count):
    length = spectra.shape[1] // 2
    return pl.pallas_call(
        functools.partial(convolve_kernel, count, length),
        out_shape=[jax.ShapeDtypeStruct((length, LANES), jnp.float32)] * count,
        in_specs=[in_smem()] + [in_vmem()] * (4 + count),
        out_specs=[in_vmem()] * count,
        scratch_shapes=[
            pltpu.VMEM((count + 1, ROWS, LANES), jnp.float32),
            pltpu.VMEM((2 * length, count * LANES), jnp.float32),
            pltpu.VMEM((6 * length, count * LANES), jnp.bfloat16),
            pltpu.VMEM((length, count * LANES), jnp.float32),
        ],
        compiler_params=params_of(),
        name="convolve",
    )(me, params, forward, inverse, spectra, *far_first_operands(messages))


def query_kernel(count, me_ref, streams, taps_in, _, *rest):
    evens, (odds, rows, taps, sems) = rest[: count // 2], rest[count // 2 :]
    length, channels = streams.shape[1:]
    tiles = channels // LANES
    part = length // count
    size = tiles * (part + 2)
    me = me_ref[0]
    load = pltpu.make_async_copy(streams.at[0], rows.at[pl.ds(ROWS, length)], sems.at[0])
    fetch = pltpu.make_async_copy(taps_in, taps, sems.at[1])
    load.start()
    fetch.start()
    rows[0:ROWS, :] = jnp.zeros((ROWS, channels), jnp.float32)
    fetch.wait()
    load.wait()
    last = rows[length + ROWS - 1 : length + ROWS, :]
    last_but_one = rows[length + ROWS - 2 : length + ROWS - 1, :]
    first = taps[0, 1:2, :] * last + taps[0, 2:3, :] * last_but_one
    second = taps[0, 2:3, :] * last
    for k in range(count):
        out, ahead = (odds, k // 2 * size) if k % 2 else (evens[k // 2], 0)
        base = pl.multiple_of((me ^ k) * part, part)
        for t in range(tiles):
            now = rows[pl.ds(pl.multiple_of(base + ROWS, ROWS), part), tile_of(t)]
            before = rows[aligned(base, part), tile_of(t)]
            out[ahead + t * part : ahead + (t + 1) * part, :] = short_filtered(
                taps, 0, tile_of(t), now, before
            )
            at = ahead + tiles * part + 2 * t
            out[at : at + 2, :] = jnp.concatenate(
                [first[:, tile_of(t)], second[:, tile_of(t)]], axis=0
            )


def query(me, streams, short_filters, params, count):
    length, channels = streams.shape[1:]
    size = channels // LANES * (length // count + 2)
    sizes = [size] * (count // 2) + [count // 2 * size]
    return pl.pallas_call(
        functools.partial(query_kernel, count),
        out_shape=[jax.ShapeDtypeStruct((rows, LANES), jnp.float32) for rows in sizes],
        in_specs=[in_smem(), in_any(), in_any(), in_any()],
        out_specs=[in_vmem()] * len(sizes),
        scratch_shapes=[
            pltpu.VMEM((length + ROWS, channels), jnp.float32),
            pltpu.VMEM(short_filters.shape, jnp.float32),
            pltpu.SemaphoreType.DMA((2,)),
        ],
        compiler_params=params_of(),
        name="query",
    )(me, streams, short_filters, params)


def hold_kernel(*refs):
    del refs


def hold(values, *others):
    return pl.pallas_call(
        hold_kernel,
        out_shape=[jax.ShapeDtypeStruct(value.shape, value.dtype) for value in values],
        in_specs=[in_any()] * (len(values) + len(others)),
        out_specs=[in_any()] * len(values),
        input_output_aliases={i: i for i in range(len(values))},
        compiler_params=params_of(),
        name="hold",
    )(*values, *others)


def pair_shares_kernel(pairs, *refs):
    evens, odds, outs = refs[:pairs], refs[pairs], refs[-pairs:]
    size = evens[0].shape[0]
    for i in range(pairs):
        outs[i][0:size, :] = evens[i][...]
        outs[i][size : 2 * size, :] = odds[(i + 1) * size : (i + 2) * size, :]


def pair_shares(evens, odds, *earlier):
    shape = jax.ShapeDtypeStruct((2 * evens[0].shape[0], LANES), jnp.float32)
    return pl.pallas_call(
        functools.partial(pair_shares_kernel, len(evens)),
        out_shape=[shape] * len(evens),
        in_specs=[in_vmem()] * (len(evens) + 1) + [in_any()] * len(earlier),
        out_specs=[in_vmem()] * len(evens),
        compiler_params=params_of(),
        name="pair_shares",
    )(*evens, odds, *earlier)


def arrange_query(count, me, shares, out, lacking):
    tiles, rows = out.shape[:2]
    part = rows // count
    lacking[...] = jnp.zeros(lacking.shape, jnp.float32)
    for k in range(count):
        r = me ^ k
        for t in range(tiles):
            for m in range(0, part, ROWS):
                at = t * part + m
                out[t, pl.ds(m * count + r, ROWS, stride=count), :] = shares[k][at : at + ROWS, :]
            at = tiles * part + t * 2
            lacking[t, pl.ds(r + 1, 2, stride=2 * count), :] = shares[k][at : at + 2, :]
    first = (me == 0).astype(jnp.float32)
    for t in range(tiles):
        for m in range(2):
            at = slice(m * count, (m + 1) * count)
            out[t, at, :] += first * lacking[t, 2 * m * count : (2 * m + 1) * count, :]


def finish_kernel(count, width, pieces, me_ref, *rest):
    messages, rest = by_partner(rest[:count]), rest[count:]
    half = count // 2
    own, odds, *pairs = rest[: half + 1]
    out, rows, query_rows, lacking, sems = rest[half + 1 :]
    me = me_ref[0]
    part = out.shape[0]
    size = own.shape[0]
    shares = [own, odds.at[pl.ds(0, size)]]
    for pair in pairs:
        shares += [pair.at[pl.ds(0, size)], pair.at[pl.ds(size, size)]]
    arrange_query(count, me, shares, query_rows, lacking)
    step = 4
    stores = []

    def block(i, _):
        at = aligned(i * step * count, step * count)
        tiles = [message[at, :] for message in messages]
        tiles = swap_tiles_and_slots(tiles, width, me, False)
        for t in range(count):
            product = query_rows[t, at, :] * tiles[t]
            for m in range(step):
                rows[i * step + m, :, tile_of(t)] = product[m * count : (m + 1) * count]
        return 0

    size = part // pieces
    for piece in range(pieces):
        lax.fori_loop(piece * size // step, (piece + 1) * size // step, block, 0)
        done = pl.ds(piece * size, size)
        store = pltpu.make_async_copy(rows.at[done], out.at[done], sems.at[piece])
        store.start()
        stores.append(store)
    for store in stores:
        store.wait()


def finish(me, messages, shares, rows, tiles, count, width):
    part = rows // count
    pieces = 4
    return pl.pallas_call(
        functools.partial(finish_kernel, count, width, pieces),
        out_shape=jax.ShapeDtypeStruct((part, count, tiles * LANES), jnp.float32),
        in_specs=[in_smem()] + [in_vmem()] * (count + len(shares)),
        out_specs=in_any(),
        scratch_shapes=[
            pltpu.VMEM((part, count, tiles * LANES), jnp.float32),
            pltpu.VMEM((tiles, rows, LANES), jnp.float32),
            pltpu.VMEM((tiles, 4 * count, LANES), jnp.float32),
            pltpu.SemaphoreType.DMA((pieces,)),
        ],
        compiler_params=params_of(),
        name="finish",
    )(me, *far_first_operands(messages), *shares)


def swapped(block, axis, k):
    return lax.ppermute(block, axis, [(i, i ^ k) for i in range(lax.axis_size(axis))])


def exchanged(messages, axis):
    received = {0: messages[0]}
    for k in range(1, len(messages)):
        received[k] = swapped(messages[k], axis, k)
    return [received[k] for k in range(len(messages))]


def wide_body(streams, short_filters, skip_gain, long_filter):
    count = lax.axis_size("seq")
    groups = lax.axis_size("grp")
    place = lax.axis_index("seq").astype(jnp.int32)
    me = place.reshape(1)
    group = lax.axis_index("grp").astype(jnp.int32).reshape(1)
    length = streams.shape[1]
    width = long_filter.shape[1] // count
    forward, inverse = (jnp.asarray(table) for table in transform_tables(length))
    *gated, params = gate(me, streams, short_filters, skip_gain, long_filter, count, width)
    half = count // 2
    tiles = streams.shape[2] // LANES
    *evens, odds = query(me, streams, short_filters, params, count)
    odds = swapped(odds, "seq", 1)
    gated = exchanged(gated, "seq")
    pairs = pair_shares(evens[1:], odds, *gated[half:half + 2])
    taps = collect_taps(me, gated, count, width, length)
    taps = [taps] + [swapped(taps, "grp", k) for k in range(1, groups)]
    pairs = [swapped(pair, "seq", 2 * i) for i, pair in enumerate(pairs, 1)]
    spectra = filter_spectra(group, params, forward, taps, count, width)
    convolved = list(convolve(me, params, forward, inverse, spectra, gated, count))
    convolved[1:half] = hold(convolved[1:half], *pairs)
    first = [swapped(convolved[k], "seq", k) for k in (half, half + 1)]
    convolved[half + 2 :] = hold(convolved[half + 2 :], *pairs, first[0])
    convolved = exchanged(convolved[:half], "seq") + first + [
        swapped(convolved[k], "seq", k) for k in range(half + 2, count)
    ]
    shares = [evens[0], odds, *pairs]
    return finish(me, convolved, shares, length, tiles, count, width)


def body(streams, short_filters, skip_gain, long_filter):
    count = lax.axis_size("seq")
    width = long_filter.shape[1] // count
    one_tile = streams.shape[2] == count * LANES and count == ROWS
    if one_tile and width == ROWS and LANES % (count * width) == 0:
        return wide_body(streams, short_filters, skip_gain, long_filter)
    return narrow_body(streams, short_filters, skip_gain, long_filter)


def solution(mesh):
    return jax.shard_map(
        body,
        mesh=mesh,
        in_specs=(P(None, "seq", "grp"), P(None, None, "grp"), P("grp"), P("seq", "grp")),
        out_specs=P("seq", None, "grp"),
        check_vma=False,
    )
```

```python
import functools
import math

import jax
import jax.numpy as jnp
import numpy as np
from jax import lax
from jax.experimental import pallas as pl
from jax.experimental.pallas import tpu as pltpu
from jax.sharding import PartitionSpec as P

LANES = 128
ROWS = 8
VMEM_BYTES = 20 * 1024 * 1024


def passed_along(block, axis, distance):
    devices = range(lax.axis_size(axis))
    route = [(i - distance, i) for i in devices if i - distance in devices]
    return lax.ppermute(block, axis, route)


def contract(pattern, matrix, values):
    return jnp.einsum(pattern, matrix, values, precision=lax.Precision.HIGHEST)


def unit_roots(row_index, col_index, period):
    phase_steps = row_index[:, None] * col_index[None, :] % period
    phases = -2.0 * math.pi / period * phase_steps.astype(jnp.float32)
    return (jnp.cos(phases), jnp.sin(phases))


def rotate(real_part, imag_part, cos_part, sin_part):
    return (
        real_part * cos_part - imag_part * sin_part,
        real_part * sin_part + imag_part * cos_part,
    )


def unrotate(real_part, imag_part, cos_part, sin_part):
    return (
        real_part * cos_part + imag_part * sin_part,
        imag_part * cos_part - real_part * sin_part,
    )


def fine_forward(cos_table, sin_table, real_part, imag_part):
    pattern = "km,imc->ikc"
    return (
        contract(pattern, cos_table, real_part) - contract(pattern, sin_table, imag_part),
        contract(pattern, cos_table, imag_part) + contract(pattern, sin_table, real_part),
    )


def fine_inverse(cos_table, sin_table, real_part, imag_part):
    pattern = "km,ikc->imc"
    return (
        contract(pattern, cos_table, real_part) + contract(pattern, sin_table, imag_part),
        contract(pattern, cos_table, imag_part) - contract(pattern, sin_table, real_part),
    )


def narrow_body(streams, short_filters, skip_gain, long_filter):
    panels = lax.axis_size("seq")
    my_panel = lax.axis_index("seq")
    length = streams.shape[1]
    channels = streams.shape[2]
    slice_len = length // panels
    points = 2 * panels * length
    rim_rows = passed_along(streams[:, length - 2 :, :], "seq", 1)
    extended = jnp.concatenate([rim_rows, streams], axis=1)
    featured = (
        short_filters[:, 0:1, :] * extended[:, 2:, :]
        + short_filters[:, 1:2, :] * extended[:, 1 : length + 1, :]
        + short_filters[:, 2:3, :] * extended[:, 0:length, :]
    )
    query_rows = featured[0]
    gated_rows = featured[1] * featured[2]
    query_cols, gated_cols, filter_cols = (
        lax.all_to_all(
            query_rows.reshape(length, 1, channels), "seq", split_axis=0, concat_axis=1, tiled=True
        ),
        lax.all_to_all(
            gated_rows.reshape(length, 1, channels), "seq", split_axis=0, concat_axis=1, tiled=True
        ),
        lax.all_to_all(
            long_filter.reshape(length, 1, long_filter.shape[1]),
            "seq",
            split_axis=0,
            concat_axis=1,
            tiled=True,
        ),
    )
    coarse = jnp.arange(2 * panels, dtype=jnp.int32)
    cross_cos, cross_sin = unit_roots(coarse, jnp.arange(panels, dtype=jnp.int32), 2 * panels)
    fine_index = jnp.arange(length, dtype=jnp.int32)
    local_cos, local_sin = unit_roots(fine_index, fine_index, length)
    own_rows = my_panel * slice_len + jnp.arange(slice_len, dtype=jnp.int32)
    twist_cos, twist_sin = unit_roots(coarse, own_rows, points)
    own_bins = 2 * my_panel + jnp.arange(2, dtype=jnp.int32)
    turn_cos, turn_sin = unit_roots(own_bins, fine_index, points)
    pattern = "kr,mrc->kmc"
    tap_real, tap_imag = rotate(
        contract(pattern, cross_cos, filter_cols),
        contract(pattern, cross_sin, filter_cols),
        twist_cos[:, :, None],
        twist_sin[:, :, None],
    )
    act_real = contract(pattern, cross_cos, gated_cols)
    act_imag = contract(pattern, cross_sin, gated_cols)
    act_real, act_imag = rotate(act_real, act_imag, twist_cos[:, :, None], twist_sin[:, :, None])
    act_real, act_imag, tap_real, tap_imag = (
        lax.all_to_all(act_real, "seq", split_axis=0, concat_axis=1, tiled=True),
        lax.all_to_all(act_imag, "seq", split_axis=0, concat_axis=1, tiled=True),
        lax.all_to_all(tap_real, "seq", split_axis=0, concat_axis=1, tiled=True),
        lax.all_to_all(tap_imag, "seq", split_axis=0, concat_axis=1, tiled=True),
    )
    act_real, act_imag = fine_forward(local_cos, local_sin, act_real, act_imag)
    tap_real, tap_imag = fine_forward(local_cos, local_sin, tap_real, tap_imag)
    tap_real, tap_imag = (
        lax.all_gather(tap_real, "grp", axis=2, tiled=True),
        lax.all_gather(tap_imag, "grp", axis=2, tiled=True),
    )
    filter_count = tap_real.shape[2]
    blocks = act_real.shape[2] // filter_count
    wide_real = act_real.reshape(2, length, blocks, filter_count)
    wide_imag = act_imag.reshape(2, length, blocks, filter_count)
    tap_wide_real = tap_real[:, :, None, :]
    tap_wide_imag = tap_imag[:, :, None, :]
    prod_real = (wide_real * tap_wide_real - wide_imag * tap_wide_imag).reshape(
        2, length, blocks * filter_count
    )
    prod_imag = (wide_real * tap_wide_imag + wide_imag * tap_wide_real).reshape(
        2, length, blocks * filter_count
    )
    back_real, back_imag = fine_inverse(local_cos, local_sin, prod_real, prod_imag)
    back_real, back_imag = unrotate(
        back_real, back_imag, turn_cos[:, :, None], turn_sin[:, :, None]
    )
    back_real, back_imag = (
        lax.all_to_all(back_real, "seq", split_axis=1, concat_axis=0, tiled=True),
        lax.all_to_all(back_imag, "seq", split_axis=1, concat_axis=0, tiled=True),
    )
    inverse_scale = 1.0 / points
    inverse_pattern = "kr,kmc->mrc"
    convolved = (
        contract(inverse_pattern, cross_cos, back_real)
        + contract(inverse_pattern, cross_sin, back_imag)
    ) * inverse_scale
    return query_cols * (convolved + skip_gain * gated_cols)


def split16(values):
    high = values.astype(jnp.bfloat16)
    low = (values - high.astype(jnp.float32)).astype(jnp.bfloat16)
    return high, low


def transform_tables(length):
    bins = np.arange(length, dtype=np.int64)[:, None]
    taps = np.arange(length, dtype=np.int64)[None, :]
    phases = ((2 * bins + 1) * taps % (4 * length)).astype(np.float64) * (math.pi / (2 * length))
    table = np.concatenate([np.cos(phases), -np.sin(phases)], axis=0).astype(np.float32)
    high = table.astype(jnp.bfloat16)
    low = (table - high.astype(np.float32)).astype(jnp.bfloat16)
    forward = np.concatenate([high, high, low], axis=1)
    inverse = np.concatenate([high.T, high.T, low.T], axis=1)
    return forward, inverse


def tile_of(t):
    return slice(t * LANES, (t + 1) * LANES)


def aligned(start, size):
    return pl.ds(pl.multiple_of(start, size), size)


def swap_tiles_and_slots(tiles, width, me, tiles_out):
    count = len(tiles)
    lane = lax.broadcasted_iota(jnp.int32, tiles[0].shape, 1)
    slot = lane // width % count
    mine = slot ^ me
    step = 1
    while step < count:
        upper = (slot & step) != 0
        other = (mine & step) != 0
        first, second = (upper, other) if tiles_out else (other, upper)
        partner = lane ^ (step * width)
        turned = list(tiles)
        for t in range(count):
            if t & step:
                continue
            low, high = tiles[t], tiles[t | step]
            moved = jnp.take_along_axis(jnp.where(first, low, high), partner, axis=1)
            kept = jnp.where(first, high, low)
            turned[t] = jnp.where(second, moved, kept)
            turned[t | step] = jnp.where(second, kept, moved)
        tiles = turned
        step *= 2
    return tiles


def short_filtered(taps, s, columns, now, before):
    shape = now.shape
    row = lax.broadcasted_iota(jnp.int32, shape, 0) % ROWS

    def later(rows):
        mixed = jnp.where(row >= ROWS - rows, before, now)
        blocks = mixed.reshape(shape[0] // ROWS, ROWS, shape[1])
        return pltpu.roll(blocks, rows, 1).reshape(shape)

    return (
        taps[s, 0:1, columns] * now
        + taps[s, 1:2, columns] * later(1)
        + taps[s, 2:3, columns] * later(2)
    )


def begun(taps, s, head):
    first = taps[s, 0:1, :] * head[0:1]
    second = taps[s, 0:1, :] * head[1:2] + taps[s, 1:2, :] * head[0:1]
    return jnp.concatenate([first, second], axis=0)


def lacked(taps, s, end):
    first = taps[s, 1:2, :] * end[1:2] + taps[s, 2:3, :] * end[0:1]
    return jnp.concatenate([first, taps[s, 2:3, :] * end[1:2]], axis=0)


def upper_half(shape, count, width):
    lane = lax.broadcasted_iota(jnp.int32, shape, 1)
    return lane // width % count // (count // 2), lane ^ (count // 2 * width)


def packed(low, high, side, count, width):
    upper, opposite = upper_half(low.shape, count, width)
    first = side == 0
    moved = jnp.take_along_axis(jnp.where(first, high, low), opposite, axis=1)
    return jnp.where(upper == side, jnp.where(first, low, high), moved)


def unpacked(tile, side, count, width, fill):
    upper, opposite = upper_half(tile.shape, count, width)
    first = side == 0
    moved = jnp.take_along_axis(tile, opposite, axis=1)
    low = jnp.where(first, tile, moved)
    high = jnp.where(first, moved, tile)
    return jnp.where(upper == side, low, fill), jnp.where(upper == side, high, fill)


def in_vmem():
    return pl.BlockSpec(memory_space=pltpu.VMEM)


def in_smem():
    return pl.BlockSpec(memory_space=pltpu.SMEM)


def in_any():
    return pl.BlockSpec(memory_space=pl.ANY)


def params_of(limit=VMEM_BYTES):
    return pltpu.CompilerParams(vmem_limit_bytes=limit)


def far_first(count):
    half = count // 2
    return [half, half + 1] + list(range(half)) + list(range(half + 2, count))


def by_partner(refs):
    ordered = [None] * len(refs)
    for k, ref in zip(far_first(len(refs)), refs):
        ordered[k] = ref
    return ordered


def far_first_operands(messages):
    return [messages[k] for k in far_first(len(messages))]


def gate_kernel(count, width, pieces, me_ref, streams, *rest):
    small, rest = rest[:3], rest[3:]
    messages, rest = rest[:count], rest[count:]
    params, key, value, query_end, taps, skip, long_filter, sems = rest
    length = streams.shape[1]
    sources = (*small, streams.at[0, pl.ds(length - ROWS, ROWS)])
    targets = (taps, skip, long_filter, query_end)
    fetches = [
        pltpu.make_async_copy(source, target, sems.at[2 * pieces + i])
        for i, (source, target) in enumerate(zip(sources, targets))
    ]
    for fetch in fetches:
        fetch.start()
    channels = streams.shape[2]
    me = me_ref[0]
    part = length // pieces
    loads = []
    for piece in range(pieces):
        for s, buffer in ((1, key), (2, value)):
            load = pltpu.make_async_copy(
                streams.at[s, pl.ds(piece * part, part)],
                buffer.at[pl.ds(ROWS + piece * part, part)],
                sems.at[2 * piece + s - 1],
            )
            load.start()
            loads.append(load)
    key[0:ROWS, :] = jnp.zeros((ROWS, channels), jnp.float32)
    value[0:ROWS, :] = jnp.zeros((ROWS, channels), jnp.float32)
    for fetch in fetches:
        fetch.wait()
    rows = jnp.concatenate(
        [taps[1], taps[2], skip[...], jnp.zeros((1, channels), jnp.float32)], axis=0
    )
    tiles = [rows[:, tile_of(t)] for t in range(count)]
    params[...] = swap_tiles_and_slots(tiles, width, me, True)[0]
    for k in range(count):
        for t in range(length // LANES):
            at = length + ROWS + t * width
            messages[k][at : at + width, :] = long_filter[aligned((me ^ k) * width, width), tile_of(t)]
    step = 8 * ROWS

    def block(i, _):
        base = i * step
        tiles = []
        for t in range(count):
            features = []
            for s, buffer in ((1, key), (2, value)):
                now = buffer[pl.ds(pl.multiple_of(base + ROWS, ROWS), step), tile_of(t)]
                before = buffer[aligned(base, step), tile_of(t)]
                features.append(short_filtered(taps, s, tile_of(t), now, before))
            tiles.append(features[0] * features[1])
        tiles = swap_tiles_and_slots(tiles, width, me, True)
        for k in range(count):
            messages[k][aligned(base, step), :] = tiles[k]
        return 0

    for piece in range(pieces):
        loads[2 * piece].wait()
        loads[2 * piece + 1].wait()
        lax.fori_loop(piece * part // step, (piece + 1) * part // step, block, 0)
    key_head, value_head = (
        begun(taps, s, buffer[ROWS : ROWS + 2, :]) for s, buffer in ((1, key), (2, value))
    )
    ends = [buffer[length + ROWS - 2 : length + ROWS, :] for buffer in (key, value)]
    rim = jnp.concatenate(
        [lacked(taps, 1, ends[0]), lacked(taps, 2, ends[1]), value_head]
        + [lacked(taps, 0, query_end[ROWS - 2 : ROWS, :])],
        axis=0,
    )
    head = jnp.concatenate([key_head, jnp.zeros((ROWS - 2, channels), jnp.float32)], axis=0)
    for rows, at, size in ((rim, length, ROWS), (head, 0, 2)):
        tiles = [rows[:, tile_of(t)] for t in range(count)]
        tiles = swap_tiles_and_slots(tiles, width, me, True)
        for k in range(count):
            messages[k][at : at + size, :] = tiles[k][0:size]


def gate(me, streams, short_filters, skip_gain, long_filter, count, width):
    length, channels = streams.shape[1], streams.shape[2]
    rows = length + ROWS + width * length // LANES
    message = jax.ShapeDtypeStruct((rows, LANES), jnp.float32)
    pieces = 4
    return pl.pallas_call(
        functools.partial(gate_kernel, count, width, pieces),
        out_shape=[message] * count + [jax.ShapeDtypeStruct((ROWS, LANES), jnp.float32)],
        in_specs=[in_smem()] + [in_any()] * 4,
        out_specs=[in_vmem()] * (count + 1),
        scratch_shapes=[
            pltpu.VMEM((length + ROWS, channels), jnp.float32),
            pltpu.VMEM((length + ROWS, channels), jnp.float32),
            pltpu.VMEM((ROWS, channels), jnp.float32),
            pltpu.VMEM(short_filters.shape, jnp.float32),
            pltpu.VMEM((1, channels), jnp.float32),
            pltpu.VMEM(long_filter.shape[::-1], jnp.float32),
            pltpu.SemaphoreType.DMA((2 * pieces + 4,)),
        ],
        compiler_params=params_of(60 * 1024 * 1024),
        name="gate",
    )(me, streams, short_filters, skip_gain.reshape(1, channels), long_filter.T)


def collect_kernel(count, width, me_ref, *rest):
    messages, out = by_partner(rest[:count]), rest[count]
    me = me_ref[0]
    rows = messages[0].shape[0]
    for k in range(count):
        out[me ^ k] = messages[k][rows - out.shape[1] : rows, :]


def collect_taps(me, messages, count, width, length):
    size = width * length // LANES
    return pl.pallas_call(
        functools.partial(collect_kernel, count, width),
        out_shape=jax.ShapeDtypeStruct((count, size, LANES), jnp.float32),
        in_specs=[in_smem()] + [in_vmem()] * count,
        out_specs=in_vmem(),
        compiler_params=params_of(),
        name="collect_taps",
    )(me, *far_first_operands(messages))


def filter_kernel(count, width, group_ref, params, forward, *rest):
    groups = len(rest) - 3
    taps, (out, columns, spectrum) = rest[:groups], rest[groups:]
    length = out.shape[1] // 2
    halves = LANES // (count * width)
    group = group_ref[0]
    for p in range(count):
        for k in range(groups):
            owner = group ^ k
            for turn in range(count * halves // groups):
                at = (owner + turn * groups) // halves + (owner % halves) * count
                for t in range(length // LANES):
                    columns[p, aligned(at * width, width), tile_of(t)] = taps[k][
                        p, t * width : (t + 1) * width, :
                    ]
    for p in range(count):
        high, low = split16(columns[p])
        stacked = jnp.concatenate([high, low, high], axis=1)
        spectrum[p] = lax.dot_general(
            forward[...], stacked, (((1,), (1,)), ((), ())), preferred_element_type=jnp.float32
        )
    parity = lax.broadcasted_iota(jnp.int32, (length, LANES), 0) % 2
    sign = 1.0 - 2.0 * parity.astype(jnp.float32)
    skip = params[6:7, :]
    for d in range(count):
        real = spectrum[d, 0:length, :]
        imag = spectrum[d, length : 2 * length, :]
        if d > 0:
            real = real - sign * spectrum[d - 1, length : 2 * length, :]
            imag = imag + sign * spectrum[d - 1, 0:length, :]
        else:
            real = real + skip
        out[d, 0:length, :] = real
        out[d, length : 2 * length, :] = imag


def filter_spectra(group, params, forward, taps, count, width):
    length = taps[0].shape[1] // width * LANES
    return pl.pallas_call(
        functools.partial(filter_kernel, count, width),
        out_shape=jax.ShapeDtypeStruct((count, 2 * length, LANES), jnp.float32),
        in_specs=[in_smem()] + [in_vmem()] * (2 + len(taps)),
        out_specs=in_vmem(),
        scratch_shapes=[
            pltpu.VMEM((count, LANES, length), jnp.float32),
            pltpu.VMEM((count, 2 * length, LANES), jnp.float32),
        ],
        compiler_params=params_of(),
        name="filter_spectra",
    )(group, params, forward, *taps)


def convolve_kernel(count, length, me_ref, params, forward, inverse, spectra, *rest):
    messages, rest = by_partner(rest[:count]), rest[count:]
    half = count // 2
    (own_home, pair, odds), outs, rest = rest[:3], rest[3 : 3 + count], rest[3 + count :]
    rims, bins, halves, result, query_rows = rest
    me = me_ref[0]
    side = me // half
    rims[0] = jnp.zeros((ROWS, LANES), jnp.float32)
    for k in range(count):
        rims[(me ^ k) + 1] = messages[k][length : length + ROWS, :]
    block_rows = 2 * ROWS
    row = lax.broadcasted_iota(jnp.int32, (block_rows, LANES), 0)
    for k in range(count):
        at = aligned((me ^ k) * LANES, LANES)
        past = rims[me ^ k]
        rim = messages[k][length : length + ROWS, :]
        first = (messages[k][0:1, :] + past[0:1]) * (rim[4:5] + past[2:3])
        second = (messages[k][1:2, :] + past[1:2]) * (rim[5:6] + past[3:4])
        top = jnp.where(row == 0, first, jnp.where(row == 1, second, messages[k][0:block_rows, :]))
        for a, b, values in ((0, block_rows, top), (block_rows, length, messages[k][block_rows:length, :])):
            high, low = split16(values)
            halves[a:b, at] = high
            halves[length + a : length + b, at] = low
            halves[2 * length + a : 2 * length + b, at] = high
    for c in range(0, count, 2):
        columns = slice(c * LANES, (c + 2) * LANES)
        bins[:, columns] = jnp.dot(
            forward[...], halves[0 : 3 * length, columns], preferred_element_type=jnp.float32
        )

    def block(i, _):
        start = pl.multiple_of(i * block_rows, block_rows)
        rows = []
        for at in (start, start + ROWS):
            real = [bins[pl.ds(at, ROWS), tile_of(r)] for r in range(count)]
            imag = [bins[pl.ds(length + at, ROWS), tile_of(r)] for r in range(count)]
            tap_real = [spectra[d, pl.ds(at, ROWS), :] for d in range(count)]
            tap_imag = [spectra[d, pl.ds(length + at, ROWS), :] for d in range(count)]
            sums = []
            for r in range(count):
                sum_real = real[r] * tap_real[0] - imag[r] * tap_imag[0]
                sum_imag = real[r] * tap_imag[0] + imag[r] * tap_real[0]
                for d in range(1, r + 1):
                    sum_real += real[r - d] * tap_real[d] - imag[r - d] * tap_imag[d]
                    sum_imag += real[r - d] * tap_imag[d] + imag[r - d] * tap_real[d]
                sums.append((sum_real, sum_imag))
            rows.append(sums)
        for r in range(count):
            for part in range(2):
                both = jnp.concatenate([rows[0][r][part], rows[1][r][part]], axis=0)
                high, low = split16(both)
                base = start + part * length
                halves[pl.ds(base, block_rows), tile_of(r)] = high
                halves[pl.ds(base + 2 * length, block_rows), tile_of(r)] = low
                halves[pl.ds(base + 4 * length, block_rows), tile_of(r)] = high
        return 0

    lax.fori_loop(0, length // block_rows, block, 0)
    for c in range(0, count, 2):
        columns = slice(c * LANES, (c + 2) * LANES)
        result[:, columns] = jnp.dot(
            inverse[...], halves[:, columns], preferred_element_type=jnp.float32
        )
    scale = 1.0 / length
    part = length // count
    rows = length // 2
    ahead = pair.shape[0] - 2 * rows
    behind = odds.shape[0] - 2 * rows
    homes = [
        own_home,
        odds.at[pl.ds(behind, rows)],
        pair.at[pl.ds(ahead, rows)],
        pair.at[pl.ds(ahead + rows, rows)],
    ]
    index = lax.broadcasted_iota(jnp.int32, (ROWS, LANES), 0)
    for k in range(half):
        r = me ^ k
        query_rows[r] = homes[k][...]
        query_rows[r ^ half] = jnp.ones((rows, LANES), jnp.float32)
        past = rims[r]
        lacking = jnp.where(index == 0, past[6:7], jnp.where(index == 1, past[7:8], 0.0))
        query_rows[r, 0:ROWS, :] += jnp.where(side == 1, lacking, 0.0)
    for k in range(count):
        for m in range(0, part, ROWS):
            for r in range(count):
                values = result[aligned((me ^ k) * part + m, ROWS), tile_of(r)] * scale
                if k >= half:
                    values *= query_rows[r, aligned((me ^ k) % half * part + m, ROWS), :]
                outs[k][pl.ds(m * count + r, ROWS, stride=count), :] = values


def convolve(me, params, forward, inverse, spectra, messages, homes, count):
    length = spectra.shape[1] // 2
    return pl.pallas_call(
        functools.partial(convolve_kernel, count, length),
        out_shape=[jax.ShapeDtypeStruct((length, LANES), jnp.float32)] * count,
        in_specs=[in_smem()] + [in_vmem()] * (7 + count),
        out_specs=[in_vmem()] * count,
        scratch_shapes=[
            pltpu.VMEM((count + 1, ROWS, LANES), jnp.float32),
            pltpu.VMEM((2 * length, count * LANES), jnp.float32),
            pltpu.VMEM((6 * length, count * LANES), jnp.bfloat16),
            pltpu.VMEM((length, count * LANES), jnp.float32),
            pltpu.VMEM((count, length // 2, LANES), jnp.float32),
        ],
        compiler_params=params_of(),
        name="convolve",
    )(me, params, forward, inverse, spectra, *far_first_operands(messages), *homes)


def share_sizes(count, tiles, part):
    size = tiles * (part + 2)
    return [size] * (count // 2) + [size // 2] * (count // 2)


def query_kernel(count, width, me_ref, streams, taps_in, gated, *rest):
    half = count // 2
    evens, (first_home, second_home, odds, rows, taps, sems) = rest[:half], rest[half:]
    length, channels = streams.shape[1:]
    tiles = channels // LANES
    part = length // count
    sizes = share_sizes(count, tiles, part)
    me = me_ref[0]
    other = 1 - me // half
    load = pltpu.make_async_copy(streams.at[0], rows.at[pl.ds(ROWS, length)], sems.at[0])
    fetch = pltpu.make_async_copy(taps_in, taps, sems.at[1])
    load.start()
    fetch.start()
    rows[0:ROWS, :] = jnp.zeros((ROWS, channels), jnp.float32)
    fetch.wait()
    load.wait()

    def features(base, size):
        return [
            short_filtered(
                taps,
                0,
                tile_of(t),
                rows[pl.ds(pl.multiple_of(base + ROWS, ROWS), size), tile_of(t)],
                rows[pl.ds(pl.multiple_of(base, ROWS), size), tile_of(t)],
            )
            for t in range(tiles)
        ]

    ends = lacked(taps, 0, rows[length + ROWS - 2 : length + ROWS, :])
    ends = [ends[:, tile_of(t)] for t in range(tiles)]
    at = gated.shape[0]
    odds[0:at, :] = gated[...]
    for k in range(count):
        out, ahead = (odds, at) if k % 2 else (evens[k // 2], 0)
        found = features((me ^ k) * part, part)
        lacking = ends
        if k >= half:
            found, lacking = (
                [packed(a, b, other, count, width) for a, b in zip(one[: tiles // 2], one[tiles // 2 :])]
                for one in (found, ends)
            )
        for t, (tile, end) in enumerate(zip(found, lacking)):
            out[ahead + t * part : ahead + (t + 1) * part, :] = tile
            last = ahead + len(found) * part + 2 * t
            out[last : last + 2, :] = end
        if k % 2:
            at += sizes[k]
    targets = [(first_home, 0), (odds, at), (second_home, 0), (odds, at + length // 2)]
    step = 2 * part
    for i in range(length // 2 // step):
        found = features(other * (length // 2) + i * step, step)
        found = swap_tiles_and_slots(found, width, me, True)
        for k, (out, ahead) in enumerate(targets):
            out[ahead + i * step : ahead + (i + 1) * step, :] = found[k]


def query(me, streams, short_filters, gated, count, width):
    length, channels = streams.shape[1:]
    half = count // 2
    sizes = share_sizes(count, channels // LANES, length // count)
    sizes = sizes[0::2] + [length // 2] * 2 + [gated.shape[0] + sum(sizes[1::2]) + length]
    return pl.pallas_call(
        functools.partial(query_kernel, count, width),
        out_shape=[jax.ShapeDtypeStruct((rows, LANES), jnp.float32) for rows in sizes],
        in_specs=[in_smem(), in_any(), in_any(), in_vmem()],
        out_specs=[in_vmem()] * len(sizes),
        scratch_shapes=[
            pltpu.VMEM((length + ROWS, channels), jnp.float32),
            pltpu.VMEM(short_filters.shape, jnp.float32),
            pltpu.SemaphoreType.DMA((2,)),
        ],
        compiler_params=params_of(),
        name="query",
    )(me, streams, short_filters, gated)


def hold_kernel(*refs):
    del refs


def hold(values, *others):
    return pl.pallas_call(
        hold_kernel,
        out_shape=[jax.ShapeDtypeStruct(value.shape, value.dtype) for value in values],
        in_specs=[in_any()] * (len(values) + len(others)),
        out_specs=[in_any()] * len(values),
        input_output_aliases={i: i for i in range(len(values))},
        compiler_params=params_of(),
        name="hold",
    )(*values, *others)


def pair_shares_kernel(pairs, *refs):
    evens, home, odds, outs = refs[:pairs], refs[pairs], refs[pairs + 1], refs[-pairs:]
    rows = home.shape[0]
    shares = evens[0].shape[0] + sum(even.shape[0] for even in evens)
    at = odds.shape[0] - 2 * rows - shares + evens[0].shape[0]
    for even, out in zip(evens, outs):
        size = even.shape[0]
        out[0:size, :] = even[...]
        out[size : 2 * size, :] = odds[at : at + size, :]
        at += size
    at = odds.shape[0] - rows
    behind = 2 * evens[0].shape[0]
    outs[0][behind : behind + rows, :] = home[...]
    outs[0][behind + rows : behind + 2 * rows, :] = odds[at : at + rows, :]


def pair_shares(evens, home, odds, *earlier):
    sizes = [2 * even.shape[0] for even in evens]
    sizes[0] += 2 * home.shape[0]
    return pl.pallas_call(
        functools.partial(pair_shares_kernel, len(evens)),
        out_shape=[jax.ShapeDtypeStruct((size, LANES), jnp.float32) for size in sizes],
        in_specs=[in_vmem()] * (len(evens) + 2) + [in_any()] * len(earlier),
        out_specs=[in_vmem()] * len(evens),
        compiler_params=params_of(),
        name="pair_shares",
    )(*evens, home, odds, *earlier)


def arrange_query(count, width, me, shares, out, lacking):
    half = count // 2
    tiles, rows = out.shape[:2]
    part = rows // count
    side = me // half
    lacking[...] = jnp.zeros(lacking.shape, jnp.float32)

    def put(t, r, tile, ends):
        for m in range(0, part, ROWS):
            out[t, pl.ds(m * count + r, ROWS, stride=count), :] = tile[m : m + ROWS]
        lacking[t, pl.ds(r + 1, 2, stride=2 * count), :] = ends

    for k in range(count):
        r = me ^ k
        near = k < half
        given = tiles if near else tiles // 2
        for t in range(given):
            tile = shares[k][t * part : (t + 1) * part, :]
            at = given * part + t * 2
            ends = shares[k][at : at + 2, :]
            if near:
                put(t, r, tile, ends)
            else:
                tile = unpacked(tile, side, count, width, 1.0)
                ends = unpacked(ends, side, count, width, 0.0)
                for i in range(2):
                    put(t + i * given, r, tile[i], ends[i])
    panel = lax.broadcasted_iota(jnp.int32, (count, LANES), 0)
    upper, _ = upper_half((count, LANES), count, width)
    first = jnp.where((me == 0) & ((panel < half) | (upper == 0)), 1.0, 0.0)
    for t in range(tiles):
        for m in range(2):
            at = slice(m * count, (m + 1) * count)
            out[t, at, :] += first * lacking[t, 2 * m * count : (2 * m + 1) * count, :]


def finish_kernel(count, width, pieces, me_ref, *rest):
    messages, rest = by_partner(rest[:count]), rest[count:]
    half = count // 2
    own, odds, *pairs = rest[: half + 1]
    out, rows, query_rows, lacking, sems = rest[half + 1 :]
    me = me_ref[0]
    part = out.shape[0]
    length = part * count
    sizes = share_sizes(count, query_rows.shape[0], part)
    start = odds.shape[0] - length - sum(sizes[1::2])
    shares = [own, odds.at[pl.ds(start, sizes[1])]]
    for i, pair in enumerate(pairs, 1):
        size = sizes[2 * i]
        shares += [pair.at[pl.ds(0, size)], pair.at[pl.ds(size, size)]]
    arrange_query(count, width, me, shares, query_rows, lacking)
    step = 4
    stores = []

    def block(i, _):
        at = aligned(i * step * count, step * count)
        tiles = [message[at, :] for message in messages]
        tiles = swap_tiles_and_slots(tiles, width, me, False)
        for t in range(count):
            product = query_rows[t, at, :] * tiles[t]
            for m in range(step):
                rows[i * step + m, :, tile_of(t)] = product[m * count : (m + 1) * count]
        return 0

    size = part // pieces
    for piece in range(pieces):
        lax.fori_loop(piece * size // step, (piece + 1) * size // step, block, 0)
        done = pl.ds(piece * size, size)
        store = pltpu.make_async_copy(rows.at[done], out.at[done], sems.at[piece])
        store.start()
        stores.append(store)
    for store in stores:
        store.wait()


def finish(me, messages, shares, rows, tiles, count, width):
    part = rows // count
    pieces = 4
    return pl.pallas_call(
        functools.partial(finish_kernel, count, width, pieces),
        out_shape=jax.ShapeDtypeStruct((part, count, tiles * LANES), jnp.float32),
        in_specs=[in_smem()] + [in_vmem()] * (count + len(shares)),
        out_specs=in_any(),
        scratch_shapes=[
            pltpu.VMEM((part, count, tiles * LANES), jnp.float32),
            pltpu.VMEM((tiles, rows, LANES), jnp.float32),
            pltpu.VMEM((tiles, 4 * count, LANES), jnp.float32),
            pltpu.SemaphoreType.DMA((pieces,)),
        ],
        compiler_params=params_of(),
        name="finish",
    )(me, *far_first_operands(messages), *shares)


def swapped(block, axis, k):
    return lax.ppermute(block, axis, [(i, i ^ k) for i in range(lax.axis_size(axis))])


def exchanged(messages, axis):
    received = {0: messages[0]}
    for k in range(1, len(messages)):
        received[k] = swapped(messages[k], axis, k)
    return [received[k] for k in range(len(messages))]


def wide_body(streams, short_filters, skip_gain, long_filter):
    count = lax.axis_size("seq")
    groups = lax.axis_size("grp")
    place = lax.axis_index("seq").astype(jnp.int32)
    me = place.reshape(1)
    group = lax.axis_index("grp").astype(jnp.int32).reshape(1)
    length = streams.shape[1]
    width = long_filter.shape[1] // count
    forward, inverse = (jnp.asarray(table) for table in transform_tables(length))
    *gated, params = gate(me, streams, short_filters, skip_gain, long_filter, count, width)
    half = count // 2
    tiles = streams.shape[2] // LANES
    *evens, own_home, next_home, odds = query(
        me, streams, short_filters, gated[1], count, width
    )
    gated[1] = odds
    gated = exchanged(gated, "seq")
    odds = gated[1]
    pairs = pair_shares(evens[1:], next_home, odds, *gated[2:])
    taps = collect_taps(me, gated, count, width, length)
    taps = [taps] + [swapped(taps, "grp", k) for k in range(1, groups)]
    pairs = [swapped(pair, "seq", 2 * i) for i, pair in enumerate(pairs, 1)]
    spectra = filter_spectra(group, params, forward, taps, count, width)
    homes = (own_home, pairs[0], odds)
    convolved = list(convolve(me, params, forward, inverse, spectra, gated, homes, count))
    convolved[1:half] = hold(convolved[1:half], *pairs)
    first = [swapped(convolved[k], "seq", k) for k in (half, half + 1)]
    convolved[half + 2 :] = hold(convolved[half + 2 :], *pairs, first[0])
    convolved = exchanged(convolved[:half], "seq") + first + [
        swapped(convolved[k], "seq", k) for k in range(half + 2, count)
    ]
    shares = [evens[0], odds, *pairs]
    return finish(me, convolved, shares, length, tiles, count, width)


def body(streams, short_filters, skip_gain, long_filter):
    count = lax.axis_size("seq")
    width = long_filter.shape[1] // count
    one_tile = streams.shape[2] == count * LANES and count == ROWS
    if one_tile and width == ROWS and LANES % (count * width) == 0:
        return wide_body(streams, short_filters, skip_gain, long_filter)
    return narrow_body(streams, short_filters, skip_gain, long_filter)


def solution(mesh):
    return jax.shard_map(
        body,
        mesh=mesh,
        in_specs=(P(None, "seq", "grp"), P(None, None, "grp"), P("grp"), P("seq", "grp")),
        out_specs=P("seq", None, "grp"),
        check_vma=False,
    )
```

```python
import functools
import math

import jax
import jax.numpy as jnp
import numpy as np
from jax import lax
from jax.experimental import pallas as pl
from jax.experimental.pallas import tpu as pltpu
from jax.sharding import PartitionSpec as P

LANES = 128
ROWS = 8
VMEM_BYTES = 20 * 1024 * 1024


def passed_along(block, axis, distance):
    devices = range(lax.axis_size(axis))
    route = [(i - distance, i) for i in devices if i - distance in devices]
    return lax.ppermute(block, axis, route)


def contract(pattern, matrix, values):
    return jnp.einsum(pattern, matrix, values, precision=lax.Precision.HIGHEST)


def unit_roots(row_index, col_index, period):
    phase_steps = row_index[:, None] * col_index[None, :] % period
    phases = -2.0 * math.pi / period * phase_steps.astype(jnp.float32)
    return (jnp.cos(phases), jnp.sin(phases))


def rotate(real_part, imag_part, cos_part, sin_part):
    return (
        real_part * cos_part - imag_part * sin_part,
        real_part * sin_part + imag_part * cos_part,
    )


def unrotate(real_part, imag_part, cos_part, sin_part):
    return (
        real_part * cos_part + imag_part * sin_part,
        imag_part * cos_part - real_part * sin_part,
    )


def fine_forward(cos_table, sin_table, real_part, imag_part):
    pattern = "km,imc->ikc"
    return (
        contract(pattern, cos_table, real_part) - contract(pattern, sin_table, imag_part),
        contract(pattern, cos_table, imag_part) + contract(pattern, sin_table, real_part),
    )


def fine_inverse(cos_table, sin_table, real_part, imag_part):
    pattern = "km,ikc->imc"
    return (
        contract(pattern, cos_table, real_part) + contract(pattern, sin_table, imag_part),
        contract(pattern, cos_table, imag_part) - contract(pattern, sin_table, real_part),
    )


def narrow_body(streams, short_filters, skip_gain, long_filter):
    panels = lax.axis_size("seq")
    my_panel = lax.axis_index("seq")
    length = streams.shape[1]
    channels = streams.shape[2]
    slice_len = length // panels
    points = 2 * panels * length
    rim_rows = passed_along(streams[:, length - 2 :, :], "seq", 1)
    extended = jnp.concatenate([rim_rows, streams], axis=1)
    featured = (
        short_filters[:, 0:1, :] * extended[:, 2:, :]
        + short_filters[:, 1:2, :] * extended[:, 1 : length + 1, :]
        + short_filters[:, 2:3, :] * extended[:, 0:length, :]
    )
    query_rows = featured[0]
    gated_rows = featured[1] * featured[2]
    query_cols, gated_cols, filter_cols = (
        lax.all_to_all(
            query_rows.reshape(length, 1, channels), "seq", split_axis=0, concat_axis=1, tiled=True
        ),
        lax.all_to_all(
            gated_rows.reshape(length, 1, channels), "seq", split_axis=0, concat_axis=1, tiled=True
        ),
        lax.all_to_all(
            long_filter.reshape(length, 1, long_filter.shape[1]),
            "seq",
            split_axis=0,
            concat_axis=1,
            tiled=True,
        ),
    )
    coarse = jnp.arange(2 * panels, dtype=jnp.int32)
    cross_cos, cross_sin = unit_roots(coarse, jnp.arange(panels, dtype=jnp.int32), 2 * panels)
    fine_index = jnp.arange(length, dtype=jnp.int32)
    local_cos, local_sin = unit_roots(fine_index, fine_index, length)
    own_rows = my_panel * slice_len + jnp.arange(slice_len, dtype=jnp.int32)
    twist_cos, twist_sin = unit_roots(coarse, own_rows, points)
    own_bins = 2 * my_panel + jnp.arange(2, dtype=jnp.int32)
    turn_cos, turn_sin = unit_roots(own_bins, fine_index, points)
    pattern = "kr,mrc->kmc"
    tap_real, tap_imag = rotate(
        contract(pattern, cross_cos, filter_cols),
        contract(pattern, cross_sin, filter_cols),
        twist_cos[:, :, None],
        twist_sin[:, :, None],
    )
    act_real = contract(pattern, cross_cos, gated_cols)
    act_imag = contract(pattern, cross_sin, gated_cols)
    act_real, act_imag = rotate(act_real, act_imag, twist_cos[:, :, None], twist_sin[:, :, None])
    act_real, act_imag, tap_real, tap_imag = (
        lax.all_to_all(act_real, "seq", split_axis=0, concat_axis=1, tiled=True),
        lax.all_to_all(act_imag, "seq", split_axis=0, concat_axis=1, tiled=True),
        lax.all_to_all(tap_real, "seq", split_axis=0, concat_axis=1, tiled=True),
        lax.all_to_all(tap_imag, "seq", split_axis=0, concat_axis=1, tiled=True),
    )
    act_real, act_imag = fine_forward(local_cos, local_sin, act_real, act_imag)
    tap_real, tap_imag = fine_forward(local_cos, local_sin, tap_real, tap_imag)
    tap_real, tap_imag = (
        lax.all_gather(tap_real, "grp", axis=2, tiled=True),
        lax.all_gather(tap_imag, "grp", axis=2, tiled=True),
    )
    filter_count = tap_real.shape[2]
    blocks = act_real.shape[2] // filter_count
    wide_real = act_real.reshape(2, length, blocks, filter_count)
    wide_imag = act_imag.reshape(2, length, blocks, filter_count)
    tap_wide_real = tap_real[:, :, None, :]
    tap_wide_imag = tap_imag[:, :, None, :]
    prod_real = (wide_real * tap_wide_real - wide_imag * tap_wide_imag).reshape(
        2, length, blocks * filter_count
    )
    prod_imag = (wide_real * tap_wide_imag + wide_imag * tap_wide_real).reshape(
        2, length, blocks * filter_count
    )
    back_real, back_imag = fine_inverse(local_cos, local_sin, prod_real, prod_imag)
    back_real, back_imag = unrotate(
        back_real, back_imag, turn_cos[:, :, None], turn_sin[:, :, None]
    )
    back_real, back_imag = (
        lax.all_to_all(back_real, "seq", split_axis=1, concat_axis=0, tiled=True),
        lax.all_to_all(back_imag, "seq", split_axis=1, concat_axis=0, tiled=True),
    )
    inverse_scale = 1.0 / points
    inverse_pattern = "kr,kmc->mrc"
    convolved = (
        contract(inverse_pattern, cross_cos, back_real)
        + contract(inverse_pattern, cross_sin, back_imag)
    ) * inverse_scale
    return query_cols * (convolved + skip_gain * gated_cols)


def split16(values):
    high = values.astype(jnp.bfloat16)
    low = (values - high.astype(jnp.float32)).astype(jnp.bfloat16)
    return high, low


def transform_tables(length):
    bins = np.arange(length, dtype=np.int64)[:, None]
    taps = np.arange(length, dtype=np.int64)[None, :]
    phases = ((2 * bins + 1) * taps % (4 * length)).astype(np.float64) * (math.pi / (2 * length))
    table = np.concatenate([np.cos(phases), -np.sin(phases)], axis=0).astype(np.float32)
    high = table.astype(jnp.bfloat16)
    low = (table - high.astype(np.float32)).astype(jnp.bfloat16)
    forward = np.concatenate([high, high, low], axis=1)
    inverse = np.concatenate([high.T, high.T, low.T], axis=1)
    return forward, inverse


def tile_of(t):
    return slice(t * LANES, (t + 1) * LANES)


def aligned(start, size):
    return pl.ds(pl.multiple_of(start, size), size)


def swap_tiles_and_slots(tiles, width, me, tiles_out):
    count = len(tiles)
    lane = lax.broadcasted_iota(jnp.int32, tiles[0].shape, 1)
    slot = lane // width % count
    mine = slot ^ me
    step = 1
    while step < count:
        upper = (slot & step) != 0
        other = (mine & step) != 0
        first, second = (upper, other) if tiles_out else (other, upper)
        partner = lane ^ (step * width)
        turned = list(tiles)
        for t in range(count):
            if t & step:
                continue
            low, high = tiles[t], tiles[t | step]
            moved = jnp.take_along_axis(jnp.where(first, low, high), partner, axis=1)
            kept = jnp.where(first, high, low)
            turned[t] = jnp.where(second, moved, kept)
            turned[t | step] = jnp.where(second, kept, moved)
        tiles = turned
        step *= 2
    return tiles


def short_filtered(taps, s, columns, now, before):
    shape = now.shape
    row = lax.broadcasted_iota(jnp.int32, shape, 0) % ROWS

    def later(rows):
        mixed = jnp.where(row >= ROWS - rows, before, now)
        blocks = mixed.reshape(shape[0] // ROWS, ROWS, shape[1])
        return pltpu.roll(blocks, rows, 1).reshape(shape)

    return (
        taps[s, 0:1, columns] * now
        + taps[s, 1:2, columns] * later(1)
        + taps[s, 2:3, columns] * later(2)
    )


def begun(taps, s, head):
    first = taps[s, 0:1, :] * head[0:1]
    second = taps[s, 0:1, :] * head[1:2] + taps[s, 1:2, :] * head[0:1]
    return jnp.concatenate([first, second], axis=0)


def lacked(taps, s, end):
    first = taps[s, 1:2, :] * end[1:2] + taps[s, 2:3, :] * end[0:1]
    return jnp.concatenate([first, taps[s, 2:3, :] * end[1:2]], axis=0)


def upper_half(shape, count, width):
    lane = lax.broadcasted_iota(jnp.int32, shape, 1)
    return lane // width % count // (count // 2), lane ^ (count // 2 * width)


def packed(low, high, side, count, width):
    upper, opposite = upper_half(low.shape, count, width)
    first = side == 0
    moved = jnp.take_along_axis(jnp.where(first, high, low), opposite, axis=1)
    return jnp.where(upper == side, jnp.where(first, low, high), moved)


def unpacked(tile, side, count, width, fill):
    upper, opposite = upper_half(tile.shape, count, width)
    first = side == 0
    moved = jnp.take_along_axis(tile, opposite, axis=1)
    low = jnp.where(first, tile, moved)
    high = jnp.where(first, moved, tile)
    return jnp.where(upper == side, low, fill), jnp.where(upper == side, high, fill)


def in_vmem():
    return pl.BlockSpec(memory_space=pltpu.VMEM)


def in_smem():
    return pl.BlockSpec(memory_space=pltpu.SMEM)


def in_any():
    return pl.BlockSpec(memory_space=pl.ANY)


def params_of(limit=VMEM_BYTES):
    return pltpu.CompilerParams(vmem_limit_bytes=limit)


def far_first(count):
    half = count // 2
    return [half, half + 1] + list(range(half)) + list(range(half + 2, count))


def by_partner(refs):
    ordered = [None] * len(refs)
    for k, ref in zip(far_first(len(refs)), refs):
        ordered[k] = ref
    return ordered


def far_first_operands(messages):
    return [messages[k] for k in far_first(len(messages))]


def gate_kernel(count, width, pieces, me_ref, streams, *rest):
    small, rest = rest[:3], rest[3:]
    messages, rest = rest[:count], rest[count:]
    params, key, value, query_end, taps, skip, long_filter, sems = rest
    length = streams.shape[1]
    sources = (*small, streams.at[0, pl.ds(length - ROWS, ROWS)])
    targets = (taps, skip, long_filter, query_end)
    fetches = [
        pltpu.make_async_copy(source, target, sems.at[2 * pieces + i])
        for i, (source, target) in enumerate(zip(sources, targets))
    ]
    for fetch in fetches:
        fetch.start()
    channels = streams.shape[2]
    me = me_ref[0]
    part = length // pieces
    loads = []
    for piece in range(pieces):
        for s, buffer in ((1, key), (2, value)):
            load = pltpu.make_async_copy(
                streams.at[s, pl.ds(piece * part, part)],
                buffer.at[pl.ds(ROWS + piece * part, part)],
                sems.at[2 * piece + s - 1],
            )
            load.start()
            loads.append(load)
    key[0:ROWS, :] = jnp.zeros((ROWS, channels), jnp.float32)
    value[0:ROWS, :] = jnp.zeros((ROWS, channels), jnp.float32)
    for fetch in fetches:
        fetch.wait()
    rows = jnp.concatenate(
        [taps[1], taps[2], skip[...], jnp.zeros((1, channels), jnp.float32)], axis=0
    )
    tiles = [rows[:, tile_of(t)] for t in range(count)]
    params[...] = swap_tiles_and_slots(tiles, width, me, True)[0]
    for k in range(count):
        for t in range(length // LANES):
            at = length + ROWS + t * width
            messages[k][at : at + width, :] = long_filter[aligned((me ^ k) * width, width), tile_of(t)]
    step = 8 * ROWS

    def block(i, _):
        base = i * step
        tiles = []
        for t in range(count):
            features = []
            for s, buffer in ((1, key), (2, value)):
                now = buffer[pl.ds(pl.multiple_of(base + ROWS, ROWS), step), tile_of(t)]
                before = buffer[aligned(base, step), tile_of(t)]
                features.append(short_filtered(taps, s, tile_of(t), now, before))
            tiles.append(features[0] * features[1])
        tiles = swap_tiles_and_slots(tiles, width, me, True)
        for k in range(count):
            messages[k][aligned(base, step), :] = tiles[k]
        return 0

    for piece in range(pieces):
        loads[2 * piece].wait()
        loads[2 * piece + 1].wait()
        lax.fori_loop(piece * part // step, (piece + 1) * part // step, block, 0)
    key_head, value_head = (
        begun(taps, s, buffer[ROWS : ROWS + 2, :]) for s, buffer in ((1, key), (2, value))
    )
    ends = [buffer[length + ROWS - 2 : length + ROWS, :] for buffer in (key, value)]
    rim = jnp.concatenate(
        [lacked(taps, 1, ends[0]), lacked(taps, 2, ends[1]), value_head]
        + [lacked(taps, 0, query_end[ROWS - 2 : ROWS, :])],
        axis=0,
    )
    head = jnp.concatenate([key_head, jnp.zeros((ROWS - 2, channels), jnp.float32)], axis=0)
    for rows, at, size in ((rim, length, ROWS), (head, 0, 2)):
        tiles = [rows[:, tile_of(t)] for t in range(count)]
        tiles = swap_tiles_and_slots(tiles, width, me, True)
        for k in range(count):
            messages[k][at : at + size, :] = tiles[k][0:size]


def gate(me, streams, short_filters, skip_gain, long_filter, count, width):
    length, channels = streams.shape[1], streams.shape[2]
    rows = length + ROWS + width * length // LANES
    message = jax.ShapeDtypeStruct((rows, LANES), jnp.float32)
    pieces = 4
    return pl.pallas_call(
        functools.partial(gate_kernel, count, width, pieces),
        out_shape=[message] * count + [jax.ShapeDtypeStruct((ROWS, LANES), jnp.float32)],
        in_specs=[in_smem()] + [in_any()] * 4,
        out_specs=[in_vmem()] * (count + 1),
        scratch_shapes=[
            pltpu.VMEM((length + ROWS, channels), jnp.float32),
            pltpu.VMEM((length + ROWS, channels), jnp.float32),
            pltpu.VMEM((ROWS, channels), jnp.float32),
            pltpu.VMEM(short_filters.shape, jnp.float32),
            pltpu.VMEM((1, channels), jnp.float32),
            pltpu.VMEM(long_filter.shape[::-1], jnp.float32),
            pltpu.SemaphoreType.DMA((2 * pieces + 4,)),
        ],
        compiler_params=params_of(60 * 1024 * 1024),
        name="gate",
    )(me, streams, short_filters, skip_gain.reshape(1, channels), long_filter.T)


def collect_kernel(count, width, me_ref, *rest):
    messages, out = by_partner(rest[:count]), rest[count]
    me = me_ref[0]
    rows = messages[0].shape[0]
    for k in range(count):
        out[me ^ k] = messages[k][rows - out.shape[1] : rows, :]


def collect_taps(me, messages, count, width, length):
    size = width * length // LANES
    return pl.pallas_call(
        functools.partial(collect_kernel, count, width),
        out_shape=jax.ShapeDtypeStruct((count, size, LANES), jnp.float32),
        in_specs=[in_smem()] + [in_vmem()] * count,
        out_specs=in_vmem(),
        compiler_params=params_of(),
        name="collect_taps",
    )(me, *far_first_operands(messages))


def filter_kernel(count, width, group_ref, params, forward, *rest):
    groups = len(rest) - 5
    given, (out, columns, spectrum, taps, sems) = rest[:groups], rest[groups:]
    loads = [
        pltpu.make_async_copy(source, taps.at[k], sems.at[k]) for k, source in enumerate(given)
    ]
    for load in loads:
        load.start()
    for load in loads:
        load.wait()
    length = out.shape[1] // 2
    halves = LANES // (count * width)
    group = group_ref[0]
    for p in range(count):
        for k in range(groups):
            owner = group ^ k
            for turn in range(count * halves // groups):
                at = (owner + turn * groups) // halves + (owner % halves) * count
                for t in range(length // LANES):
                    columns[p, aligned(at * width, width), tile_of(t)] = taps[
                        k, p, t * width : (t + 1) * width, :
                    ]
    for p in range(count):
        high, low = split16(columns[p])
        stacked = jnp.concatenate([high, low, high], axis=1)
        spectrum[p] = lax.dot_general(
            forward[...], stacked, (((1,), (1,)), ((), ())), preferred_element_type=jnp.float32
        )
    parity = lax.broadcasted_iota(jnp.int32, (length, LANES), 0) % 2
    sign = 1.0 - 2.0 * parity.astype(jnp.float32)
    skip = params[6:7, :]
    for d in range(count):
        real = spectrum[d, 0:length, :]
        imag = spectrum[d, length : 2 * length, :]
        if d > 0:
            real = real - sign * spectrum[d - 1, length : 2 * length, :]
            imag = imag + sign * spectrum[d - 1, 0:length, :]
        else:
            real = real + skip
        out[d, 0:length, :] = real
        out[d, length : 2 * length, :] = imag


def filter_spectra(group, params, forward, taps, count, width):
    length = taps[0].shape[1] // width * LANES
    return pl.pallas_call(
        functools.partial(filter_kernel, count, width),
        out_shape=jax.ShapeDtypeStruct((count, 2 * length, LANES), jnp.float32),
        in_specs=[in_smem()] + [in_vmem()] * 2 + [in_any()] * len(taps),
        out_specs=in_vmem(),
        scratch_shapes=[
            pltpu.VMEM((count, LANES, length), jnp.float32),
            pltpu.VMEM((count, 2 * length, LANES), jnp.float32),
            pltpu.VMEM((len(taps), *taps[0].shape), jnp.float32),
            pltpu.SemaphoreType.DMA((len(taps),)),
        ],
        compiler_params=params_of(),
        name="filter_spectra",
    )(group, params, forward, *taps)


def gated_bins_kernel(count, length, me_ref, forward, *rest):
    messages, (bins, rims, halves) = by_partner(rest[:count]), rest[count:]
    me = me_ref[0]
    rims[0] = jnp.zeros((ROWS, LANES), jnp.float32)
    for k in range(count):
        rims[(me ^ k) + 1] = messages[k][length : length + ROWS, :]
    block_rows = 2 * ROWS
    row = lax.broadcasted_iota(jnp.int32, (block_rows, LANES), 0)
    for k in range(count):
        at = aligned((me ^ k) * LANES, LANES)
        past = rims[me ^ k]
        rim = messages[k][length : length + ROWS, :]
        first = (messages[k][0:1, :] + past[0:1]) * (rim[4:5] + past[2:3])
        second = (messages[k][1:2, :] + past[1:2]) * (rim[5:6] + past[3:4])
        top = jnp.where(row == 0, first, jnp.where(row == 1, second, messages[k][0:block_rows, :]))
        for a, b, values in ((0, block_rows, top), (block_rows, length, messages[k][block_rows:length, :])):
            high, low = split16(values)
            halves[a:b, at] = high
            halves[length + a : length + b, at] = low
            halves[2 * length + a : 2 * length + b, at] = high
    for c in range(0, count, 2):
        columns = slice(c * LANES, (c + 2) * LANES)
        bins[:, columns] = jnp.dot(
            forward[...], halves[0 : 3 * length, columns], preferred_element_type=jnp.float32
        )


def gated_bins(me, forward, messages, count):
    length = forward.shape[0] // 2
    return pl.pallas_call(
        functools.partial(gated_bins_kernel, count, length),
        out_shape=[
            jax.ShapeDtypeStruct((2 * length, count * LANES), jnp.float32),
            jax.ShapeDtypeStruct((count + 1, ROWS, LANES), jnp.float32),
        ],
        in_specs=[in_smem()] + [in_vmem()] * (1 + count),
        out_specs=[in_vmem()] * 2,
        scratch_shapes=[pltpu.VMEM((3 * length, count * LANES), jnp.bfloat16)],
        compiler_params=params_of(),
        name="gated_bins",
    )(me, forward, *far_first_operands(messages))


def convolve_kernel(count, length, me_ref, inverse, spectra, bins, rims, *rest):
    half = count // 2
    (own_home, pair, odds), outs, rest = rest[:3], rest[3 : 3 + count], rest[3 + count :]
    halves, result, query_rows = rest
    me = me_ref[0]
    side = me // half
    block_rows = 2 * ROWS

    def block(i, _):
        start = pl.multiple_of(i * block_rows, block_rows)
        rows = []
        for at in (start, start + ROWS):
            real = [bins[pl.ds(at, ROWS), tile_of(r)] for r in range(count)]
            imag = [bins[pl.ds(length + at, ROWS), tile_of(r)] for r in range(count)]
            tap_real = [spectra[d, pl.ds(at, ROWS), :] for d in range(count)]
            tap_imag = [spectra[d, pl.ds(length + at, ROWS), :] for d in range(count)]
            sums = []
            for r in range(count):
                sum_real = real[r] * tap_real[0] - imag[r] * tap_imag[0]
                sum_imag = real[r] * tap_imag[0] + imag[r] * tap_real[0]
                for d in range(1, r + 1):
                    sum_real += real[r - d] * tap_real[d] - imag[r - d] * tap_imag[d]
                    sum_imag += real[r - d] * tap_imag[d] + imag[r - d] * tap_real[d]
                sums.append((sum_real, sum_imag))
            rows.append(sums)
        for r in range(count):
            for part in range(2):
                both = jnp.concatenate([rows[0][r][part], rows[1][r][part]], axis=0)
                high, low = split16(both)
                base = start + part * length
                halves[pl.ds(base, block_rows), tile_of(r)] = high
                halves[pl.ds(base + 2 * length, block_rows), tile_of(r)] = low
                halves[pl.ds(base + 4 * length, block_rows), tile_of(r)] = high
        return 0

    lax.fori_loop(0, length // block_rows, block, 0)
    for c in range(0, count, 2):
        columns = slice(c * LANES, (c + 2) * LANES)
        result[:, columns] = jnp.dot(
            inverse[...], halves[:, columns], preferred_element_type=jnp.float32
        )
    scale = 1.0 / length
    part = length // count
    rows = length // 2
    ahead = pair.shape[0] - 2 * rows
    behind = odds.shape[0] - 2 * rows
    homes = [
        own_home,
        odds.at[pl.ds(behind, rows)],
        pair.at[pl.ds(ahead, rows)],
        pair.at[pl.ds(ahead + rows, rows)],
    ]
    index = lax.broadcasted_iota(jnp.int32, (ROWS, LANES), 0)
    for k in range(half):
        r = me ^ k
        query_rows[r] = homes[k][...]
        query_rows[r ^ half] = jnp.ones((rows, LANES), jnp.float32)
        past = rims[r]
        lacking = jnp.where(index == 0, past[6:7], jnp.where(index == 1, past[7:8], 0.0))
        query_rows[r, 0:ROWS, :] += jnp.where(side == 1, lacking, 0.0)
    for k in range(count):
        for m in range(0, part, ROWS):
            for r in range(count):
                values = result[aligned((me ^ k) * part + m, ROWS), tile_of(r)] * scale
                if k >= half:
                    values *= query_rows[r, aligned((me ^ k) % half * part + m, ROWS), :]
                outs[k][pl.ds(m * count + r, ROWS, stride=count), :] = values


def convolve(me, inverse, spectra, bins, rims, homes, count):
    length = spectra.shape[1] // 2
    return pl.pallas_call(
        functools.partial(convolve_kernel, count, length),
        out_shape=[jax.ShapeDtypeStruct((length, LANES), jnp.float32)] * count,
        in_specs=[in_smem()] + [in_vmem()] * 7,
        out_specs=[in_vmem()] * count,
        scratch_shapes=[
            pltpu.VMEM((6 * length, count * LANES), jnp.bfloat16),
            pltpu.VMEM((length, count * LANES), jnp.float32),
            pltpu.VMEM((count, length // 2, LANES), jnp.float32),
        ],
        compiler_params=params_of(),
        name="convolve",
    )(me, inverse, spectra, bins, rims, *homes)


def share_sizes(count, tiles, part):
    size = tiles * (part + 2)
    return [size] * (count // 2) + [size // 2] * (count // 2)


def query_kernel(count, width, me_ref, streams, taps_in, gated, *rest):
    half = count // 2
    evens, (first_home, second_home, odds, rows, taps, sems) = rest[:half], rest[half:]
    length, channels = streams.shape[1:]
    tiles = channels // LANES
    part = length // count
    sizes = share_sizes(count, tiles, part)
    me = me_ref[0]
    other = 1 - me // half
    load = pltpu.make_async_copy(streams.at[0], rows.at[pl.ds(ROWS, length)], sems.at[0])
    fetch = pltpu.make_async_copy(taps_in, taps, sems.at[1])
    load.start()
    fetch.start()
    rows[0:ROWS, :] = jnp.zeros((ROWS, channels), jnp.float32)
    fetch.wait()
    load.wait()

    def features(base, size):
        return [
            short_filtered(
                taps,
                0,
                tile_of(t),
                rows[pl.ds(pl.multiple_of(base + ROWS, ROWS), size), tile_of(t)],
                rows[pl.ds(pl.multiple_of(base, ROWS), size), tile_of(t)],
            )
            for t in range(tiles)
        ]

    ends = lacked(taps, 0, rows[length + ROWS - 2 : length + ROWS, :])
    ends = [ends[:, tile_of(t)] for t in range(tiles)]
    at = gated.shape[0]
    odds[0:at, :] = gated[...]
    for k in range(count):
        out, ahead = (odds, at) if k % 2 else (evens[k // 2], 0)
        found = features((me ^ k) * part, part)
        lacking = ends
        if k >= half:
            found, lacking = (
                [packed(a, b, other, count, width) for a, b in zip(one[: tiles // 2], one[tiles // 2 :])]
                for one in (found, ends)
            )
        for t, (tile, end) in enumerate(zip(found, lacking)):
            out[ahead + t * part : ahead + (t + 1) * part, :] = tile
            last = ahead + len(found) * part + 2 * t
            out[last : last + 2, :] = end
        if k % 2:
            at += sizes[k]
    targets = [(first_home, 0), (odds, at), (second_home, 0), (odds, at + length // 2)]
    step = 2 * part
    for i in range(length // 2 // step):
        found = features(other * (length // 2) + i * step, step)
        found = swap_tiles_and_slots(found, width, me, True)
        for k, (out, ahead) in enumerate(targets):
            out[ahead + i * step : ahead + (i + 1) * step, :] = found[k]


def query(me, streams, short_filters, gated, count, width):
    length, channels = streams.shape[1:]
    half = count // 2
    sizes = share_sizes(count, channels // LANES, length // count)
    sizes = sizes[0::2] + [length // 2] * 2 + [gated.shape[0] + sum(sizes[1::2]) + length]
    return pl.pallas_call(
        functools.partial(query_kernel, count, width),
        out_shape=[jax.ShapeDtypeStruct((rows, LANES), jnp.float32) for rows in sizes],
        in_specs=[in_smem(), in_any(), in_any(), in_vmem()],
        out_specs=[in_vmem()] * len(sizes),
        scratch_shapes=[
            pltpu.VMEM((length + ROWS, channels), jnp.float32),
            pltpu.VMEM(short_filters.shape, jnp.float32),
            pltpu.SemaphoreType.DMA((2,)),
        ],
        compiler_params=params_of(),
        name="query",
    )(me, streams, short_filters, gated)


def hold_kernel(*refs):
    del refs


def hold(values, *others):
    return pl.pallas_call(
        hold_kernel,
        out_shape=[jax.ShapeDtypeStruct(value.shape, value.dtype) for value in values],
        in_specs=[in_any()] * (len(values) + len(others)),
        out_specs=[in_any()] * len(values),
        input_output_aliases={i: i for i in range(len(values))},
        compiler_params=params_of(),
        name="hold",
    )(*values, *others)


def pair_shares_kernel(pairs, *refs):
    evens, home, odds, outs = refs[:pairs], refs[pairs], refs[pairs + 1], refs[-pairs:]
    rows = home.shape[0]
    shares = evens[0].shape[0] + sum(even.shape[0] for even in evens)
    at = odds.shape[0] - 2 * rows - shares + evens[0].shape[0]
    for even, out in zip(evens, outs):
        size = even.shape[0]
        out[0:size, :] = even[...]
        out[size : 2 * size, :] = odds[at : at + size, :]
        at += size
    at = odds.shape[0] - rows
    behind = 2 * evens[0].shape[0]
    outs[0][behind : behind + rows, :] = home[...]
    outs[0][behind + rows : behind + 2 * rows, :] = odds[at : at + rows, :]


def pair_shares(evens, home, odds, *earlier):
    sizes = [2 * even.shape[0] for even in evens]
    sizes[0] += 2 * home.shape[0]
    return pl.pallas_call(
        functools.partial(pair_shares_kernel, len(evens)),
        out_shape=[jax.ShapeDtypeStruct((size, LANES), jnp.float32) for size in sizes],
        in_specs=[in_vmem()] * (len(evens) + 2) + [in_any()] * len(earlier),
        out_specs=[in_vmem()] * len(evens),
        compiler_params=params_of(),
        name="pair_shares",
    )(*evens, home, odds, *earlier)


def arrange_query(count, width, me, shares, out, lacking):
    half = count // 2
    tiles, rows = out.shape[:2]
    part = rows // count
    side = me // half
    lacking[...] = jnp.zeros(lacking.shape, jnp.float32)

    def put(t, r, tile, ends):
        for m in range(0, part, ROWS):
            out[t, pl.ds(m * count + r, ROWS, stride=count), :] = tile[m : m + ROWS]
        lacking[t, pl.ds(r + 1, 2, stride=2 * count), :] = ends

    for k in range(count):
        r = me ^ k
        near = k < half
        given = tiles if near else tiles // 2
        for t in range(given):
            tile = shares[k][t * part : (t + 1) * part, :]
            at = given * part + t * 2
            ends = shares[k][at : at + 2, :]
            if near:
                put(t, r, tile, ends)
            else:
                tile = unpacked(tile, side, count, width, 1.0)
                ends = unpacked(ends, side, count, width, 0.0)
                for i in range(2):
                    put(t + i * given, r, tile[i], ends[i])
    panel = lax.broadcasted_iota(jnp.int32, (count, LANES), 0)
    upper, _ = upper_half((count, LANES), count, width)
    first = jnp.where((me == 0) & ((panel < half) | (upper == 0)), 1.0, 0.0)
    for t in range(tiles):
        for m in range(2):
            at = slice(m * count, (m + 1) * count)
            out[t, at, :] += first * lacking[t, 2 * m * count : (2 * m + 1) * count, :]


def finish_kernel(count, width, pieces, me_ref, *rest):
    messages, rest = by_partner(rest[:count]), rest[count:]
    half = count // 2
    own, odds, *pairs = rest[: half + 1]
    out, rows, query_rows, lacking, sems = rest[half + 1 :]
    me = me_ref[0]
    part = out.shape[0]
    length = part * count
    sizes = share_sizes(count, query_rows.shape[0], part)
    start = odds.shape[0] - length - sum(sizes[1::2])
    shares = [own, odds.at[pl.ds(start, sizes[1])]]
    for i, pair in enumerate(pairs, 1):
        size = sizes[2 * i]
        shares += [pair.at[pl.ds(0, size)], pair.at[pl.ds(size, size)]]
    arrange_query(count, width, me, shares, query_rows, lacking)
    step = 4
    stores = []

    def block(i, _):
        at = aligned(i * step * count, step * count)
        tiles = [message[at, :] for message in messages]
        tiles = swap_tiles_and_slots(tiles, width, me, False)
        for t in range(count):
            product = query_rows[t, at, :] * tiles[t]
            for m in range(step):
                rows[i * step + m, :, tile_of(t)] = product[m * count : (m + 1) * count]
        return 0

    size = part // pieces
    for piece in range(pieces):
        lax.fori_loop(piece * size // step, (piece + 1) * size // step, block, 0)
        done = pl.ds(piece * size, size)
        store = pltpu.make_async_copy(rows.at[done], out.at[done], sems.at[piece])
        store.start()
        stores.append(store)
    for store in stores:
        store.wait()


def finish(me, messages, shares, rows, tiles, count, width):
    part = rows // count
    pieces = 4
    return pl.pallas_call(
        functools.partial(finish_kernel, count, width, pieces),
        out_shape=jax.ShapeDtypeStruct((part, count, tiles * LANES), jnp.float32),
        in_specs=[in_smem()] + [in_vmem()] * (count + len(shares)),
        out_specs=in_any(),
        scratch_shapes=[
            pltpu.VMEM((part, count, tiles * LANES), jnp.float32),
            pltpu.VMEM((tiles, rows, LANES), jnp.float32),
            pltpu.VMEM((tiles, 4 * count, LANES), jnp.float32),
            pltpu.SemaphoreType.DMA((pieces,)),
        ],
        compiler_params=params_of(),
        name="finish",
    )(me, *far_first_operands(messages), *shares)


def swapped(block, axis, k):
    return lax.ppermute(block, axis, [(i, i ^ k) for i in range(lax.axis_size(axis))])


def exchanged(messages, axis):
    received = {0: messages[0]}
    for k in range(1, len(messages)):
        received[k] = swapped(messages[k], axis, k)
    return [received[k] for k in range(len(messages))]


def wide_body(streams, short_filters, skip_gain, long_filter):
    count = lax.axis_size("seq")
    groups = lax.axis_size("grp")
    place = lax.axis_index("seq").astype(jnp.int32)
    me = place.reshape(1)
    group = lax.axis_index("grp").astype(jnp.int32).reshape(1)
    length = streams.shape[1]
    width = long_filter.shape[1] // count
    forward, inverse = (jnp.asarray(table) for table in transform_tables(length))
    *gated, params = gate(me, streams, short_filters, skip_gain, long_filter, count, width)
    half = count // 2
    tiles = streams.shape[2] // LANES
    *evens, own_home, next_home, odds = query(
        me, streams, short_filters, gated[1], count, width
    )
    gated[1] = odds
    gated = exchanged(gated, "seq")
    odds = gated[1]
    taps = collect_taps(me, gated, count, width, length)
    taps = [taps] + [swapped(taps, "grp", k) for k in range(1, groups)]
    pairs = pair_shares(evens[1:], next_home, odds, taps[1])
    pairs = [swapped(pair, "seq", 2 * i) for i, pair in enumerate(pairs, 1)]
    spectra = filter_spectra(group, params, forward, taps, count, width)
    homes = (own_home, pairs[0], odds)
    bins, rims = gated_bins(me, forward, gated, count)
    convolved = list(convolve(me, inverse, spectra, bins, rims, homes, count))
    convolved[1:half] = hold(convolved[1:half], *pairs)
    first = [swapped(convolved[k], "seq", k) for k in (half, half + 1)]
    convolved[half + 2 :] = hold(convolved[half + 2 :], *pairs, first[0])
    convolved = exchanged(convolved[:half], "seq") + first + [
        swapped(convolved[k], "seq", k) for k in range(half + 2, count)
    ]
    shares = [evens[0], odds, *pairs]
    return finish(me, convolved, shares, length, tiles, count, width)


def body(streams, short_filters, skip_gain, long_filter):
    count = lax.axis_size("seq")
    width = long_filter.shape[1] // count
    one_tile = streams.shape[2] == count * LANES and count == ROWS
    if one_tile and width == ROWS and LANES % (count * width) == 0:
        return wide_body(streams, short_filters, skip_gain, long_filter)
    return narrow_body(streams, short_filters, skip_gain, long_filter)


def solution(mesh):
    return jax.shard_map(
        body,
        mesh=mesh,
        in_specs=(P(None, "seq", "grp"), P(None, None, "grp"), P("grp"), P("seq", "grp")),
        out_specs=P("seq", None, "grp"),
        check_vma=False,
    )
```

```python
import functools
import math

import jax
import jax.numpy as jnp
import numpy as np
from jax import lax
from jax.experimental import pallas as pl
from jax.experimental.pallas import tpu as pltpu
from jax.sharding import PartitionSpec as P

LANES = 128
ROWS = 8
VMEM_BYTES = 20 * 1024 * 1024


def passed_along(block, axis, distance):
    devices = range(lax.axis_size(axis))
    route = [(i - distance, i) for i in devices if i - distance in devices]
    return lax.ppermute(block, axis, route)


def contract(pattern, matrix, values):
    return jnp.einsum(pattern, matrix, values, precision=lax.Precision.HIGHEST)


def unit_roots(row_index, col_index, period):
    phase_steps = row_index[:, None] * col_index[None, :] % period
    phases = -2.0 * math.pi / period * phase_steps.astype(jnp.float32)
    return (jnp.cos(phases), jnp.sin(phases))


def rotate(real_part, imag_part, cos_part, sin_part):
    return (
        real_part * cos_part - imag_part * sin_part,
        real_part * sin_part + imag_part * cos_part,
    )


def unrotate(real_part, imag_part, cos_part, sin_part):
    return (
        real_part * cos_part + imag_part * sin_part,
        imag_part * cos_part - real_part * sin_part,
    )


def fine_forward(cos_table, sin_table, real_part, imag_part):
    pattern = "km,imc->ikc"
    return (
        contract(pattern, cos_table, real_part) - contract(pattern, sin_table, imag_part),
        contract(pattern, cos_table, imag_part) + contract(pattern, sin_table, real_part),
    )


def fine_inverse(cos_table, sin_table, real_part, imag_part):
    pattern = "km,ikc->imc"
    return (
        contract(pattern, cos_table, real_part) + contract(pattern, sin_table, imag_part),
        contract(pattern, cos_table, imag_part) - contract(pattern, sin_table, real_part),
    )


def narrow_body(streams, short_filters, skip_gain, long_filter):
    panels = lax.axis_size("seq")
    my_panel = lax.axis_index("seq")
    length = streams.shape[1]
    channels = streams.shape[2]
    slice_len = length // panels
    points = 2 * panels * length
    rim_rows = passed_along(streams[:, length - 2 :, :], "seq", 1)
    extended = jnp.concatenate([rim_rows, streams], axis=1)
    featured = (
        short_filters[:, 0:1, :] * extended[:, 2:, :]
        + short_filters[:, 1:2, :] * extended[:, 1 : length + 1, :]
        + short_filters[:, 2:3, :] * extended[:, 0:length, :]
    )
    query_rows = featured[0]
    gated_rows = featured[1] * featured[2]
    query_cols, gated_cols, filter_cols = (
        lax.all_to_all(
            query_rows.reshape(length, 1, channels), "seq", split_axis=0, concat_axis=1, tiled=True
        ),
        lax.all_to_all(
            gated_rows.reshape(length, 1, channels), "seq", split_axis=0, concat_axis=1, tiled=True
        ),
        lax.all_to_all(
            long_filter.reshape(length, 1, long_filter.shape[1]),
            "seq",
            split_axis=0,
            concat_axis=1,
            tiled=True,
        ),
    )
    coarse = jnp.arange(2 * panels, dtype=jnp.int32)
    cross_cos, cross_sin = unit_roots(coarse, jnp.arange(panels, dtype=jnp.int32), 2 * panels)
    fine_index = jnp.arange(length, dtype=jnp.int32)
    local_cos, local_sin = unit_roots(fine_index, fine_index, length)
    own_rows = my_panel * slice_len + jnp.arange(slice_len, dtype=jnp.int32)
    twist_cos, twist_sin = unit_roots(coarse, own_rows, points)
    own_bins = 2 * my_panel + jnp.arange(2, dtype=jnp.int32)
    turn_cos, turn_sin = unit_roots(own_bins, fine_index, points)
    pattern = "kr,mrc->kmc"
    tap_real, tap_imag = rotate(
        contract(pattern, cross_cos, filter_cols),
        contract(pattern, cross_sin, filter_cols),
        twist_cos[:, :, None],
        twist_sin[:, :, None],
    )
    act_real = contract(pattern, cross_cos, gated_cols)
    act_imag = contract(pattern, cross_sin, gated_cols)
    act_real, act_imag = rotate(act_real, act_imag, twist_cos[:, :, None], twist_sin[:, :, None])
    act_real, act_imag, tap_real, tap_imag = (
        lax.all_to_all(act_real, "seq", split_axis=0, concat_axis=1, tiled=True),
        lax.all_to_all(act_imag, "seq", split_axis=0, concat_axis=1, tiled=True),
        lax.all_to_all(tap_real, "seq", split_axis=0, concat_axis=1, tiled=True),
        lax.all_to_all(tap_imag, "seq", split_axis=0, concat_axis=1, tiled=True),
    )
    act_real, act_imag = fine_forward(local_cos, local_sin, act_real, act_imag)
    tap_real, tap_imag = fine_forward(local_cos, local_sin, tap_real, tap_imag)
    tap_real, tap_imag = (
        lax.all_gather(tap_real, "grp", axis=2, tiled=True),
        lax.all_gather(tap_imag, "grp", axis=2, tiled=True),
    )
    filter_count = tap_real.shape[2]
    blocks = act_real.shape[2] // filter_count
    wide_real = act_real.reshape(2, length, blocks, filter_count)
    wide_imag = act_imag.reshape(2, length, blocks, filter_count)
    tap_wide_real = tap_real[:, :, None, :]
    tap_wide_imag = tap_imag[:, :, None, :]
    prod_real = (wide_real * tap_wide_real - wide_imag * tap_wide_imag).reshape(
        2, length, blocks * filter_count
    )
    prod_imag = (wide_real * tap_wide_imag + wide_imag * tap_wide_real).reshape(
        2, length, blocks * filter_count
    )
    back_real, back_imag = fine_inverse(local_cos, local_sin, prod_real, prod_imag)
    back_real, back_imag = unrotate(
        back_real, back_imag, turn_cos[:, :, None], turn_sin[:, :, None]
    )
    back_real, back_imag = (
        lax.all_to_all(back_real, "seq", split_axis=1, concat_axis=0, tiled=True),
        lax.all_to_all(back_imag, "seq", split_axis=1, concat_axis=0, tiled=True),
    )
    inverse_scale = 1.0 / points
    inverse_pattern = "kr,kmc->mrc"
    convolved = (
        contract(inverse_pattern, cross_cos, back_real)
        + contract(inverse_pattern, cross_sin, back_imag)
    ) * inverse_scale
    return query_cols * (convolved + skip_gain * gated_cols)


def split16(values):
    high = values.astype(jnp.bfloat16)
    low = (values - high.astype(jnp.float32)).astype(jnp.bfloat16)
    return high, low


def transform_tables(length):
    bins = np.arange(length, dtype=np.int64)[:, None]
    taps = np.arange(length, dtype=np.int64)[None, :]
    phases = ((2 * bins + 1) * taps % (4 * length)).astype(np.float64) * (math.pi / (2 * length))
    table = np.concatenate([np.cos(phases), -np.sin(phases)], axis=0).astype(np.float32)
    high = table.astype(jnp.bfloat16)
    low = (table - high.astype(np.float32)).astype(jnp.bfloat16)
    forward = np.concatenate([high, high, low], axis=1)
    inverse = np.concatenate([high.T, high.T, low.T], axis=1)
    return forward, inverse


def tile_of(t):
    return slice(t * LANES, (t + 1) * LANES)


def aligned(start, size):
    return pl.ds(pl.multiple_of(start, size), size)


def swap_tiles_and_slots(tiles, width, me, tiles_out):
    count = len(tiles)
    lane = lax.broadcasted_iota(jnp.int32, tiles[0].shape, 1)
    slot = lane // width % count
    mine = slot ^ me
    step = 1
    while step < count:
        upper = (slot & step) != 0
        other = (mine & step) != 0
        first, second = (upper, other) if tiles_out else (other, upper)
        partner = lane ^ (step * width)
        turned = list(tiles)
        for t in range(count):
            if t & step:
                continue
            low, high = tiles[t], tiles[t | step]
            moved = jnp.take_along_axis(jnp.where(first, low, high), partner, axis=1)
            kept = jnp.where(first, high, low)
            turned[t] = jnp.where(second, moved, kept)
            turned[t | step] = jnp.where(second, kept, moved)
        tiles = turned
        step *= 2
    return tiles


def short_filtered(taps, s, columns, now, before):
    shape = now.shape
    row = lax.broadcasted_iota(jnp.int32, shape, 0) % ROWS

    def later(rows):
        mixed = jnp.where(row >= ROWS - rows, before, now)
        blocks = mixed.reshape(shape[0] // ROWS, ROWS, shape[1])
        return pltpu.roll(blocks, rows, 1).reshape(shape)

    return (
        taps[s, 0:1, columns] * now
        + taps[s, 1:2, columns] * later(1)
        + taps[s, 2:3, columns] * later(2)
    )


def begun(taps, s, head):
    first = taps[s, 0:1, :] * head[0:1]
    second = taps[s, 0:1, :] * head[1:2] + taps[s, 1:2, :] * head[0:1]
    return jnp.concatenate([first, second], axis=0)


def lacked(taps, s, end):
    first = taps[s, 1:2, :] * end[1:2] + taps[s, 2:3, :] * end[0:1]
    return jnp.concatenate([first, taps[s, 2:3, :] * end[1:2]], axis=0)


def upper_half(shape, count, width):
    lane = lax.broadcasted_iota(jnp.int32, shape, 1)
    return lane // width % count // (count // 2), lane ^ (count // 2 * width)


def packed(low, high, side, count, width):
    upper, opposite = upper_half(low.shape, count, width)
    first = side == 0
    moved = jnp.take_along_axis(jnp.where(first, high, low), opposite, axis=1)
    return jnp.where(upper == side, jnp.where(first, low, high), moved)


def unpacked(tile, side, count, width, fill):
    upper, opposite = upper_half(tile.shape, count, width)
    first = side == 0
    moved = jnp.take_along_axis(tile, opposite, axis=1)
    low = jnp.where(first, tile, moved)
    high = jnp.where(first, moved, tile)
    return jnp.where(upper == side, low, fill), jnp.where(upper == side, high, fill)


def in_vmem():
    return pl.BlockSpec(memory_space=pltpu.VMEM)


def in_smem():
    return pl.BlockSpec(memory_space=pltpu.SMEM)


def in_any():
    return pl.BlockSpec(memory_space=pl.ANY)


def params_of(limit=VMEM_BYTES):
    return pltpu.CompilerParams(vmem_limit_bytes=limit)


def far_first(count):
    half = count // 2
    return [half, half + 1] + list(range(half)) + list(range(half + 2, count))


def by_partner(refs):
    ordered = [None] * len(refs)
    for k, ref in zip(far_first(len(refs)), refs):
        ordered[k] = ref
    return ordered


def far_first_operands(messages):
    return [messages[k] for k in far_first(len(messages))]


def gate_kernel(count, width, pieces, me_ref, streams, *rest):
    small, rest = rest[:3], rest[3:]
    messages, rest = rest[:count], rest[count:]
    params, key, value, query_end, taps, skip, long_filter, sems = rest
    length = streams.shape[1]
    sources = (*small, streams.at[0, pl.ds(length - ROWS, ROWS)])
    targets = (taps, skip, long_filter, query_end)
    fetches = [
        pltpu.make_async_copy(source, target, sems.at[2 * pieces + i])
        for i, (source, target) in enumerate(zip(sources, targets))
    ]
    for fetch in fetches:
        fetch.start()
    channels = streams.shape[2]
    me = me_ref[0]
    part = length // pieces
    loads = []
    for piece in range(pieces):
        for s, buffer in ((1, key), (2, value)):
            load = pltpu.make_async_copy(
                streams.at[s, pl.ds(piece * part, part)],
                buffer.at[pl.ds(ROWS + piece * part, part)],
                sems.at[2 * piece + s - 1],
            )
            load.start()
            loads.append(load)
    key[0:ROWS, :] = jnp.zeros((ROWS, channels), jnp.float32)
    value[0:ROWS, :] = jnp.zeros((ROWS, channels), jnp.float32)
    for fetch in fetches:
        fetch.wait()
    rows = jnp.concatenate(
        [taps[1], taps[2], skip[...], jnp.zeros((1, channels), jnp.float32)], axis=0
    )
    tiles = [rows[:, tile_of(t)] for t in range(count)]
    params[...] = swap_tiles_and_slots(tiles, width, me, True)[0]
    for k in range(count):
        for t in range(length // LANES):
            at = length + ROWS + t * width
            messages[k][at : at + width, :] = long_filter[aligned((me ^ k) * width, width), tile_of(t)]
    step = 8 * ROWS

    def block(i, _):
        base = i * step
        tiles = []
        for t in range(count):
            features = []
            for s, buffer in ((1, key), (2, value)):
                now = buffer[pl.ds(pl.multiple_of(base + ROWS, ROWS), step), tile_of(t)]
                before = buffer[aligned(base, step), tile_of(t)]
                features.append(short_filtered(taps, s, tile_of(t), now, before))
            tiles.append(features[0] * features[1])
        tiles = swap_tiles_and_slots(tiles, width, me, True)
        for k in range(count):
            messages[k][aligned(base, step), :] = tiles[k]
        return 0

    for piece in range(pieces):
        loads[2 * piece].wait()
        loads[2 * piece + 1].wait()
        lax.fori_loop(piece * part // step, (piece + 1) * part // step, block, 0)
    key_head, value_head = (
        begun(taps, s, buffer[ROWS : ROWS + 2, :]) for s, buffer in ((1, key), (2, value))
    )
    ends = [buffer[length + ROWS - 2 : length + ROWS, :] for buffer in (key, value)]
    rim = jnp.concatenate(
        [lacked(taps, 1, ends[0]), lacked(taps, 2, ends[1]), value_head]
        + [lacked(taps, 0, query_end[ROWS - 2 : ROWS, :])],
        axis=0,
    )
    head = jnp.concatenate([key_head, jnp.zeros((ROWS - 2, channels), jnp.float32)], axis=0)
    for rows, at, size in ((rim, length, ROWS), (head, 0, 2)):
        tiles = [rows[:, tile_of(t)] for t in range(count)]
        tiles = swap_tiles_and_slots(tiles, width, me, True)
        for k in range(count):
            messages[k][at : at + size, :] = tiles[k][0:size]


def gate(me, streams, short_filters, skip_gain, long_filter, count, width):
    length, channels = streams.shape[1], streams.shape[2]
    rows = length + ROWS + width * length // LANES
    message = jax.ShapeDtypeStruct((rows, LANES), jnp.float32)
    pieces = 4
    return pl.pallas_call(
        functools.partial(gate_kernel, count, width, pieces),
        out_shape=[message] * count + [jax.ShapeDtypeStruct((ROWS, LANES), jnp.float32)],
        in_specs=[in_smem()] + [in_any()] * 4,
        out_specs=[in_vmem()] * (count + 1),
        scratch_shapes=[
            pltpu.VMEM((length + ROWS, channels), jnp.float32),
            pltpu.VMEM((length + ROWS, channels), jnp.float32),
            pltpu.VMEM((ROWS, channels), jnp.float32),
            pltpu.VMEM(short_filters.shape, jnp.float32),
            pltpu.VMEM((1, channels), jnp.float32),
            pltpu.VMEM(long_filter.shape[::-1], jnp.float32),
            pltpu.SemaphoreType.DMA((2 * pieces + 4,)),
        ],
        compiler_params=params_of(60 * 1024 * 1024),
        name="gate",
    )(me, streams, short_filters, skip_gain.reshape(1, channels), long_filter.T)


def collect_kernel(count, width, me_ref, *rest):
    messages, out = by_partner(rest[:count]), rest[count]
    me = me_ref[0]
    rows = messages[0].shape[0]
    for k in range(count):
        out[me ^ k] = messages[k][rows - out.shape[1] : rows, :]


def collect_taps(me, messages, count, width, length):
    size = width * length // LANES
    return pl.pallas_call(
        functools.partial(collect_kernel, count, width),
        out_shape=jax.ShapeDtypeStruct((count, size, LANES), jnp.float32),
        in_specs=[in_smem()] + [in_vmem()] * count,
        out_specs=in_vmem(),
        compiler_params=params_of(),
        name="collect_taps",
    )(me, *far_first_operands(messages))


def filter_kernel(count, width, group_ref, params, forward, *rest):
    groups = len(rest) - 5
    given, (out, columns, spectrum, taps, sems) = rest[:groups], rest[groups:]
    loads = [
        pltpu.make_async_copy(source, taps.at[k], sems.at[k]) for k, source in enumerate(given)
    ]
    for load in loads:
        load.start()
    for load in loads:
        load.wait()
    length = out.shape[1] // 2
    halves = LANES // (count * width)
    group = group_ref[0]
    for p in range(count):
        for k in range(groups):
            owner = group ^ k
            for turn in range(count * halves // groups):
                at = (owner + turn * groups) // halves + (owner % halves) * count
                for t in range(length // LANES):
                    columns[p, aligned(at * width, width), tile_of(t)] = taps[
                        k, p, t * width : (t + 1) * width, :
                    ]
    for p in range(0, count, 2):
        high, low = split16(columns[p : p + 2].reshape(2 * LANES, length))
        stacked = jnp.concatenate([high, low, high], axis=1)
        both = lax.dot_general(
            forward[...], stacked, (((1,), (1,)), ((), ())), preferred_element_type=jnp.float32
        )
        spectrum[p] = both[:, 0:LANES]
        spectrum[p + 1] = both[:, LANES : 2 * LANES]
    parity = lax.broadcasted_iota(jnp.int32, (length, LANES), 0) % 2
    sign = 1.0 - 2.0 * parity.astype(jnp.float32)
    skip = params[6:7, :]
    for d in range(count):
        real = spectrum[d, 0:length, :]
        imag = spectrum[d, length : 2 * length, :]
        if d > 0:
            real = real - sign * spectrum[d - 1, length : 2 * length, :]
            imag = imag + sign * spectrum[d - 1, 0:length, :]
        else:
            real = real + skip
        out[d, 0:length, :] = real
        out[d, length : 2 * length, :] = imag


def filter_spectra(group, params, forward, taps, count, width):
    length = taps[0].shape[1] // width * LANES
    return pl.pallas_call(
        functools.partial(filter_kernel, count, width),
        out_shape=jax.ShapeDtypeStruct((count, 2 * length, LANES), jnp.float32),
        in_specs=[in_smem()] + [in_vmem()] * 2 + [in_any()] * len(taps),
        out_specs=in_vmem(),
        scratch_shapes=[
            pltpu.VMEM((count, LANES, length), jnp.float32),
            pltpu.VMEM((count, 2 * length, LANES), jnp.float32),
            pltpu.VMEM((len(taps), *taps[0].shape), jnp.float32),
            pltpu.SemaphoreType.DMA((len(taps),)),
        ],
        compiler_params=params_of(),
        name="filter_spectra",
    )(group, params, forward, *taps)


def gated_bins_kernel(count, length, me_ref, forward, *rest):
    messages, (bins, rims, halves) = by_partner(rest[:count]), rest[count:]
    me = me_ref[0]
    rims[0] = jnp.zeros((ROWS, LANES), jnp.float32)
    for k in range(count):
        rims[(me ^ k) + 1] = messages[k][length : length + ROWS, :]
    block_rows = 2 * ROWS
    row = lax.broadcasted_iota(jnp.int32, (block_rows, LANES), 0)
    for k in range(count):
        at = aligned((me ^ k) * LANES, LANES)
        past = rims[me ^ k]
        rim = messages[k][length : length + ROWS, :]
        first = (messages[k][0:1, :] + past[0:1]) * (rim[4:5] + past[2:3])
        second = (messages[k][1:2, :] + past[1:2]) * (rim[5:6] + past[3:4])
        top = jnp.where(row == 0, first, jnp.where(row == 1, second, messages[k][0:block_rows, :]))
        for a, b, values in ((0, block_rows, top), (block_rows, length, messages[k][block_rows:length, :])):
            high, low = split16(values)
            halves[a:b, at] = high
            halves[length + a : length + b, at] = low
            halves[2 * length + a : 2 * length + b, at] = high
    for c in range(0, count, 2):
        columns = slice(c * LANES, (c + 2) * LANES)
        bins[:, columns] = jnp.dot(
            forward[...], halves[0 : 3 * length, columns], preferred_element_type=jnp.float32
        )


def gated_bins(me, forward, messages, count):
    length = forward.shape[0] // 2
    return pl.pallas_call(
        functools.partial(gated_bins_kernel, count, length),
        out_shape=[
            jax.ShapeDtypeStruct((2 * length, count * LANES), jnp.float32),
            jax.ShapeDtypeStruct((count + 1, ROWS, LANES), jnp.float32),
        ],
        in_specs=[in_smem()] + [in_vmem()] * (1 + count),
        out_specs=[in_vmem()] * 2,
        scratch_shapes=[pltpu.VMEM((3 * length, count * LANES), jnp.bfloat16)],
        compiler_params=params_of(),
        name="gated_bins",
    )(me, forward, *far_first_operands(messages))


def convolve_kernel(count, length, me_ref, inverse, spectra, bins, rims, *rest):
    half = count // 2
    (own_home, pair, odds), outs, rest = rest[:3], rest[3 : 3 + count], rest[3 + count :]
    halves, result, query_rows = rest
    me = me_ref[0]
    side = me // half
    block_rows = 2 * ROWS

    def block(i, _):
        start = pl.multiple_of(i * block_rows, block_rows)
        rows = []
        for at in (start, start + ROWS):
            real = [bins[pl.ds(at, ROWS), tile_of(r)] for r in range(count)]
            imag = [bins[pl.ds(length + at, ROWS), tile_of(r)] for r in range(count)]
            tap_real = [spectra[d, pl.ds(at, ROWS), :] for d in range(count)]
            tap_imag = [spectra[d, pl.ds(length + at, ROWS), :] for d in range(count)]
            sums = []
            for r in range(count):
                sum_real = real[r] * tap_real[0] - imag[r] * tap_imag[0]
                sum_imag = real[r] * tap_imag[0] + imag[r] * tap_real[0]
                for d in range(1, r + 1):
                    sum_real += real[r - d] * tap_real[d] - imag[r - d] * tap_imag[d]
                    sum_imag += real[r - d] * tap_imag[d] + imag[r - d] * tap_real[d]
                sums.append((sum_real, sum_imag))
            rows.append(sums)
        for r in range(count):
            for part in range(2):
                both = jnp.concatenate([rows[0][r][part], rows[1][r][part]], axis=0)
                high, low = split16(both)
                base = start + part * length
                halves[pl.ds(base, block_rows), tile_of(r)] = high
                halves[pl.ds(base + 2 * length, block_rows), tile_of(r)] = low
                halves[pl.ds(base + 4 * length, block_rows), tile_of(r)] = high
        return 0

    lax.fori_loop(0, length // block_rows, block, 0)
    for c in range(0, count, 2):
        columns = slice(c * LANES, (c + 2) * LANES)
        result[:, columns] = jnp.dot(
            inverse[...], halves[:, columns], preferred_element_type=jnp.float32
        )
    scale = 1.0 / length
    part = length // count
    rows = length // 2
    ahead = pair.shape[0] - 2 * rows
    behind = odds.shape[0] - 2 * rows
    homes = [
        own_home,
        odds.at[pl.ds(behind, rows)],
        pair.at[pl.ds(ahead, rows)],
        pair.at[pl.ds(ahead + rows, rows)],
    ]
    index = lax.broadcasted_iota(jnp.int32, (ROWS, LANES), 0)
    for k in range(half):
        r = me ^ k
        query_rows[r] = homes[k][...]
        query_rows[r ^ half] = jnp.ones((rows, LANES), jnp.float32)
        past = rims[r]
        lacking = jnp.where(index == 0, past[6:7], jnp.where(index == 1, past[7:8], 0.0))
        query_rows[r, 0:ROWS, :] += jnp.where(side == 1, lacking, 0.0)
    for k in range(count):
        for m in range(0, part, ROWS):
            for r in range(count):
                values = result[aligned((me ^ k) * part + m, ROWS), tile_of(r)] * scale
                if k >= half:
                    values *= query_rows[r, aligned((me ^ k) % half * part + m, ROWS), :]
                outs[k][pl.ds(m * count + r, ROWS, stride=count), :] = values


def convolve(me, inverse, spectra, bins, rims, homes, count):
    length = spectra.shape[1] // 2
    return pl.pallas_call(
        functools.partial(convolve_kernel, count, length),
        out_shape=[jax.ShapeDtypeStruct((length, LANES), jnp.float32)] * count,
        in_specs=[in_smem()] + [in_vmem()] * 7,
        out_specs=[in_vmem()] * count,
        scratch_shapes=[
            pltpu.VMEM((6 * length, count * LANES), jnp.bfloat16),
            pltpu.VMEM((length, count * LANES), jnp.float32),
            pltpu.VMEM((count, length // 2, LANES), jnp.float32),
        ],
        compiler_params=params_of(),
        name="convolve",
    )(me, inverse, spectra, bins, rims, *homes)


def share_sizes(count, tiles, part):
    size = tiles * (part + 2)
    return [size] * (count // 2) + [size // 2] * (count // 2)


def query_kernel(count, width, me_ref, streams, taps_in, gated, *rest):
    half = count // 2
    evens, (first_home, second_home, odds, rows, taps, sems) = rest[:half], rest[half:]
    length, channels = streams.shape[1:]
    tiles = channels // LANES
    part = length // count
    sizes = share_sizes(count, tiles, part)
    me = me_ref[0]
    other = 1 - me // half
    load = pltpu.make_async_copy(streams.at[0], rows.at[pl.ds(ROWS, length)], sems.at[0])
    fetch = pltpu.make_async_copy(taps_in, taps, sems.at[1])
    load.start()
    fetch.start()
    rows[0:ROWS, :] = jnp.zeros((ROWS, channels), jnp.float32)
    fetch.wait()
    load.wait()

    def features(base, size):
        return [
            short_filtered(
                taps,
                0,
                tile_of(t),
                rows[pl.ds(pl.multiple_of(base + ROWS, ROWS), size), tile_of(t)],
                rows[pl.ds(pl.multiple_of(base, ROWS), size), tile_of(t)],
            )
            for t in range(tiles)
        ]

    ends = lacked(taps, 0, rows[length + ROWS - 2 : length + ROWS, :])
    ends = [ends[:, tile_of(t)] for t in range(tiles)]
    at = gated.shape[0]
    odds[0:at, :] = gated[...]
    for k in range(count):
        out, ahead = (odds, at) if k % 2 else (evens[k // 2], 0)
        found = features((me ^ k) * part, part)
        lacking = ends
        if k >= half:
            found, lacking = (
                [packed(a, b, other, count, width) for a, b in zip(one[: tiles // 2], one[tiles // 2 :])]
                for one in (found, ends)
            )
        for t, (tile, end) in enumerate(zip(found, lacking)):
            out[ahead + t * part : ahead + (t + 1) * part, :] = tile
            last = ahead + len(found) * part + 2 * t
            out[last : last + 2, :] = end
        if k % 2:
            at += sizes[k]
    targets = [(first_home, 0), (odds, at), (second_home, 0), (odds, at + length // 2)]
    step = 2 * part
    for i in range(length // 2 // step):
        found = features(other * (length // 2) + i * step, step)
        found = swap_tiles_and_slots(found, width, me, True)
        for k, (out, ahead) in enumerate(targets):
            out[ahead + i * step : ahead + (i + 1) * step, :] = found[k]


def query(me, streams, short_filters, gated, count, width):
    length, channels = streams.shape[1:]
    half = count // 2
    sizes = share_sizes(count, channels // LANES, length // count)
    sizes = sizes[0::2] + [length // 2] * 2 + [gated.shape[0] + sum(sizes[1::2]) + length]
    return pl.pallas_call(
        functools.partial(query_kernel, count, width),
        out_shape=[jax.ShapeDtypeStruct((rows, LANES), jnp.float32) for rows in sizes],
        in_specs=[in_smem(), in_any(), in_any(), in_vmem()],
        out_specs=[in_vmem()] * len(sizes),
        scratch_shapes=[
            pltpu.VMEM((length + ROWS, channels), jnp.float32),
            pltpu.VMEM(short_filters.shape, jnp.float32),
            pltpu.SemaphoreType.DMA((2,)),
        ],
        compiler_params=params_of(),
        name="query",
    )(me, streams, short_filters, gated)


def hold_kernel(*refs):
    del refs


def hold(values, *others):
    return pl.pallas_call(
        hold_kernel,
        out_shape=[jax.ShapeDtypeStruct(value.shape, value.dtype) for value in values],
        in_specs=[in_any()] * (len(values) + len(others)),
        out_specs=[in_any()] * len(values),
        input_output_aliases={i: i for i in range(len(values))},
        compiler_params=params_of(),
        name="hold",
    )(*values, *others)


def pair_shares_kernel(pairs, *refs):
    evens, home, odds, outs = refs[:pairs], refs[pairs], refs[pairs + 1], refs[-pairs:]
    rows = home.shape[0]
    shares = evens[0].shape[0] + sum(even.shape[0] for even in evens)
    at = odds.shape[0] - 2 * rows - shares + evens[0].shape[0]
    for even, out in zip(evens, outs):
        size = even.shape[0]
        out[0:size, :] = even[...]
        out[size : 2 * size, :] = odds[at : at + size, :]
        at += size
    at = odds.shape[0] - rows
    behind = 2 * evens[0].shape[0]
    outs[0][behind : behind + rows, :] = home[...]
    outs[0][behind + rows : behind + 2 * rows, :] = odds[at : at + rows, :]


def pair_shares(evens, home, odds, *earlier):
    sizes = [2 * even.shape[0] for even in evens]
    sizes[0] += 2 * home.shape[0]
    return pl.pallas_call(
        functools.partial(pair_shares_kernel, len(evens)),
        out_shape=[jax.ShapeDtypeStruct((size, LANES), jnp.float32) for size in sizes],
        in_specs=[in_vmem()] * (len(evens) + 2) + [in_any()] * len(earlier),
        out_specs=[in_vmem()] * len(evens),
        compiler_params=params_of(),
        name="pair_shares",
    )(*evens, home, odds, *earlier)


def arrange_query(count, width, me, shares, out, lacking):
    half = count // 2
    tiles, rows = out.shape[:2]
    part = rows // count
    side = me // half
    lacking[...] = jnp.zeros(lacking.shape, jnp.float32)

    def put(t, r, tile, ends):
        for m in range(0, part, ROWS):
            out[t, pl.ds(m * count + r, ROWS, stride=count), :] = tile[m : m + ROWS]
        lacking[t, pl.ds(r + 1, 2, stride=2 * count), :] = ends

    for k in range(count):
        r = me ^ k
        near = k < half
        given = tiles if near else tiles // 2
        for t in range(given):
            tile = shares[k][t * part : (t + 1) * part, :]
            at = given * part + t * 2
            ends = shares[k][at : at + 2, :]
            if near:
                put(t, r, tile, ends)
            else:
                tile = unpacked(tile, side, count, width, 1.0)
                ends = unpacked(ends, side, count, width, 0.0)
                for i in range(2):
                    put(t + i * given, r, tile[i], ends[i])
    panel = lax.broadcasted_iota(jnp.int32, (count, LANES), 0)
    upper, _ = upper_half((count, LANES), count, width)
    first = jnp.where((me == 0) & ((panel < half) | (upper == 0)), 1.0, 0.0)
    for t in range(tiles):
        for m in range(2):
            at = slice(m * count, (m + 1) * count)
            out[t, at, :] += first * lacking[t, 2 * m * count : (2 * m + 1) * count, :]


def arrange_kernel(count, width, me_ref, *rest):
    (own, odds, *pairs), (out, lacking) = rest[: count // 2 + 1], rest[count // 2 + 1 :]
    tiles, length = out.shape[:2]
    sizes = share_sizes(count, tiles, length // count)
    start = odds.shape[0] - length - sum(sizes[1::2])
    shares = [own, odds.at[pl.ds(start, sizes[1])]]
    for i, pair in enumerate(pairs, 1):
        size = sizes[2 * i]
        shares += [pair.at[pl.ds(0, size)], pair.at[pl.ds(size, size)]]
    arrange_query(count, width, me_ref[0], shares, out, lacking)


def arrange(me, shares, rows, tiles, count, width):
    return pl.pallas_call(
        functools.partial(arrange_kernel, count, width),
        out_shape=jax.ShapeDtypeStruct((tiles, rows, LANES), jnp.float32),
        in_specs=[in_smem()] + [in_vmem()] * len(shares),
        out_specs=in_vmem(),
        scratch_shapes=[pltpu.VMEM((tiles, 4 * count, LANES), jnp.float32)],
        compiler_params=params_of(),
        name="arrange",
    )(me, *shares)


def finish_kernel(count, width, pieces, me_ref, *rest):
    messages, rest = by_partner(rest[:count]), rest[count:]
    query_rows, out, rows, sems = rest
    me = me_ref[0]
    part = out.shape[0]
    step = 4
    stores = []

    def block(i, _):
        at = aligned(i * step * count, step * count)
        tiles = [message[at, :] for message in messages]
        tiles = swap_tiles_and_slots(tiles, width, me, False)
        for t in range(count):
            product = query_rows[t, at, :] * tiles[t]
            for m in range(step):
                rows[i * step + m, :, tile_of(t)] = product[m * count : (m + 1) * count]
        return 0

    size = part // pieces
    for piece in range(pieces):
        lax.fori_loop(piece * size // step, (piece + 1) * size // step, block, 0)
        done = pl.ds(piece * size, size)
        store = pltpu.make_async_copy(rows.at[done], out.at[done], sems.at[piece])
        store.start()
        stores.append(store)
    for store in stores:
        store.wait()


def finish(me, messages, query_rows, count, width):
    tiles, rows = query_rows.shape[:2]
    part = rows // count
    pieces = 8
    return pl.pallas_call(
        functools.partial(finish_kernel, count, width, pieces),
        out_shape=jax.ShapeDtypeStruct((part, count, tiles * LANES), jnp.float32),
        in_specs=[in_smem()] + [in_vmem()] * (count + 1),
        out_specs=in_any(),
        scratch_shapes=[
            pltpu.VMEM((part, count, tiles * LANES), jnp.float32),
            pltpu.SemaphoreType.DMA((pieces,)),
        ],
        compiler_params=params_of(),
        name="finish",
    )(me, *far_first_operands(messages), query_rows)


def swapped(block, axis, k):
    return lax.ppermute(block, axis, [(i, i ^ k) for i in range(lax.axis_size(axis))])


def exchanged(messages, axis):
    received = {0: messages[0]}
    for k in range(1, len(messages)):
        received[k] = swapped(messages[k], axis, k)
    return [received[k] for k in range(len(messages))]


def wide_body(streams, short_filters, skip_gain, long_filter):
    count = lax.axis_size("seq")
    groups = lax.axis_size("grp")
    place = lax.axis_index("seq").astype(jnp.int32)
    me = place.reshape(1)
    group = lax.axis_index("grp").astype(jnp.int32).reshape(1)
    length = streams.shape[1]
    width = long_filter.shape[1] // count
    forward, inverse = (jnp.asarray(table) for table in transform_tables(length))
    *gated, params = gate(me, streams, short_filters, skip_gain, long_filter, count, width)
    half = count // 2
    tiles = streams.shape[2] // LANES
    *evens, own_home, next_home, odds = query(
        me, streams, short_filters, gated[1], count, width
    )
    gated[1] = odds
    gated = exchanged(gated, "seq")
    odds = gated[1]
    taps = collect_taps(me, gated, count, width, length)
    taps = [taps] + [swapped(taps, "grp", k) for k in range(1, groups)]
    pairs = pair_shares(evens[1:], next_home, odds, taps[1])
    pairs = [swapped(pair, "seq", 2 * i) for i, pair in enumerate(pairs, 1)]
    spectra = filter_spectra(group, params, forward, taps, count, width)
    homes = (own_home, pairs[0], odds)
    bins, rims = gated_bins(me, forward, gated, count)
    convolved = list(convolve(me, inverse, spectra, bins, rims, homes, count))
    convolved[1:half] = hold(convolved[1:half], *pairs)
    first = [swapped(convolved[k], "seq", k) for k in (half, half + 1)]
    convolved[half + 2 :] = hold(convolved[half + 2 :], *pairs, first[0])
    convolved = exchanged(convolved[:half], "seq") + first + [
        swapped(convolved[k], "seq", k) for k in range(half + 2, count)
    ]
    query_rows = arrange(me, [evens[0], odds, *pairs], length, tiles, count, width)
    return finish(me, convolved, query_rows, count, width)


def body(streams, short_filters, skip_gain, long_filter):
    count = lax.axis_size("seq")
    width = long_filter.shape[1] // count
    one_tile = streams.shape[2] == count * LANES and count == ROWS
    if one_tile and width == ROWS and LANES % (count * width) == 0:
        return wide_body(streams, short_filters, skip_gain, long_filter)
    return narrow_body(streams, short_filters, skip_gain, long_filter)


def solution(mesh):
    return jax.shard_map(
        body,
        mesh=mesh,
        in_specs=(P(None, "seq", "grp"), P(None, None, "grp"), P("grp"), P("seq", "grp")),
        out_specs=P("seq", None, "grp"),
        check_vma=False,
    )
```

```python
import functools
import math

import jax
import jax.numpy as jnp
import numpy as np
from jax import lax
from jax.experimental import pallas as pl
from jax.experimental.pallas import tpu as pltpu
from jax.sharding import PartitionSpec as P

LANES = 128
ROWS = 8
VMEM_BYTES = 20 * 1024 * 1024


def passed_along(block, axis, distance):
    devices = range(lax.axis_size(axis))
    route = [(i - distance, i) for i in devices if i - distance in devices]
    return lax.ppermute(block, axis, route)


def contract(pattern, matrix, values):
    return jnp.einsum(pattern, matrix, values, precision=lax.Precision.HIGHEST)


def unit_roots(row_index, col_index, period):
    phase_steps = row_index[:, None] * col_index[None, :] % period
    phases = -2.0 * math.pi / period * phase_steps.astype(jnp.float32)
    return (jnp.cos(phases), jnp.sin(phases))


def rotate(real_part, imag_part, cos_part, sin_part):
    return (
        real_part * cos_part - imag_part * sin_part,
        real_part * sin_part + imag_part * cos_part,
    )


def unrotate(real_part, imag_part, cos_part, sin_part):
    return (
        real_part * cos_part + imag_part * sin_part,
        imag_part * cos_part - real_part * sin_part,
    )


def fine_forward(cos_table, sin_table, real_part, imag_part):
    pattern = "km,imc->ikc"
    return (
        contract(pattern, cos_table, real_part) - contract(pattern, sin_table, imag_part),
        contract(pattern, cos_table, imag_part) + contract(pattern, sin_table, real_part),
    )


def fine_inverse(cos_table, sin_table, real_part, imag_part):
    pattern = "km,ikc->imc"
    return (
        contract(pattern, cos_table, real_part) + contract(pattern, sin_table, imag_part),
        contract(pattern, cos_table, imag_part) - contract(pattern, sin_table, real_part),
    )


def narrow_body(streams, short_filters, skip_gain, long_filter):
    panels = lax.axis_size("seq")
    my_panel = lax.axis_index("seq")
    length = streams.shape[1]
    channels = streams.shape[2]
    slice_len = length // panels
    points = 2 * panels * length
    rim_rows = passed_along(streams[:, length - 2 :, :], "seq", 1)
    extended = jnp.concatenate([rim_rows, streams], axis=1)
    featured = (
        short_filters[:, 0:1, :] * extended[:, 2:, :]
        + short_filters[:, 1:2, :] * extended[:, 1 : length + 1, :]
        + short_filters[:, 2:3, :] * extended[:, 0:length, :]
    )
    query_rows = featured[0]
    gated_rows = featured[1] * featured[2]
    query_cols, gated_cols, filter_cols = (
        lax.all_to_all(
            query_rows.reshape(length, 1, channels), "seq", split_axis=0, concat_axis=1, tiled=True
        ),
        lax.all_to_all(
            gated_rows.reshape(length, 1, channels), "seq", split_axis=0, concat_axis=1, tiled=True
        ),
        lax.all_to_all(
            long_filter.reshape(length, 1, long_filter.shape[1]),
            "seq",
            split_axis=0,
            concat_axis=1,
            tiled=True,
        ),
    )
    coarse = jnp.arange(2 * panels, dtype=jnp.int32)
    cross_cos, cross_sin = unit_roots(coarse, jnp.arange(panels, dtype=jnp.int32), 2 * panels)
    fine_index = jnp.arange(length, dtype=jnp.int32)
    local_cos, local_sin = unit_roots(fine_index, fine_index, length)
    own_rows = my_panel * slice_len + jnp.arange(slice_len, dtype=jnp.int32)
    twist_cos, twist_sin = unit_roots(coarse, own_rows, points)
    own_bins = 2 * my_panel + jnp.arange(2, dtype=jnp.int32)
    turn_cos, turn_sin = unit_roots(own_bins, fine_index, points)
    pattern = "kr,mrc->kmc"
    tap_real, tap_imag = rotate(
        contract(pattern, cross_cos, filter_cols),
        contract(pattern, cross_sin, filter_cols),
        twist_cos[:, :, None],
        twist_sin[:, :, None],
    )
    act_real = contract(pattern, cross_cos, gated_cols)
    act_imag = contract(pattern, cross_sin, gated_cols)
    act_real, act_imag = rotate(act_real, act_imag, twist_cos[:, :, None], twist_sin[:, :, None])
    act_real, act_imag, tap_real, tap_imag = (
        lax.all_to_all(act_real, "seq", split_axis=0, concat_axis=1, tiled=True),
        lax.all_to_all(act_imag, "seq", split_axis=0, concat_axis=1, tiled=True),
        lax.all_to_all(tap_real, "seq", split_axis=0, concat_axis=1, tiled=True),
        lax.all_to_all(tap_imag, "seq", split_axis=0, concat_axis=1, tiled=True),
    )
    act_real, act_imag = fine_forward(local_cos, local_sin, act_real, act_imag)
    tap_real, tap_imag = fine_forward(local_cos, local_sin, tap_real, tap_imag)
    tap_real, tap_imag = (
        lax.all_gather(tap_real, "grp", axis=2, tiled=True),
        lax.all_gather(tap_imag, "grp", axis=2, tiled=True),
    )
    filter_count = tap_real.shape[2]
    blocks = act_real.shape[2] // filter_count
    wide_real = act_real.reshape(2, length, blocks, filter_count)
    wide_imag = act_imag.reshape(2, length, blocks, filter_count)
    tap_wide_real = tap_real[:, :, None, :]
    tap_wide_imag = tap_imag[:, :, None, :]
    prod_real = (wide_real * tap_wide_real - wide_imag * tap_wide_imag).reshape(
        2, length, blocks * filter_count
    )
    prod_imag = (wide_real * tap_wide_imag + wide_imag * tap_wide_real).reshape(
        2, length, blocks * filter_count
    )
    back_real, back_imag = fine_inverse(local_cos, local_sin, prod_real, prod_imag)
    back_real, back_imag = unrotate(
        back_real, back_imag, turn_cos[:, :, None], turn_sin[:, :, None]
    )
    back_real, back_imag = (
        lax.all_to_all(back_real, "seq", split_axis=1, concat_axis=0, tiled=True),
        lax.all_to_all(back_imag, "seq", split_axis=1, concat_axis=0, tiled=True),
    )
    inverse_scale = 1.0 / points
    inverse_pattern = "kr,kmc->mrc"
    convolved = (
        contract(inverse_pattern, cross_cos, back_real)
        + contract(inverse_pattern, cross_sin, back_imag)
    ) * inverse_scale
    return query_cols * (convolved + skip_gain * gated_cols)


def split16(values):
    high = values.astype(jnp.bfloat16)
    low = (values - high.astype(jnp.float32)).astype(jnp.bfloat16)
    return high, low


def transform_tables(length):
    bins = np.arange(length, dtype=np.int64)[:, None]
    taps = np.arange(length, dtype=np.int64)[None, :]
    phases = ((2 * bins + 1) * taps % (4 * length)).astype(np.float64) * (math.pi / (2 * length))
    table = np.concatenate([np.cos(phases), -np.sin(phases)], axis=0).astype(np.float32)
    high = table.astype(jnp.bfloat16)
    low = (table - high.astype(np.float32)).astype(jnp.bfloat16)
    forward = np.concatenate([high, high, low], axis=1)
    inverse = np.concatenate([high.T, high.T, low.T], axis=1)
    return forward, inverse


def tile_of(t):
    return slice(t * LANES, (t + 1) * LANES)


def aligned(start, size):
    return pl.ds(pl.multiple_of(start, size), size)


def swap_tiles_and_slots(tiles, width, me, tiles_out):
    count = len(tiles)
    lane = lax.broadcasted_iota(jnp.int32, tiles[0].shape, 1)
    slot = lane // width % count
    mine = slot ^ me
    step = 1
    while step < count:
        upper = (slot & step) != 0
        other = (mine & step) != 0
        first, second = (upper, other) if tiles_out else (other, upper)
        partner = lane ^ (step * width)
        turned = list(tiles)
        for t in range(count):
            if t & step:
                continue
            low, high = tiles[t], tiles[t | step]
            moved = jnp.take_along_axis(jnp.where(first, low, high), partner, axis=1)
            kept = jnp.where(first, high, low)
            turned[t] = jnp.where(second, moved, kept)
            turned[t | step] = jnp.where(second, kept, moved)
        tiles = turned
        step *= 2
    return tiles


def short_filtered(taps, s, columns, now, before):
    shape = now.shape
    row = lax.broadcasted_iota(jnp.int32, shape, 0) % ROWS

    def later(rows):
        mixed = jnp.where(row >= ROWS - rows, before, now)
        blocks = mixed.reshape(shape[0] // ROWS, ROWS, shape[1])
        return pltpu.roll(blocks, rows, 1).reshape(shape)

    return (
        taps[s, 0:1, columns] * now
        + taps[s, 1:2, columns] * later(1)
        + taps[s, 2:3, columns] * later(2)
    )


def begun(taps, s, head):
    first = taps[s, 0:1, :] * head[0:1]
    second = taps[s, 0:1, :] * head[1:2] + taps[s, 1:2, :] * head[0:1]
    return jnp.concatenate([first, second], axis=0)


def lacked(taps, s, end):
    first = taps[s, 1:2, :] * end[1:2] + taps[s, 2:3, :] * end[0:1]
    return jnp.concatenate([first, taps[s, 2:3, :] * end[1:2]], axis=0)


def upper_half(shape, count, width):
    lane = lax.broadcasted_iota(jnp.int32, shape, 1)
    return lane // width % count // (count // 2), lane ^ (count // 2 * width)


def packed(low, high, side, count, width):
    upper, opposite = upper_half(low.shape, count, width)
    first = side == 0
    moved = jnp.take_along_axis(jnp.where(first, high, low), opposite, axis=1)
    return jnp.where(upper == side, jnp.where(first, low, high), moved)


def unpacked(tile, side, count, width, fill):
    upper, opposite = upper_half(tile.shape, count, width)
    first = side == 0
    moved = jnp.take_along_axis(tile, opposite, axis=1)
    low = jnp.where(first, tile, moved)
    high = jnp.where(first, moved, tile)
    return jnp.where(upper == side, low, fill), jnp.where(upper == side, high, fill)


def in_vmem():
    return pl.BlockSpec(memory_space=pltpu.VMEM)


def in_smem():
    return pl.BlockSpec(memory_space=pltpu.SMEM)


def in_any():
    return pl.BlockSpec(memory_space=pl.ANY)


def params_of(limit=VMEM_BYTES):
    return pltpu.CompilerParams(vmem_limit_bytes=limit)


def far_first(count):
    half = count // 2
    return [half, half + 1] + list(range(half)) + list(range(half + 2, count))


def by_partner(refs):
    ordered = [None] * len(refs)
    for k, ref in zip(far_first(len(refs)), refs):
        ordered[k] = ref
    return ordered


def far_first_operands(messages):
    return [messages[k] for k in far_first(len(messages))]


def gate_kernel(count, width, pieces, me_ref, streams, *rest):
    small, rest = rest[:3], rest[3:]
    messages, rest = rest[:count], rest[count:]
    params, key, value, query_end, taps, skip, long_filter, sems = rest
    length = streams.shape[1]
    sources = (*small, streams.at[0, pl.ds(length - ROWS, ROWS)])
    targets = (taps, skip, long_filter, query_end)
    fetches = [
        pltpu.make_async_copy(source, target, sems.at[2 * pieces + i])
        for i, (source, target) in enumerate(zip(sources, targets))
    ]
    channels = streams.shape[2]
    me = me_ref[0]
    part = length // pieces
    loads = []
    for piece in range(pieces):
        for s, buffer in ((1, key), (2, value)):
            load = pltpu.make_async_copy(
                streams.at[s, pl.ds(piece * part, part)],
                buffer.at[pl.ds(ROWS + piece * part, part)],
                sems.at[2 * piece + s - 1],
            )
            load.start()
            loads.append(load)
        if piece == 0:
            for fetch in fetches:
                fetch.start()
    key[0:ROWS, :] = jnp.zeros((ROWS, channels), jnp.float32)
    value[0:ROWS, :] = jnp.zeros((ROWS, channels), jnp.float32)
    for fetch in fetches:
        fetch.wait()
    rows = jnp.concatenate(
        [taps[1], taps[2], skip[...], jnp.zeros((1, channels), jnp.float32)], axis=0
    )
    tiles = [rows[:, tile_of(t)] for t in range(count)]
    params[...] = swap_tiles_and_slots(tiles, width, me, True)[0]
    for k in range(count):
        for t in range(length // LANES):
            at = length + ROWS + t * width
            messages[k][at : at + width, :] = long_filter[aligned((me ^ k) * width, width), tile_of(t)]
    step = 8 * ROWS

    def block(i, _):
        base = i * step
        tiles = []
        for t in range(count):
            features = []
            for s, buffer in ((1, key), (2, value)):
                now = buffer[pl.ds(pl.multiple_of(base + ROWS, ROWS), step), tile_of(t)]
                before = buffer[aligned(base, step), tile_of(t)]
                features.append(short_filtered(taps, s, tile_of(t), now, before))
            tiles.append(features[0] * features[1])
        tiles = swap_tiles_and_slots(tiles, width, me, True)
        for k in range(count):
            messages[k][aligned(base, step), :] = tiles[k]
        return 0

    for piece in range(pieces):
        loads[2 * piece].wait()
        loads[2 * piece + 1].wait()
        lax.fori_loop(piece * part // step, (piece + 1) * part // step, block, 0)
    key_head, value_head = (
        begun(taps, s, buffer[ROWS : ROWS + 2, :]) for s, buffer in ((1, key), (2, value))
    )
    ends = [buffer[length + ROWS - 2 : length + ROWS, :] for buffer in (key, value)]
    rim = jnp.concatenate(
        [lacked(taps, 1, ends[0]), lacked(taps, 2, ends[1]), value_head]
        + [lacked(taps, 0, query_end[ROWS - 2 : ROWS, :])],
        axis=0,
    )
    head = jnp.concatenate([key_head, jnp.zeros((ROWS - 2, channels), jnp.float32)], axis=0)
    for rows, at, size in ((rim, length, ROWS), (head, 0, 2)):
        tiles = [rows[:, tile_of(t)] for t in range(count)]
        tiles = swap_tiles_and_slots(tiles, width, me, True)
        for k in range(count):
            messages[k][at : at + size, :] = tiles[k][0:size]


def gate(me, streams, short_filters, skip_gain, long_filter, count, width):
    length, channels = streams.shape[1], streams.shape[2]
    rows = length + ROWS + width * length // LANES
    message = jax.ShapeDtypeStruct((rows, LANES), jnp.float32)
    pieces = 4
    return pl.pallas_call(
        functools.partial(gate_kernel, count, width, pieces),
        out_shape=[message] * count + [jax.ShapeDtypeStruct((ROWS, LANES), jnp.float32)],
        in_specs=[in_smem()] + [in_any()] * 4,
        out_specs=[in_vmem()] * (count + 1),
        scratch_shapes=[
            pltpu.VMEM((length + ROWS, channels), jnp.float32),
            pltpu.VMEM((length + ROWS, channels), jnp.float32),
            pltpu.VMEM((ROWS, channels), jnp.float32),
            pltpu.VMEM(short_filters.shape, jnp.float32),
            pltpu.VMEM((1, channels), jnp.float32),
            pltpu.VMEM(long_filter.shape[::-1], jnp.float32),
            pltpu.SemaphoreType.DMA((2 * pieces + 4,)),
        ],
        compiler_params=params_of(60 * 1024 * 1024),
        name="gate",
    )(me, streams, short_filters, skip_gain.reshape(1, channels), long_filter.T)


def collect_kernel(count, width, me_ref, *rest):
    messages, out = by_partner(rest[:count]), rest[count]
    me = me_ref[0]
    rows = messages[0].shape[0]
    for k in range(count):
        out[me ^ k] = messages[k][rows - out.shape[1] : rows, :]


def collect_taps(me, messages, count, width, length):
    size = width * length // LANES
    return pl.pallas_call(
        functools.partial(collect_kernel, count, width),
        out_shape=jax.ShapeDtypeStruct((count, size, LANES), jnp.float32),
        in_specs=[in_smem()] + [in_vmem()] * count,
        out_specs=in_vmem(),
        compiler_params=params_of(),
        name="collect_taps",
    )(me, *far_first_operands(messages))


def filter_kernel(count, width, group_ref, params, forward, *rest):
    groups = len(rest) - 5
    given, (out, columns, spectrum, taps, sems) = rest[:groups], rest[groups:]
    loads = [
        pltpu.make_async_copy(source, taps.at[k], sems.at[k]) for k, source in enumerate(given)
    ]
    for load in loads:
        load.start()
    for load in loads:
        load.wait()
    length = out.shape[1] // 2
    halves = LANES // (count * width)
    group = group_ref[0]
    for p in range(count):
        for k in range(groups):
            owner = group ^ k
            for turn in range(count * halves // groups):
                at = (owner + turn * groups) // halves + (owner % halves) * count
                for t in range(length // LANES):
                    columns[p, aligned(at * width, width), tile_of(t)] = taps[
                        k, p, t * width : (t + 1) * width, :
                    ]
    for p in range(0, count, 2):
        high, low = split16(columns[p : p + 2].reshape(2 * LANES, length))
        stacked = jnp.concatenate([high, low, high], axis=1)
        both = lax.dot_general(
            forward[...], stacked, (((1,), (1,)), ((), ())), preferred_element_type=jnp.float32
        )
        spectrum[p] = both[:, 0:LANES]
        spectrum[p + 1] = both[:, LANES : 2 * LANES]
    parity = lax.broadcasted_iota(jnp.int32, (length, LANES), 0) % 2
    sign = 1.0 - 2.0 * parity.astype(jnp.float32)
    skip = params[6:7, :]
    for d in range(count):
        real = spectrum[d, 0:length, :]
        imag = spectrum[d, length : 2 * length, :]
        if d > 0:
            real = real - sign * spectrum[d - 1, length : 2 * length, :]
            imag = imag + sign * spectrum[d - 1, 0:length, :]
        else:
            real = real + skip
        out[d, 0:length, :] = real
        out[d, length : 2 * length, :] = imag


def filter_spectra(group, params, forward, taps, count, width):
    length = taps[0].shape[1] // width * LANES
    return pl.pallas_call(
        functools.partial(filter_kernel, count, width),
        out_shape=jax.ShapeDtypeStruct((count, 2 * length, LANES), jnp.float32),
        in_specs=[in_smem()] + [in_vmem()] * 2 + [in_any()] * len(taps),
        out_specs=in_vmem(),
        scratch_shapes=[
            pltpu.VMEM((count, LANES, length), jnp.float32),
            pltpu.VMEM((count, 2 * length, LANES), jnp.float32),
            pltpu.VMEM((len(taps), *taps[0].shape), jnp.float32),
            pltpu.SemaphoreType.DMA((len(taps),)),
        ],
        compiler_params=params_of(),
        name="filter_spectra",
    )(group, params, forward, *taps)


def gated_bins_kernel(count, length, me_ref, forward, *rest):
    messages, (bins, rims, halves) = by_partner(rest[:count]), rest[count:]
    me = me_ref[0]
    rims[0] = jnp.zeros((ROWS, LANES), jnp.float32)
    for k in range(count):
        rims[(me ^ k) + 1] = messages[k][length : length + ROWS, :]
    block_rows = 2 * ROWS
    row = lax.broadcasted_iota(jnp.int32, (block_rows, LANES), 0)
    for k in range(count):
        at = aligned((me ^ k) * LANES, LANES)
        past = rims[me ^ k]
        rim = messages[k][length : length + ROWS, :]
        first = (messages[k][0:1, :] + past[0:1]) * (rim[4:5] + past[2:3])
        second = (messages[k][1:2, :] + past[1:2]) * (rim[5:6] + past[3:4])
        top = jnp.where(row == 0, first, jnp.where(row == 1, second, messages[k][0:block_rows, :]))
        for a, b, values in ((0, block_rows, top), (block_rows, length, messages[k][block_rows:length, :])):
            high, low = split16(values)
            halves[a:b, at] = high
            halves[length + a : length + b, at] = low
            halves[2 * length + a : 2 * length + b, at] = high
    for c in range(0, count, 2):
        columns = slice(c * LANES, (c + 2) * LANES)
        bins[:, columns] = jnp.dot(
            forward[...], halves[0 : 3 * length, columns], preferred_element_type=jnp.float32
        )


def gated_bins(me, forward, messages, count):
    length = forward.shape[0] // 2
    return pl.pallas_call(
        functools.partial(gated_bins_kernel, count, length),
        out_shape=[
            jax.ShapeDtypeStruct((2 * length, count * LANES), jnp.float32),
            jax.ShapeDtypeStruct((count + 1, ROWS, LANES), jnp.float32),
        ],
        in_specs=[in_smem()] + [in_vmem()] * (1 + count),
        out_specs=[in_vmem()] * 2,
        scratch_shapes=[pltpu.VMEM((3 * length, count * LANES), jnp.bfloat16)],
        compiler_params=params_of(),
        name="gated_bins",
    )(me, forward, *far_first_operands(messages))


def convolve_kernel(count, length, me_ref, inverse, spectra, bins, rims, *rest):
    half = count // 2
    (own_home, pair, odds), outs, rest = rest[:3], rest[3 : 3 + count], rest[3 + count :]
    halves, result, query_rows = rest
    me = me_ref[0]
    side = me // half
    block_rows = 2 * ROWS

    def block(i, _):
        start = pl.multiple_of(i * block_rows, block_rows)
        rows = []
        for at in (start, start + ROWS):
            real = [bins[pl.ds(at, ROWS), tile_of(r)] for r in range(count)]
            imag = [bins[pl.ds(length + at, ROWS), tile_of(r)] for r in range(count)]
            tap_real = [spectra[d, pl.ds(at, ROWS), :] for d in range(count)]
            tap_imag = [spectra[d, pl.ds(length + at, ROWS), :] for d in range(count)]
            sums = []
            for r in range(count):
                sum_real = real[r] * tap_real[0] - imag[r] * tap_imag[0]
                sum_imag = real[r] * tap_imag[0] + imag[r] * tap_real[0]
                for d in range(1, r + 1):
                    sum_real += real[r - d] * tap_real[d] - imag[r - d] * tap_imag[d]
                    sum_imag += real[r - d] * tap_imag[d] + imag[r - d] * tap_real[d]
                sums.append((sum_real, sum_imag))
            rows.append(sums)
        for r in range(count):
            for part in range(2):
                both = jnp.concatenate([rows[0][r][part], rows[1][r][part]], axis=0)
                high, low = split16(both)
                base = start + part * length
                halves[pl.ds(base, block_rows), tile_of(r)] = high
                halves[pl.ds(base + 2 * length, block_rows), tile_of(r)] = low
                halves[pl.ds(base + 4 * length, block_rows), tile_of(r)] = high
        return 0

    lax.fori_loop(0, length // block_rows, block, 0)
    for c in range(0, count, 2):
        columns = slice(c * LANES, (c + 2) * LANES)
        result[:, columns] = jnp.dot(
            inverse[...], halves[:, columns], preferred_element_type=jnp.float32
        )
    scale = 1.0 / length
    part = length // count
    rows = length // 2
    ahead = pair.shape[0] - 2 * rows
    behind = odds.shape[0] - 2 * rows
    homes = [
        own_home,
        odds.at[pl.ds(behind, rows)],
        pair.at[pl.ds(ahead, rows)],
        pair.at[pl.ds(ahead + rows, rows)],
    ]
    index = lax.broadcasted_iota(jnp.int32, (ROWS, LANES), 0)
    for k in range(half):
        r = me ^ k
        query_rows[r] = homes[k][...]
        query_rows[r ^ half] = jnp.ones((rows, LANES), jnp.float32)
        past = rims[r]
        lacking = jnp.where(index == 0, past[6:7], jnp.where(index == 1, past[7:8], 0.0))
        query_rows[r, 0:ROWS, :] += jnp.where(side == 1, lacking, 0.0)
    for k in range(count):
        for m in range(0, part, ROWS):
            for r in range(count):
                values = result[aligned((me ^ k) * part + m, ROWS), tile_of(r)] * scale
                if k >= half:
                    values *= query_rows[r, aligned((me ^ k) % half * part + m, ROWS), :]
                outs[k][pl.ds(m * count + r, ROWS, stride=count), :] = values


def convolve(me, inverse, spectra, bins, rims, homes, count):
    length = spectra.shape[1] // 2
    return pl.pallas_call(
        functools.partial(convolve_kernel, count, length),
        out_shape=[jax.ShapeDtypeStruct((length, LANES), jnp.float32)] * count,
        in_specs=[in_smem()] + [in_vmem()] * 7,
        out_specs=[in_vmem()] * count,
        scratch_shapes=[
            pltpu.VMEM((6 * length, count * LANES), jnp.bfloat16),
            pltpu.VMEM((length, count * LANES), jnp.float32),
            pltpu.VMEM((count, length // 2, LANES), jnp.float32),
        ],
        compiler_params=params_of(),
        name="convolve",
    )(me, inverse, spectra, bins, rims, *homes)


def share_sizes(count, tiles, part):
    size = tiles * (part + 2)
    return [size] * (count // 2) + [size // 2] * (count // 2)


def query_kernel(count, width, me_ref, streams, taps_in, gated, *rest):
    half = count // 2
    evens, (first_home, second_home, odds, rows, taps, sems) = rest[:half], rest[half:]
    length, channels = streams.shape[1:]
    tiles = channels // LANES
    part = length // count
    sizes = share_sizes(count, tiles, part)
    me = me_ref[0]
    other = 1 - me // half
    load = pltpu.make_async_copy(streams.at[0], rows.at[pl.ds(ROWS, length)], sems.at[0])
    fetch = pltpu.make_async_copy(taps_in, taps, sems.at[1])
    load.start()
    fetch.start()
    rows[0:ROWS, :] = jnp.zeros((ROWS, channels), jnp.float32)
    fetch.wait()
    load.wait()

    def features(base, size):
        return [
            short_filtered(
                taps,
                0,
                tile_of(t),
                rows[pl.ds(pl.multiple_of(base + ROWS, ROWS), size), tile_of(t)],
                rows[pl.ds(pl.multiple_of(base, ROWS), size), tile_of(t)],
            )
            for t in range(tiles)
        ]

    ends = lacked(taps, 0, rows[length + ROWS - 2 : length + ROWS, :])
    ends = [ends[:, tile_of(t)] for t in range(tiles)]
    at = gated.shape[0]
    odds[0:at, :] = gated[...]
    for k in range(count):
        out, ahead = (odds, at) if k % 2 else (evens[k // 2], 0)
        found = features((me ^ k) * part, part)
        lacking = ends
        if k >= half:
            found, lacking = (
                [packed(a, b, other, count, width) for a, b in zip(one[: tiles // 2], one[tiles // 2 :])]
                for one in (found, ends)
            )
        for t, (tile, end) in enumerate(zip(found, lacking)):
            out[ahead + t * part : ahead + (t + 1) * part, :] = tile
            last = ahead + len(found) * part + 2 * t
            out[last : last + 2, :] = end
        if k % 2:
            at += sizes[k]
    targets = [(first_home, 0), (odds, at), (second_home, 0), (odds, at + length // 2)]
    step = 2 * part
    for i in range(length // 2 // step):
        found = features(other * (length // 2) + i * step, step)
        found = swap_tiles_and_slots(found, width, me, True)
        for k, (out, ahead) in enumerate(targets):
            out[ahead + i * step : ahead + (i + 1) * step, :] = found[k]


def query(me, streams, short_filters, gated, count, width):
    length, channels = streams.shape[1:]
    half = count // 2
    sizes = share_sizes(count, channels // LANES, length // count)
    sizes = sizes[0::2] + [length // 2] * 2 + [gated.shape[0] + sum(sizes[1::2]) + length]
    return pl.pallas_call(
        functools.partial(query_kernel, count, width),
        out_shape=[jax.ShapeDtypeStruct((rows, LANES), jnp.float32) for rows in sizes],
        in_specs=[in_smem(), in_any(), in_any(), in_vmem()],
        out_specs=[in_vmem()] * len(sizes),
        scratch_shapes=[
            pltpu.VMEM((length + ROWS, channels), jnp.float32),
            pltpu.VMEM(short_filters.shape, jnp.float32),
            pltpu.SemaphoreType.DMA((2,)),
        ],
        compiler_params=params_of(),
        name="query",
    )(me, streams, short_filters, gated)


def hold_kernel(*refs):
    del refs


def hold(values, *others):
    return pl.pallas_call(
        hold_kernel,
        out_shape=[jax.ShapeDtypeStruct(value.shape, value.dtype) for value in values],
        in_specs=[in_any()] * (len(values) + len(others)),
        out_specs=[in_any()] * len(values),
        input_output_aliases={i: i for i in range(len(values))},
        compiler_params=params_of(),
        name="hold",
    )(*values, *others)


def pair_shares_kernel(pairs, *refs):
    evens, home, odds, outs = refs[:pairs], refs[pairs], refs[pairs + 1], refs[-pairs:]
    rows = home.shape[0]
    shares = evens[0].shape[0] + sum(even.shape[0] for even in evens)
    at = odds.shape[0] - 2 * rows - shares + evens[0].shape[0]
    for even, out in zip(evens, outs):
        size = even.shape[0]
        out[0:size, :] = even[...]
        out[size : 2 * size, :] = odds[at : at + size, :]
        at += size
    at = odds.shape[0] - rows
    behind = 2 * evens[0].shape[0]
    outs[0][behind : behind + rows, :] = home[...]
    outs[0][behind + rows : behind + 2 * rows, :] = odds[at : at + rows, :]


def pair_shares(evens, home, odds, *earlier):
    sizes = [2 * even.shape[0] for even in evens]
    sizes[0] += 2 * home.shape[0]
    return pl.pallas_call(
        functools.partial(pair_shares_kernel, len(evens)),
        out_shape=[jax.ShapeDtypeStruct((size, LANES), jnp.float32) for size in sizes],
        in_specs=[in_vmem()] * (len(evens) + 2) + [in_any()] * len(earlier),
        out_specs=[in_vmem()] * len(evens),
        compiler_params=params_of(),
        name="pair_shares",
    )(*evens, home, odds, *earlier)


def arrange_query(count, width, me, shares, out, lacking):
    half = count // 2
    tiles, rows = out.shape[:2]
    part = rows // count
    side = me // half
    lacking[...] = jnp.zeros(lacking.shape, jnp.float32)

    def put(t, r, tile, ends):
        for m in range(0, part, ROWS):
            out[t, pl.ds(m * count + r, ROWS, stride=count), :] = tile[m : m + ROWS]
        lacking[t, pl.ds(r + 1, 2, stride=2 * count), :] = ends

    for k in range(count):
        r = me ^ k
        near = k < half
        given = tiles if near else tiles // 2
        for t in range(given):
            tile = shares[k][t * part : (t + 1) * part, :]
            at = given * part + t * 2
            ends = shares[k][at : at + 2, :]
            if near:
                put(t, r, tile, ends)
            else:
                tile = unpacked(tile, side, count, width, 1.0)
                ends = unpacked(ends, side, count, width, 0.0)
                for i in range(2):
                    put(t + i * given, r, tile[i], ends[i])
    panel = lax.broadcasted_iota(jnp.int32, (count, LANES), 0)
    upper, _ = upper_half((count, LANES), count, width)
    first = jnp.where((me == 0) & ((panel < half) | (upper == 0)), 1.0, 0.0)
    for t in range(tiles):
        for m in range(2):
            at = slice(m * count, (m + 1) * count)
            out[t, at, :] += first * lacking[t, 2 * m * count : (2 * m + 1) * count, :]


def arrange_kernel(count, width, me_ref, *rest):
    (own, odds, *pairs), (out, lacking) = rest[: count // 2 + 1], rest[count // 2 + 1 :]
    tiles, length = out.shape[:2]
    sizes = share_sizes(count, tiles, length // count)
    start = odds.shape[0] - length - sum(sizes[1::2])
    shares = [own, odds.at[pl.ds(start, sizes[1])]]
    for i, pair in enumerate(pairs, 1):
        size = sizes[2 * i]
        shares += [pair.at[pl.ds(0, size)], pair.at[pl.ds(size, size)]]
    arrange_query(count, width, me_ref[0], shares, out, lacking)


def arrange(me, shares, rows, tiles, count, width):
    return pl.pallas_call(
        functools.partial(arrange_kernel, count, width),
        out_shape=jax.ShapeDtypeStruct((tiles, rows, LANES), jnp.float32),
        in_specs=[in_smem()] + [in_vmem()] * len(shares),
        out_specs=in_vmem(),
        scratch_shapes=[pltpu.VMEM((tiles, 4 * count, LANES), jnp.float32)],
        compiler_params=params_of(),
        name="arrange",
    )(me, *shares)


def finish_kernel(count, width, pieces, me_ref, *rest):
    messages, rest = by_partner(rest[:count]), rest[count:]
    query_rows, out, rows, sems = rest
    me = me_ref[0]
    part = out.shape[0]
    step = 4
    stores = []

    def block(i, _):
        at = aligned(i * step * count, step * count)
        tiles = [message[at, :] for message in messages]
        tiles = swap_tiles_and_slots(tiles, width, me, False)
        for t in range(count):
            product = query_rows[t, at, :] * tiles[t]
            for m in range(step):
                rows[i * step + m, :, tile_of(t)] = product[m * count : (m + 1) * count]
        return 0

    size = part // pieces
    for piece in range(pieces):
        lax.fori_loop(piece * size // step, (piece + 1) * size // step, block, 0)
        done = pl.ds(piece * size, size)
        store = pltpu.make_async_copy(rows.at[done], out.at[done], sems.at[piece])
        store.start()
        stores.append(store)
    for store in stores:
        store.wait()


def finish(me, messages, query_rows, count, width):
    tiles, rows = query_rows.shape[:2]
    part = rows // count
    pieces = 8
    return pl.pallas_call(
        functools.partial(finish_kernel, count, width, pieces),
        out_shape=jax.ShapeDtypeStruct((part, count, tiles * LANES), jnp.float32),
        in_specs=[in_smem()] + [in_vmem()] * (count + 1),
        out_specs=in_any(),
        scratch_shapes=[
            pltpu.VMEM((part, count, tiles * LANES), jnp.float32),
            pltpu.SemaphoreType.DMA((pieces,)),
        ],
        compiler_params=params_of(),
        name="finish",
    )(me, *far_first_operands(messages), query_rows)


def swapped(block, axis, k):
    return lax.ppermute(block, axis, [(i, i ^ k) for i in range(lax.axis_size(axis))])


def exchanged(messages, axis):
    received = {0: messages[0]}
    for k in range(1, len(messages)):
        received[k] = swapped(messages[k], axis, k)
    return [received[k] for k in range(len(messages))]


def wide_body(streams, short_filters, skip_gain, long_filter):
    count = lax.axis_size("seq")
    groups = lax.axis_size("grp")
    place = lax.axis_index("seq").astype(jnp.int32)
    me = place.reshape(1)
    group = lax.axis_index("grp").astype(jnp.int32).reshape(1)
    length = streams.shape[1]
    width = long_filter.shape[1] // count
    forward, inverse = (jnp.asarray(table) for table in transform_tables(length))
    *gated, params = gate(me, streams, short_filters, skip_gain, long_filter, count, width)
    half = count // 2
    tiles = streams.shape[2] // LANES
    *evens, own_home, next_home, odds = query(
        me, streams, short_filters, gated[1], count, width
    )
    gated[1] = odds
    gated = exchanged(gated, "seq")
    odds = gated[1]
    taps = collect_taps(me, gated, count, width, length)
    taps = [taps] + [swapped(taps, "grp", k) for k in range(1, groups)]
    pairs = pair_shares(evens[1:], next_home, odds, taps[1])
    pairs = [swapped(pair, "seq", 2 * i) for i, pair in enumerate(pairs, 1)]
    spectra = filter_spectra(group, params, forward, taps, count, width)
    homes = (own_home, pairs[0], odds)
    bins, rims = gated_bins(me, forward, gated, count)
    convolved = list(convolve(me, inverse, spectra, bins, rims, homes, count))
    convolved[1:half] = hold(convolved[1:half], *pairs)
    first = [swapped(convolved[k], "seq", k) for k in (half, half + 1)]
    convolved[half + 2 :] = hold(convolved[half + 2 :], *pairs, first[0])
    convolved = exchanged(convolved[:half], "seq") + first + [
        swapped(convolved[k], "seq", k) for k in range(half + 2, count)
    ]
    query_rows = arrange(me, [evens[0], odds, *pairs], length, tiles, count, width)
    return finish(me, convolved, query_rows, count, width)


def body(streams, short_filters, skip_gain, long_filter):
    count = lax.axis_size("seq")
    width = long_filter.shape[1] // count
    one_tile = streams.shape[2] == count * LANES and count == ROWS
    if one_tile and width == ROWS and LANES % (count * width) == 0:
        return wide_body(streams, short_filters, skip_gain, long_filter)
    return narrow_body(streams, short_filters, skip_gain, long_filter)


def solution(mesh):
    return jax.shard_map(
        body,
        mesh=mesh,
        in_specs=(P(None, "seq", "grp"), P(None, None, "grp"), P("grp"), P("seq", "grp")),
        out_specs=P("seq", None, "grp"),
        check_vma=False,
    )
```
